32 devices in a mesh: fsdp: 4 (over y, x), rep: 8 (over z, core).
Axes of the slice: x: 2, y: 2, z: 4, core: 2. Of those that a mesh axis runs over, the one named last changes fastest.
Arguments:
- tokens: bfloat16 [10240, 1600], P(('rep', 'fsdp')), may hold values from -6 to 6
- lengths: int32 [8, 4], P('rep'), may hold values from 1 to 1277, as said below
- w_query: bfloat16 [2560000], P(('fsdp', 'rep')), may hold values from -0.15625 to 0.15625
- w_key: bfloat16 [512000], P(('fsdp', 'rep')), may hold values from -0.15625 to 0.15625
- w_value: bfloat16 [512000], P(('fsdp', 'rep')), may hold values from -0.15625 to 0.15625
- w_attn_out: bfloat16 [2560000], P(('fsdp', 'rep')), may hold values from -0.15625 to 0.15625
- w_inner: bfloat16 [5120000], P(('fsdp', 'rep')), may hold values from -0.15625 to 0.15625
- w_gate_z: bfloat16 [5120000], P(('fsdp', 'rep')), may hold values from -0.15625 to 0.15625
- w_bc: bfloat16 [51200], P(('fsdp', 'rep')), may hold values from -0.15625 to 0.15625
- w_step: bfloat16 [80000], P(('fsdp', 'rep')), may hold values from -0.15625 to 0.15625
- w_mamba_out: bfloat16 [5120000], P(('fsdp', 'rep')), may hold values from -0.109375 to 0.109375
- w_ffn_gate: bfloat16 [8806400], P(('fsdp', 'rep')), may hold values from -0.15625 to 0.15625
- w_ffn_up: bfloat16 [8806400], P(('fsdp', 'rep')), may hold values from -0.15625 to 0.15625
- w_ffn_down: bfloat16 [8806400], P(('fsdp', 'rep')), may hold values from -0.078125 to 0.078125
- norm_gains: float32 [4, 1600], replicated, may hold values from 0.5 to 1.5
- step_bias: float32 [50], replicated, may hold values from -2 to 1
- decay_log: float32 [50], replicated, may hold values from -9 to -3
- skip_gain: float32 [50], replicated, may hold values from 0.5 to 1.5
- cotangent: bfloat16 [10240, 1600], P(('rep', 'fsdp')), may hold values from -6 to 6
Outputs:
- output: bfloat16 [10240, 1600], P(('rep', 'fsdp'))
- grad_tokens: float32 [10240, 1600], P(('rep', 'fsdp'))
- grad_w_query: float32 [2560000], P(('fsdp', 'rep'))
- grad_w_key: float32 [512000], P(('fsdp', 'rep'))
- grad_w_value: float32 [512000], P(('fsdp', 'rep'))
- grad_w_attn_out: float32 [2560000], P(('fsdp', 'rep'))
- grad_w_inner: float32 [5120000], P(('fsdp', 'rep'))
- grad_w_gate_z: float32 [5120000], P(('fsdp', 'rep'))
- grad_w_bc: float32 [51200], P(('fsdp', 'rep'))
- grad_w_step: float32 [80000], P(('fsdp', 'rep'))
- grad_w_mamba_out: float32 [5120000], P(('fsdp', 'rep'))
- grad_w_ffn_gate: float32 [8806400], P(('fsdp', 'rep'))
- grad_w_ffn_up: float32 [8806400], P(('fsdp', 'rep'))
- grad_w_ffn_down: float32 [8806400], P(('fsdp', 'rep'))
- grad_norm_gains: float32 [4, 1600], replicated
- grad_step_bias: float32 [50], replicated
- grad_decay_log: float32 [50], replicated
- grad_skip_gain: float32 [50], replicated
The draws below stay inside these ranges and needn't reach their ends.
Inputs may be any that keep to these rules, and one draw needn't show every extreme that they name: Each row gives the lengths of the 4 sequences of one group of 1280 tokens and sums to 1280; the first sequence is 1 to 63 long, the third and fourth 1 to 31, so the second starts on the group's first device and ends on its last.
All inputs are finite; a program needn't handle non-finite values.
Results may differ from the reference program's by a relative error of at most 0.022.
Values may be sent and summed in bfloat16 or wider, within the bound.
No kernel may reach another device: no remote copies, remote signals or barrier semaphores. Data moves between devices by JAX's collectives and lax.ppermute only.
A program may use at most 704 MiB of HBM per device.

```python
import math
import jax
import jax.numpy as jnp
from jax import lax

D = 1600
QUERY_HEADS = 25
KEY_VALUE_HEADS = 5
HEAD_SIZE = 64
WIN = 1024
MI = 3200
NS = 16
FF = 5504
KV = 320
MH = 50
STRETCH = 64
TOK_DEV = 320
GROUP = 1280
TOKENS = 10240
N_FSDP = 4
N_REP = 8


def draw_lengths(key, part):
    key = jax.random.fold_in(key, 7)
    first_lens = jax.random.randint(key, (N_REP, 1), 1, STRETCH)
    tail_lens = jax.random.randint(jax.random.fold_in(key, 2), (N_REP, 2), 1, (STRETCH - 1) // 2 + 1)
    short_lens = jnp.concatenate([first_lens, tail_lens], axis=1)
    chosen = jax.random.randint(jax.random.fold_in(key, 1), (), 0, N_REP)
    short_lens = jnp.where(jnp.arange(N_REP)[:, None] == chosen, 1, short_lens)
    longest = N_FSDP * TOK_DEV - jnp.sum(short_lens, axis=1)
    return jnp.stack([short_lens[:, 0], longest, short_lens[:, 1], short_lens[:, 2]], axis=1).astype(jnp.int32)


def shard_levels(own_key, dims, pieces, smallest, largest):
    factor_of = 1.0
    for dim, shards_of in pieces:
        draws = jax.random.uniform(jax.random.fold_in(jax.random.fold_in(own_key, 6), dim), (shards_of,), jnp.float32, smallest / len(pieces), largest / len(pieces))
        factor_of = factor_of * jnp.repeat(jnp.exp(draws), dims[dim] // shards_of).reshape((-1,) + (1,) * (len(dims) - 1 - dim))
    return factor_of


def scatter_about(rng, extent, scale, most, pieces=(), kind=jnp.bfloat16):
    level = shard_levels(rng, extent, pieces, -0.22, 0.18) if pieces else 1.0
    values = jax.random.normal(rng, extent, jnp.float32) * scale * level
    return jnp.minimum(jnp.maximum(values, -most), most).astype(kind)


def setup_inputs(seed: int = 0) -> dict:
    arg_keys = jax.random.split(jax.random.key(seed), 20)
    return {
        "tokens": scatter_about(arg_keys[0], (TOKENS, D), 1.0, 6.0, ((0, 32),)),
        "lengths": draw_lengths(jax.random.fold_in(arg_keys[19], 71), 0),
        "w_query": scatter_about(arg_keys[2], (D * D,), D ** -0.5, 0.15625, ((0, 32),)),
        "w_key": scatter_about(arg_keys[3], (D * KV,), D ** -0.5, 0.15625, ((0, 32),)),
        "w_value": scatter_about(arg_keys[4], (D * KV,), D ** -0.5, 0.15625, ((0, 32),)),
        "w_attn_out": scatter_about(arg_keys[5], (D * D,), D ** -0.5, 0.15625, ((0, 32),)),
        "w_inner": scatter_about(arg_keys[6], (D * MI,), D ** -0.5, 0.15625, ((0, 32),)),
        "w_gate_z": scatter_about(arg_keys[7], (D * MI,), D ** -0.5, 0.15625, ((0, 32),)),
        "w_bc": scatter_about(arg_keys[8], (D * 2 * NS,), D ** -0.5, 0.15625, ((0, 32),)),
        "w_step": scatter_about(arg_keys[9], (D * MH,), D ** -0.5, 0.15625, ((0, 32),)),
        "w_mamba_out": scatter_about(arg_keys[10], (MI * D,), MI ** -0.5, 0.109375, ((0, 32),)),
        "w_ffn_gate": scatter_about(arg_keys[11], (D * FF,), D ** -0.5, 0.15625, ((0, 32),)),
        "w_ffn_up": scatter_about(arg_keys[12], (D * FF,), D ** -0.5, 0.15625, ((0, 32),)),
        "w_ffn_down": scatter_about(arg_keys[13], (FF * D,), FF ** -0.5, 0.078125, ((0, 32),)),
        "norm_gains": jnp.clip(1.0 + 0.1 * jax.random.normal(arg_keys[14], (4, D), jnp.float32), 0.5, 1.5),
        "step_bias": jnp.clip(jax.random.uniform(arg_keys[15], (MH,), jnp.float32, -2.0, 1.0), -2.0, 1.0),
        "decay_log": jnp.clip(jax.random.uniform(arg_keys[16], (MH,), jnp.float32, -9.0, -3.0), -9.0, -3.0),
        "skip_gain": jnp.clip(jax.random.uniform(arg_keys[17], (MH,), jnp.float32, 0.5, 1.5), 0.5, 1.5),
        "cotangent": scatter_about(arg_keys[18], (TOKENS, D), 1.0, 6.0, ((0, 32),)),
    }


epsilon = 1e-06
masked_score = -1e+30
highest = lax.Precision.HIGHEST

@jax.custom_vjp
def reduced_precision(v):
    return lax.optimization_barrier(v.astype(jnp.bfloat16)).astype(jnp.float32)

@jax.custom_vjp
def reduced_precision_back(v):
    return v

def low_keep(v):
    return (reduced_precision(v), None)

def low_pass(kept, grad):
    return (grad,)

def back_keep(v):
    return (v, None)

def back_low(kept, grad):
    return (reduced_precision(grad),)
reduced_precision.defvjp(low_keep, low_pass)
reduced_precision_back.defvjp(back_keep, back_low)

def matrix_product(value_rows, matrix):
    return jnp.dot(value_rows, matrix, precision=highest, preferred_element_type=jnp.float32)

def rms_scale(value_rows, gain):
    return value_rows * lax.rsqrt(lax.optimization_barrier(jnp.mean(value_rows * value_rows, axis=-1, keepdims=True)) + epsilon) * gain

def silu(value_rows):
    return value_rows * jax.nn.sigmoid(value_rows)

def sequence_layout(seq_lengths, position):
    seq_ends = jnp.cumsum(seq_lengths, dtype=jnp.int32)
    seq_starts = seq_ends - seq_lengths
    segment = lax.optimization_barrier(jnp.sum((position[:, None] >= seq_ends[None, :]).astype(jnp.int32), axis=1, dtype=jnp.int32))
    labels = jnp.arange(seq_lengths.shape[0], dtype=jnp.int32)
    seq_begin = lax.optimization_barrier(jnp.sum(jnp.where(segment[:, None] == labels[None, :], seq_starts[None, :], 0), axis=1, dtype=jnp.int32))
    return (segment, (position - seq_begin).astype(jnp.float32))

def apply_rotary(value_rows, place, sign):
    half_width = value_rows.shape[-1] // 2
    frequency = jnp.exp(jnp.arange(half_width, dtype=jnp.float32) * (-2.0 * math.log(10000.0) / value_rows.shape[-1]))
    angles = place[:, None] * frequency[None, :]
    cosine = jnp.cos(angles)[:, None, :]
    sine_part = sign * jnp.sin(angles)[:, None, :]
    first_half = value_rows[..., :half_width]
    second_half = value_rows[..., half_width:]
    return jnp.concatenate([first_half * cosine - second_half * sine_part, second_half * cosine + first_half * sine_part], axis=-1)

def stretch_scan(carry, block):
    state, seg_prev = carry
    inner_q, b_q, c_q, rate_q, step_q, seg_q = block
    length = inner_q.shape[0]
    cumul = jnp.cumsum(rate_q, axis=0)
    order = jnp.arange(length, dtype=jnp.int32)
    live = (seg_q[:, None] == seg_q[None, :]) & (order[:, None] >= order[None, :])
    spread = jnp.where(live[:, :, None], cumul[:, None, :] - cumul[None, :, :], 0.0)
    decay = jnp.where(live[:, :, None], jnp.exp(spread), 0.0)
    intersection = jnp.dot(c_q, b_q.T, precision=highest, preferred_element_type=jnp.float32)
    mixing = decay * intersection[:, :, None] * step_q[None, :, :]
    result = jnp.einsum('ijh,jhp->ihp', mixing, inner_q, precision=highest)
    carried = jnp.where((seg_q == seg_prev)[:, None], jnp.exp(cumul), 0.0)
    result = result + carried[:, :, None] * jnp.einsum('in,hpn->ihp', c_q, state, precision=highest)
    tail_sum = cumul[-1]
    last_seg = seg_q[-1]
    ending = jnp.where((seg_q == last_seg)[:, None], jnp.exp(tail_sum[None, :] - cumul), 0.0) * step_q
    fresh = jnp.einsum('jh,jhp,jn->hpn', ending, inner_q, b_q, precision=highest)
    fresh = fresh + jnp.where(last_seg == seg_prev, jnp.exp(tail_sum), 0.0)[:, None, None] * state
    return ((fresh, last_seg), result)

def group_layer(x_group, seq_lengths, params):
    wq, key_weight, value_weight, wo, wx, wz, wbc, wdt, wom, wg, wu, wd, gains, bias, alog, skip = params
    item_count = x_group.shape[0]
    index = jnp.arange(item_count, dtype=jnp.int32)
    segment, place = sequence_layout(seq_lengths, index)
    normalized_input = reduced_precision(rms_scale(x_group, gains[0]))
    q_raw = reduced_precision_back(matrix_product(normalized_input, wq)).reshape(item_count, QUERY_HEADS, HEAD_SIZE)
    query_rows = reduced_precision(apply_rotary(q_raw, place, 1.0))
    key_unrotated = reduced_precision_back(matrix_product(normalized_input, key_weight)).reshape(item_count, KEY_VALUE_HEADS, HEAD_SIZE)
    keys_rot = reduced_precision(apply_rotary(key_unrotated, place, 1.0))
    value_rows = reduced_precision(reduced_precision_back(matrix_product(normalized_input, value_weight))).reshape(item_count, KEY_VALUE_HEADS, HEAD_SIZE)
    rows_per_block = math.gcd(512, item_count)
    split_parts = item_count // rows_per_block
    query_block_list = query_rows.reshape(split_parts, rows_per_block, KEY_VALUE_HEADS, QUERY_HEADS // KEY_VALUE_HEADS, HEAD_SIZE)
    index_blocks = index.reshape(split_parts, rows_per_block)
    seg_blocks = segment.reshape(split_parts, rows_per_block)

    def attend_rows(item):
        q_part, index_part, seg_part = item
        scores = reduced_precision_back(jnp.einsum('bcgd,kcd->cgbk', q_part, keys_rot, precision=highest) * HEAD_SIZE ** (-0.5))
        offset = index_part[:, None] - index[None, :]
        visible = (seg_part[:, None] == segment[None, :]) & (offset >= 0) & (offset < WIN)
        scores = jnp.where(visible[None, None], scores, masked_score)
        top_score = lax.optimization_barrier(jnp.max(scores, axis=-1, keepdims=True))
        exponent = jnp.exp(scores - top_score)
        probs_low = reduced_precision(exponent / lax.optimization_barrier(jnp.sum(exponent, axis=-1, keepdims=True)))
        return jnp.einsum('cgbk,kcd->bcgd', probs_low, value_rows, precision=highest)
    attn_vals = lax.map(jax.checkpoint(attend_rows), (query_block_list, index_blocks, seg_blocks)).reshape(item_count, D)
    attn_vals = reduced_precision(reduced_precision_back(attn_vals))
    attn_proj = reduced_precision_back(matrix_product(attn_vals, wo))
    branch_attn = rms_scale(attn_proj, gains[1])
    inner = reduced_precision(reduced_precision_back(matrix_product(normalized_input, wx))).reshape(item_count, MH, HEAD_SIZE)
    gate_z = reduced_precision_back(matrix_product(normalized_input, wz))
    bc_vals = reduced_precision(reduced_precision_back(matrix_product(normalized_input, wbc)))
    step_raw = reduced_precision_back(matrix_product(normalized_input, wdt))
    step_size = jax.nn.softplus(step_raw + bias)
    rates = -step_size * jnp.exp(alog)
    stretches = item_count // STRETCH
    blocks = (inner.reshape(stretches, STRETCH, MH, HEAD_SIZE), bc_vals[:, :NS].reshape(stretches, STRETCH, NS), bc_vals[:, NS:].reshape(stretches, STRETCH, NS), rates.reshape(stretches, STRETCH, MH), step_size.reshape(stretches, STRETCH, MH), segment.reshape(stretches, STRETCH))
    start = (jnp.zeros((MH, HEAD_SIZE, NS), jnp.float32), jnp.int32(-1))
    _, ssm_out = lax.scan(jax.checkpoint(stretch_scan), start, blocks)
    y_total = ssm_out.reshape(item_count, MH, HEAD_SIZE) + skip[None, :, None] * inner
    mixed_in = reduced_precision(y_total.reshape(item_count, MI) * silu(gate_z))
    mamba_proj = reduced_precision_back(matrix_product(mixed_in, wom))
    branch_mamba = rms_scale(mamba_proj, gains[2])
    mix = x_group + 0.5 * (branch_attn + branch_mamba)
    normed_two = reduced_precision(rms_scale(mix, gains[3]))
    fgate = reduced_precision_back(matrix_product(normed_two, wg))
    fup = reduced_precision_back(matrix_product(normed_two, wu))
    hidden = reduced_precision(silu(fgate) * fup)
    return mix + reduced_precision_back(matrix_product(hidden, wd))

def reference(tokens, lengths, w_query, w_key, w_value, w_attn_out, w_inner, w_gate_z, w_bc, w_step, w_mamba_out, w_ffn_gate, w_ffn_up, w_ffn_down, norm_gains, step_bias, decay_log, skip_gain, cotangent):
    shapes = ((D, D), (D, KV), (D, KV), (D, D), (D, MI), (D, MI), (D, 2 * NS), (D, MH), (MI, D), (D, FF), (D, FF), (FF, D))
    flats = (w_query, w_key, w_value, w_attn_out, w_inner, w_gate_z, w_bc, w_step, w_mamba_out, w_ffn_gate, w_ffn_up, w_ffn_down)
    matrices = tuple((flat.astype(jnp.float32).reshape(shape) for flat, shape in zip(flats, shapes)))
    params = matrices + (norm_gains, step_bias, decay_log, skip_gain)
    x_all = tokens.astype(jnp.float32).reshape(N_REP, GROUP, D)

    def whole_layer(x_groups, weights):

        def one_group(item):
            return group_layer(item[0], item[1], weights)
        return lax.map(jax.checkpoint(one_group), (x_groups, lengths))
    result, pull = jax.vjp(whole_layer, x_all, params)
    grad_x, grads = pull(cotangent.astype(jnp.float32).reshape(N_REP, GROUP, D))
    return (result.reshape(TOKENS, D).astype(jnp.bfloat16), grad_x.reshape(TOKENS, D), grads[0].reshape(-1), grads[1].reshape(-1), grads[2].reshape(-1), grads[3].reshape(-1), grads[4].reshape(-1), grads[5].reshape(-1), grads[6].reshape(-1), grads[7].reshape(-1), grads[8].reshape(-1), grads[9].reshape(-1), grads[10].reshape(-1), grads[11].reshape(-1), grads[12], grads[13], grads[14], grads[15])
```

```python
import functools
import math

import jax
import jax.numpy as jnp
from jax import lax
from jax.experimental import pallas as pl
from jax.experimental.layout import Layout, with_layout_constraint
from jax.experimental.pallas import tpu as pltpu
from jax.sharding import PartitionSpec as P

D = 1600
QUERY_HEADS = 25
KEY_VALUE_HEADS = 5
HEAD_SIZE = 64
WIN = 1024
MI = 3200
NS = 16
FF = 5504
MH = 50
KV = KEY_VALUE_HEADS * HEAD_SIZE
HEADS_PER_GROUP = QUERY_HEADS // KEY_VALUE_HEADS
SCALE = HEAD_SIZE ** (-0.5)
CHUNK = 128
QUERY_BLOCK = 256
STEP_ROWS = 16
VMEM_BYTES = 50 * 1024 * 1024

epsilon = 1e-06
masked_score = -1e30
highest = lax.Precision.HIGHEST
f32 = jnp.float32
bf16 = jnp.bfloat16


def rms_scale(value_rows, gain):
    return (
        value_rows
        * lax.rsqrt(jnp.mean(value_rows * value_rows, axis=-1, keepdims=True) + epsilon)
        * gain
    )


def norm_back(grad_in, value_rows, gain):
    factor = lax.rsqrt(jnp.mean(value_rows * value_rows, axis=-1, keepdims=True) + epsilon)
    weighted = grad_in * gain
    spread = jnp.mean(weighted * value_rows, axis=-1, keepdims=True)
    return (
        factor * weighted - value_rows * factor * factor * factor * spread,
        jnp.sum(grad_in * value_rows * factor, axis=0),
    )


def silu(value_rows):
    return value_rows * jax.nn.sigmoid(value_rows)


def silu_slope(value_rows):
    sigmoid_v = jax.nn.sigmoid(value_rows)
    return sigmoid_v * (1.0 + value_rows * (1.0 - sigmoid_v))


def dot(a, b, ca, cb, precision=None):
    return lax.dot_general(
        a, b, (((ca,), (cb,)), ((), ())), precision=precision, preferred_element_type=f32
    )


def sequence_layout(seq_lengths, position):
    seq_ends = jnp.cumsum(seq_lengths, dtype=jnp.int32)
    seq_starts = seq_ends - seq_lengths
    segment = jnp.sum(
        (position[:, None] >= seq_ends[None, :]).astype(jnp.int32), axis=1, dtype=jnp.int32
    )
    labels = jnp.arange(seq_lengths.shape[0], dtype=jnp.int32)
    seq_begin = jnp.sum(
        jnp.where(segment[:, None] == labels[None, :], seq_starts[None, :], 0),
        axis=1,
        dtype=jnp.int32,
    )
    return (segment, (position - seq_begin).astype(f32))


def key_range(i):
    low = max(0, i * QUERY_BLOCK - (WIN - 1)) // QUERY_BLOCK * QUERY_BLOCK
    return low, (i + 1) * QUERY_BLOCK


def fill_mask(seg_col, seg_row, mask, blocks):
    for i in range(blocks):
        low, high = key_range(i)
        cols = slice(i * QUERY_BLOCK, (i + 1) * QUERY_BLOCK)
        shape = (high - low, QUERY_BLOCK)
        key = lax.broadcasted_iota(jnp.int32, shape, 0) + low
        query = lax.broadcasted_iota(jnp.int32, shape, 1) + i * QUERY_BLOCK
        gap = query - key
        visible = (seg_col[low:high, :] == seg_row[:, cols]) & (gap >= 0) & (gap < WIN)
        mask[low:high, cols] = jnp.where(visible, 0.0, masked_score)


def rotate(value, cosine, sine):
    half = HEAD_SIZE // 2
    a, b = value[:half], value[half:]
    return jnp.concatenate([a * cosine - b * sine, b * cosine + a * sine], axis=0)


def attn_fwd_kernel(
    kvmap, kv_ref, q_ref, cosine, sine, seg_row, seg_col, o_ref, qt_ref, kt_ref, kn_ref, vn_ref, mask, vt, *, blocks
):
    h = pl.program_id(0)

    @pl.when(h == 0)
    def _():
        fill_mask(seg_col, seg_row, mask, blocks)
        for c in range(KEY_VALUE_HEADS):
            k = rotate(kv_ref[c], cosine[...], sine[...])
            kt_ref[c] = k.astype(bf16)
            kn_ref[c] = k.T.astype(bf16)
            v = kv_ref[KEY_VALUE_HEADS + c]
            vt[c] = v.astype(bf16)
            vn_ref[c] = v.T.astype(bf16)

    kv = kvmap[h]
    tokens = o_ref.shape[3]
    for i in range(blocks):
        low, high = key_range(i)
        start, stop = i * QUERY_BLOCK, (i + 1) * QUERY_BLOCK
        cols = slice(start, stop)
        q = (rotate(q_ref[0, :, cols], cosine[:, cols], sine[:, cols]) * SCALE).astype(bf16)
        qt_ref[0, :, cols] = q
        s = dot(kn_ref[kv, low:high, :], q, 1, 0) + mask[low:high, cols]
        p = jnp.exp(s - jnp.max(s, axis=0, keepdims=True))
        total = jnp.sum(p, axis=0, keepdims=True)
        o = dot(vt[kv, :, low:high], p.astype(bf16), 1, 0)
        o = (o / total).astype(bf16)
        for d in range(o_ref.shape[0]):
            first, last = max(start, d * tokens), min(stop, (d + 1) * tokens)
            if first < last:
                part = o[:, first - start : last - start]
                o_ref[d, 0, :, first - d * tokens : last - d * tokens] = part


def attn_fwd(kvmap, proj, cosine, sine, seg_row, seg_col, devices):
    heads = proj.shape[0] - 2 * KEY_VALUE_HEADS
    group = proj.shape[2]
    tokens = group // devices
    per_head = pl.BlockSpec((1, HEAD_SIZE, group), lambda h, m: (h, 0, 0))
    angle = pl.BlockSpec((HEAD_SIZE // 2, group), lambda h, m: (0, 0))
    kv_t = (KEY_VALUE_HEADS, HEAD_SIZE, group)
    kv_n = (KEY_VALUE_HEADS, group, HEAD_SIZE)
    whole_t = pl.BlockSpec(kv_t, lambda h, m: (0, 0, 0))
    whole_n = pl.BlockSpec(kv_n, lambda h, m: (0, 0, 0))
    return pl.pallas_call(
        functools.partial(attn_fwd_kernel, blocks=group // QUERY_BLOCK),
        out_shape=(
            jax.ShapeDtypeStruct((devices, heads, HEAD_SIZE, tokens), bf16),
            jax.ShapeDtypeStruct((heads, HEAD_SIZE, group), bf16),
            jax.ShapeDtypeStruct(kv_t, bf16),
            jax.ShapeDtypeStruct(kv_n, bf16),
            jax.ShapeDtypeStruct(kv_n, bf16),
        ),
        grid_spec=pltpu.PrefetchScalarGridSpec(
            num_scalar_prefetch=1,
            grid=(heads,),
            in_specs=[
                pl.BlockSpec((2 * KEY_VALUE_HEADS, HEAD_SIZE, group), lambda h, m: (0, 0, 0)),
                pl.BlockSpec((1, HEAD_SIZE, group), lambda h, m: (h + 2 * KEY_VALUE_HEADS, 0, 0)),
                angle,
                angle,
                pl.BlockSpec((1, group), lambda h, m: (0, 0)),
                pl.BlockSpec((group, 1), lambda h, m: (0, 0)),
            ],
            out_specs=(
                pl.BlockSpec((devices, 1, HEAD_SIZE, tokens), lambda h, m: (0, h, 0, 0)),
                per_head,
                whole_t,
                whole_n,
                whole_n,
            ),
            scratch_shapes=[pltpu.VMEM((group, group), f32), pltpu.VMEM(kv_t, bf16)],
        ),
        compiler_params=pltpu.CompilerParams(vmem_limit_bytes=VMEM_BYTES),
        cost_estimate=pl.CostEstimate(
            flops=group * group, bytes_accessed=group * HEAD_SIZE, transcendentals=group,
        ),
        name="attn_fwd",
    )(kvmap, proj, proj, cosine, sine, seg_row, seg_col)


def attn_bwd_kernel(kvmap, *refs, blocks, devices):
    do_parts = refs[:devices]
    q_ref, kn_ref, kt_ref, vn_ref, cosine, sine, seg_row, seg_col = refs[devices : devices + 8]
    g_ref, mask, dk, dv, do_all = refs[devices + 8 :]
    h = pl.program_id(0)

    @pl.when(h == 0)
    def _():
        fill_mask(seg_col, seg_row, mask, blocks)
        dk[...] = jnp.zeros(dk.shape, f32)
        dv[...] = jnp.zeros(dv.shape, f32)

    kv = kvmap[h]
    tokens = do_parts[0].shape[3]
    for d in range(devices):
        do_all[:, d * tokens : (d + 1) * tokens] = do_parts[d][0, 0]
    for i in range(blocks):
        low, high = key_range(i)
        cols = slice(i * QUERY_BLOCK, (i + 1) * QUERY_BLOCK)
        q = q_ref[0, :, cols]
        do = do_all[:, cols]
        s = dot(kn_ref[kv, low:high, :], q, 1, 0) + mask[low:high, cols]
        p = jnp.exp(s - jnp.max(s, axis=0, keepdims=True))
        p = p * (1.0 / jnp.sum(p, axis=0, keepdims=True))
        dp = dot(vn_ref[kv, low:high, :], do, 1, 0)
        delta = jnp.sum(p * dp, axis=0, keepdims=True)
        ds = (p * (dp - delta)).astype(bf16)
        dv[kv, low:high, :] += dot(p.astype(bf16), do, 1, 1)
        dk[kv, low:high, :] += dot(ds, q, 1, 1)
        dq = dot(kt_ref[kv, :, low:high], ds, 1, 0) * SCALE
        dq = rotate(dq, cosine[:, cols], -sine[:, cols])
        g_ref[2 * KEY_VALUE_HEADS + h, :, cols] = dq.astype(bf16)

    @pl.when(h == pl.num_programs(0) - 1)
    def _():
        for c in range(KEY_VALUE_HEADS):
            g_ref[c] = rotate(dk[c].T, cosine[...], -sine[...]).astype(bf16)
            g_ref[KEY_VALUE_HEADS + c] = dv[c].T.astype(bf16)


def attn_bwd(kvmap, do_blocks, q_t, k_n, k_t, v_n, cosine, sine, seg_row, seg_col):
    devices, heads, _, tokens = do_blocks.shape
    group = q_t.shape[2]
    angle = pl.BlockSpec((HEAD_SIZE // 2, group), lambda h, m: (0, 0))
    kv_t = (KEY_VALUE_HEADS, HEAD_SIZE, group)
    kv_n = (KEY_VALUE_HEADS, group, HEAD_SIZE)
    whole_n = pl.BlockSpec(kv_n, lambda h, m: (0, 0, 0))
    out = (2 * KEY_VALUE_HEADS + heads, HEAD_SIZE, group)

    def block_spec(d):
        return pl.BlockSpec((1, 1, HEAD_SIZE, tokens), lambda h, m: (m[heads + d], h, 0, 0))

    return pl.pallas_call(
        functools.partial(attn_bwd_kernel, blocks=group // QUERY_BLOCK, devices=devices),
        out_shape=jax.ShapeDtypeStruct(out, bf16),
        grid_spec=pltpu.PrefetchScalarGridSpec(
            num_scalar_prefetch=1,
            grid=(heads,),
            in_specs=[block_spec(d) for d in range(devices)]
            + [
                pl.BlockSpec((1, HEAD_SIZE, group), lambda h, m: (h, 0, 0)),
                whole_n,
                pl.BlockSpec(kv_t, lambda h, m: (0, 0, 0)),
                whole_n,
                angle,
                angle,
                pl.BlockSpec((1, group), lambda h, m: (0, 0)),
                pl.BlockSpec((group, 1), lambda h, m: (0, 0)),
            ],
            out_specs=pl.BlockSpec(out, lambda h, m: (0, 0, 0)),
            scratch_shapes=[
                pltpu.VMEM((group, group), f32),
                pltpu.VMEM(kv_n, f32),
                pltpu.VMEM(kv_n, f32),
                pltpu.VMEM((HEAD_SIZE, group), bf16),
            ],
        ),
        compiler_params=pltpu.CompilerParams(vmem_limit_bytes=VMEM_BYTES),
        cost_estimate=pl.CostEstimate(
            flops=group * group, bytes_accessed=group * HEAD_SIZE, transcendentals=group,
        ),
        name="attn_bwd",
    )(kvmap, *([do_blocks] * devices), q_t, k_n, k_t, v_n, cosine, sine, seg_row, seg_col)


def block_setup(p_ref, bias, decay, marks, seg_col, channels):
    at = 2 * channels
    b_t = p_ref[at : at + NS].astype(bf16)
    c_t = p_ref[at + NS : at + 2 * NS].astype(bf16)
    raw = p_ref[at + 2 * NS : at + 2 * NS + STEP_ROWS] + bias[...]
    step = jnp.maximum(raw, 0.0) + jnp.log1p(jnp.exp(-jnp.abs(raw)))
    rate = -step * decay[...]
    rows = lax.broadcasted_iota(jnp.int32, (CHUNK, CHUNK), 0)
    cols = lax.broadcasted_iota(jnp.int32, (CHUNK, CHUNK), 1)
    a_t = dot(rate, (rows <= cols).astype(f32), 1, 0, highest)
    a_n = a_t.T
    visible = (seg_col[...] == marks[0:1]) & (rows <= cols)
    hidden = jnp.where(visible, 0.0, masked_score)
    return b_t, c_t, raw, step, rate, a_t, a_n, rows, cols, hidden


def ssm_fwd_kernel(p_ref, bias, decay, marks, seg_col, skip, y_ref, mixed_ref, states, state, *, heads):
    channels = heads * HEAD_SIZE

    @pl.when(pl.program_id(0) == 0)
    def _():
        state[...] = jnp.zeros(state.shape, f32)

    states[0] = state[...]
    b_t, c_t, _, step, _, a_t, a_n, _, _, hidden = block_setup(
        p_ref, bias, decay, marks, seg_col, channels
    )
    block = dot(b_t, c_t, 0, 0)
    enter, leave, through = marks[1:2], marks[2:3], marks[3:4, 0:1]
    for h in range(heads):
        at = slice(h * HEAD_SIZE, (h + 1) * HEAD_SIZE)
        a_row = a_t[h : h + 1]
        a_end = a_t[h : h + 1, CHUNK - 1 :]
        x = p_ref[at].astype(bf16).astype(f32)
        z = p_ref[channels + h * HEAD_SIZE : channels + (h + 1) * HEAD_SIZE]
        mixing = (jnp.exp(a_row - a_n[:, h : h + 1] + hidden) * block).astype(bf16)
        xs = x * step[h : h + 1]
        y = dot(xs.astype(bf16), mixing, 1, 0)
        s = state[at]
        y = y + dot(s.astype(bf16), c_t, 1, 0) * (enter * jnp.exp(a_row)) + skip[h] * x
        y_ref[at] = y
        mixed_ref[at] = (y * silu(z)).astype(bf16)
        xw = (xs * (leave * jnp.exp(a_end - a_row))).astype(bf16)
        state[at] = through * jnp.exp(a_end) * s + dot(xw, b_t, 1, 1)


def ssm_specs(height, order):
    column = pl.BlockSpec((STEP_ROWS, 1), lambda c: (0, 0))
    return [
        pl.BlockSpec((height, CHUNK), lambda c: (0, order(c))),
        column,
        column,
        pl.BlockSpec((8, CHUNK), lambda c: (0, order(c))),
        pl.BlockSpec((CHUNK, 1), lambda c: (order(c), 0)),
        pl.BlockSpec(memory_space=pltpu.SMEM),
    ]


def ssm_fwd(heads, proj, bias, decay, marks, seg_col, skip):
    height, group = proj.shape
    channels = heads * HEAD_SIZE
    count = group // CHUNK
    by_block = pl.BlockSpec((channels, CHUNK), lambda c: (0, c))
    return pl.pallas_call(
        functools.partial(ssm_fwd_kernel, heads=heads),
        out_shape=(
            jax.ShapeDtypeStruct((channels, group), f32),
            jax.ShapeDtypeStruct((channels, group), bf16),
            jax.ShapeDtypeStruct((count, channels, NS), f32),
        ),
        grid=(count,),
        in_specs=ssm_specs(height, lambda c: c),
        out_specs=(by_block, by_block, pl.BlockSpec((1, channels, NS), lambda c: (c, 0, 0))),
        scratch_shapes=[pltpu.VMEM((channels, NS), f32)],
        compiler_params=pltpu.CompilerParams(vmem_limit_bytes=VMEM_BYTES),
        cost_estimate=pl.CostEstimate(
            flops=group * group, bytes_accessed=group * HEAD_SIZE, transcendentals=group,
        ),
        name="ssm_fwd",
    )(proj, bias, decay, marks, seg_col, skip)


def ssm_bwd_kernel(
    p_ref,
    bias,
    decay,
    marks,
    seg_col,
    skip,
    up_ref,
    y_ref,
    states,
    g_ref,
    sums,
    adjoint,
    after,
    before,
    gstep,
    grate,
    *,
    heads,
):
    channels = heads * HEAD_SIZE

    @pl.when(pl.program_id(0) == 0)
    def _():
        for ref in (adjoint, sums, after, before, gstep, grate):
            ref[...] = jnp.zeros(ref.shape, f32)

    b_t, c_t, raw, step_all, rate_all, a_t, a_n, rows, cols, hidden = block_setup(
        p_ref, bias, decay, marks, seg_col, channels
    )
    block = dot(b_t, c_t, 0, 0)
    enter, leave, through = marks[1:2], marks[2:3], marks[3:4, 0:1]
    from_here = (rows >= cols).astype(f32)
    from_here_low = from_here.astype(bf16)
    strictly = (rows < cols).astype(f32)
    pair_sum = jnp.zeros((CHUNK, CHUNK), f32)
    gc = jnp.zeros((NS, CHUNK), f32)
    gb = jnp.zeros((NS, CHUNK), f32)
    at_skip = 2 * STEP_ROWS
    for h in range(heads):
        at = slice(h * HEAD_SIZE, (h + 1) * HEAD_SIZE)
        at_gate = slice(channels + h * HEAD_SIZE, channels + (h + 1) * HEAD_SIZE)
        one = slice(h, h + 1)
        a_row = a_t[one]
        a_end = a_t[one, CHUNK - 1 :]
        step = step_all[one]
        x = p_ref[at].astype(bf16).astype(f32)
        z = p_ref[at_gate]
        g = up_ref[at]
        sigmoid_z = jax.nn.sigmoid(z)
        gy = g * z * sigmoid_z
        gz = g * y_ref[at] * sigmoid_z * (1.0 + z * (1.0 - sigmoid_z))
        g_ref[at_gate] = gz.astype(bf16)
        sums[at_skip + h : at_skip + h + 1] += jnp.sum(gy * x, axis=0, keepdims=True)
        reach = jnp.exp(a_row - a_n[:, one] + hidden)
        gy_low = gy.astype(bf16)
        xs = x * step
        u = dot(gy_low, (reach * block).astype(bf16), 1, 1)
        lam = adjoint[at]
        lam_low = lam.astype(bf16)
        out_weight = leave * jnp.exp(a_end - a_row)
        u_state = dot(lam_low, b_t, 1, 0) * out_weight
        u = u + u_state
        g_ref[at] = (step * u + skip[h] * gy).astype(bf16)
        gstep[one] = jnp.sum(x * u, axis=0, keepdims=True)
        before[one] = jnp.sum(xs * u_state, axis=0, keepdims=True)
        pairs = dot(xs.astype(bf16), gy_low, 0, 0) * reach
        pair_sum = pair_sum + pairs
        crossing = dot((pairs * block).astype(bf16), from_here_low, 1, 0)
        crossed = jnp.sum(crossing * strictly, axis=0, keepdims=True)
        gyw = gy * (enter * jnp.exp(a_row))
        gyw_low = gyw.astype(bf16)
        s = states[0, at]
        s_low = s.astype(bf16)
        after[one] = jnp.sum(gyw * dot(s_low, c_t, 1, 0), axis=0, keepdims=True)
        gc = gc + dot(s_low, gyw_low, 0, 0)
        gb = gb + dot(lam_low, (xs * out_weight).astype(bf16), 0, 0)
        passing = through * jnp.exp(a_end)
        product = jnp.sum(jnp.sum(lam * s, axis=1, keepdims=True), axis=0, keepdims=True)
        grate[one] = crossed + passing * product
        adjoint[at] = passing * lam + dot(gyw_low, c_t, 1, 1)
    grate_all = (
        grate[...]
        + dot(after[...], from_here, 1, 0, highest)
        + dot(before[...], strictly, 1, 0, highest)
    )
    pair_low = pair_sum.astype(bf16)
    small = 2 * channels
    g_ref[small : small + NS] = (gb + dot(c_t, pair_low, 1, 1)).astype(bf16)
    g_ref[small + NS : small + 2 * NS] = (gc + dot(b_t, pair_low, 1, 0)).astype(bf16)
    graw = (gstep[...] - grate_all * decay[...]) * jax.nn.sigmoid(raw)
    at_step = small + 2 * NS
    g_ref[at_step : at_step + STEP_ROWS] = graw.astype(bf16)
    rest = g_ref.shape[0] - at_step - STEP_ROWS
    g_ref[at_step + STEP_ROWS :] = jnp.zeros((rest, CHUNK), bf16)
    sums[:STEP_ROWS] += graw
    sums[STEP_ROWS:at_skip] += grate_all * rate_all


def ssm_bwd(heads, proj, bias, decay, marks, seg_col, skip, up_t, y_t, states):
    height, group = proj.shape
    channels = heads * HEAD_SIZE
    count = group // CHUNK

    def order(c):
        return count - 1 - c

    by_block = pl.BlockSpec((channels, CHUNK), lambda c: (0, order(c)))
    small = pltpu.VMEM((STEP_ROWS, CHUNK), f32)
    return pl.pallas_call(
        functools.partial(ssm_bwd_kernel, heads=heads),
        out_shape=(
            jax.ShapeDtypeStruct((height, group), bf16),
            jax.ShapeDtypeStruct((3 * STEP_ROWS, CHUNK), f32),
        ),
        grid=(count,),
        in_specs=ssm_specs(height, order)
        + [by_block, by_block, pl.BlockSpec((1, channels, NS), lambda c: (order(c), 0, 0))],
        out_specs=(
            pl.BlockSpec((height, CHUNK), lambda c: (0, order(c))),
            pl.BlockSpec((3 * STEP_ROWS, CHUNK), lambda c: (0, 0)),
        ),
        scratch_shapes=[pltpu.VMEM((channels, NS), f32), small, small, small, small],
        compiler_params=pltpu.CompilerParams(vmem_limit_bytes=VMEM_BYTES),
        cost_estimate=pl.CostEstimate(
            flops=group * group, bytes_accessed=group * HEAD_SIZE, transcendentals=group,
        ),
        name="ssm_bwd",
    )(proj, bias, decay, marks, seg_col, skip, up_t, y_t, states)


def pad_to(value, multiple):
    return -(-value // multiple) * multiple


def place_columns(block, start, width):
    return jnp.pad(block, ((0, 0), (start, width - start - block.shape[1])))


def peers(devices, k):
    return [(i, i ^ k) for i in range(devices)]


def one_hot(rows, cols, wanted):
    row = wanted(jnp.arange(rows, dtype=jnp.int32))
    return (row[:, None] == jnp.arange(cols, dtype=jnp.int32)[None, :]).astype(bf16)


def tie(*values):
    return lax.optimization_barrier(values)


def row_major(value):
    return with_layout_constraint(value, Layout(tuple(range(value.ndim))))


def send_to_peers(parts):
    devices = lax.axis_size("fsdp")
    return [lax.ppermute(parts[k - 1], "fsdp", peers(devices, k)) for k in range(1, devices)]


def place_blocks(own, received):
    devices, mine = lax.axis_size("fsdp"), lax.axis_index("fsdp")
    result = jnp.broadcast_to(own[None], (devices,) + own.shape)
    for k in range(1, devices):
        result = lax.dynamic_update_index_in_dim(result, received[k - 1], mine ^ k, 0)
    return result


def take_blocks(blocks):
    devices, mine = lax.axis_size("fsdp"), lax.axis_index("fsdp")
    return [lax.dynamic_index_in_dim(blocks, mine ^ k, 0, False) for k in range(devices)]


def exchange(blocks):
    parts = take_blocks(blocks)
    return place_blocks(parts[0], send_to_peers(parts[1:]))


def gather_rows(part, hold=lambda received: received):
    devices = lax.axis_size("fsdp")
    received = hold(send_to_peers([part] * (devices - 1)))
    return place_blocks(part, received).reshape((devices * part.shape[0],) + part.shape[1:])


def add_up(own, received):
    total = own.astype(f32)
    for part in received:
        total = total + part.astype(f32)
    return total


def row_blocks(partial):
    devices = lax.axis_size("fsdp")
    return partial.reshape((devices, partial.shape[0] // devices) + partial.shape[1:])


def scatter_rows(partial):
    parts = take_blocks(row_blocks(partial))
    return add_up(parts[0], send_to_peers(parts[1:]))


def all_sum(value):
    for axis in ("fsdp", "rep"):
        devices, k = lax.axis_size(axis), 1
        while k < devices:
            value = value + lax.ppermute(value, axis, peers(devices, k))
            k *= 2
    return value


def local(
    tokens,
    lengths,
    w_query,
    w_key,
    w_value,
    w_attn_out,
    w_inner,
    w_gate_z,
    w_bc,
    w_step,
    w_mamba_out,
    w_ffn_gate,
    w_ffn_up,
    w_ffn_down,
    norm_gains,
    step_bias,
    decay_log,
    skip_gain,
    cotangent,
):
    F, R = lax.axis_size("fsdp"), lax.axis_size("rep")
    mine = lax.axis_index("fsdp")
    rows = tokens.shape[0]
    group = rows * F
    aligned = D % (F * R) == 0 and FF % (F * R) == 0
    depth = D // (F * R) if aligned else D // F

    heads_q = -(-QUERY_HEADS // F)
    width_q = heads_q * HEAD_SIZE
    per_dev = MI // F
    first_head = [per_dev * d // HEAD_SIZE for d in range(F)]
    shift = [per_dev * d % HEAD_SIZE for d in range(F)]
    heads_s = max(-(-(s + per_dev) // HEAD_SIZE) for s in shift)
    channels = heads_s * HEAD_SIZE
    at_small = 2 * channels
    at_step = at_small + 2 * NS
    width_att = 2 * KV + width_q
    width_ssm = at_small + 64
    hidden_dev = FF // F
    blocks = R if aligned else 1
    rows_o, rows_m, rows_f = (D // F // blocks, per_dev // blocks, hidden_dev // blocks)
    pad_o, pad_m, pad_f = (pad_to(n, 8) for n in (rows_o, rows_m, rows_f))
    width_f = blocks * pad_f

    if aligned:

        def old_place(n):
            return (n // depth % F) * (R * depth) + n // (F * depth) * depth + n % depth

        order = one_hot(D, D, old_place)

        def permute(v):
            return dot(v, order, 1, 1).astype(v.dtype)

        def restore(v):
            return dot(v, order, 1, 0).astype(v.dtype)

        gains = norm_gains.reshape(4, F, R, depth).transpose(0, 2, 1, 3).reshape(4, D)
    else:

        def permute(v):
            return v

        restore = permute
        gains = norm_gains

    def pad_rows(matrix, height):
        return jnp.pad(matrix, ((0, height - matrix.shape[0]), (0, 0)))

    def rep_gather(flat, width):
        return lax.all_gather(flat, "rep", axis=0, tiled=True).reshape(-1, width)

    def read(flat, width):
        return flat.reshape(depth, width) if aligned else rep_gather(flat, width)

    def collect(part):
        if aligned:
            part = part.reshape(F * depth, part.shape[2])
            return lax.all_gather(part, "rep", axis=0, tiled=True)
        return part.reshape(D, part.shape[2])

    index = jnp.arange(group, dtype=jnp.int32)
    segment, place = sequence_layout(lengths[0], index)
    frequency = jnp.exp(
        jnp.arange(HEAD_SIZE // 2, dtype=f32) * (-2.0 * math.log(10000.0) / HEAD_SIZE)
    )
    angles = frequency[:, None] * place[None, :]
    cosine, sine = jnp.cos(angles), jnp.sin(angles)
    seg_row, seg_col = segment[None, :], segment[:, None]
    by_chunk = segment.reshape(group // CHUNK, CHUNK)
    last = by_chunk[:, -1:]
    prior = jnp.concatenate([jnp.full((1, 1), -1, jnp.int32), last[:-1]], axis=0)
    marks = jnp.stack(
        [
            by_chunk,
            (by_chunk == prior).astype(jnp.int32),
            (by_chunk == last).astype(jnp.int32),
            jnp.broadcast_to((last == prior).astype(jnp.int32), by_chunk.shape),
        ]
    ).reshape(4, group)
    marks = jnp.concatenate([marks, jnp.zeros((4, group), jnp.int32)], axis=0).astype(f32)
    seg_col_f = seg_col.astype(f32)
    distance = jnp.arange(F, dtype=jnp.int32) ^ mine
    kvmap = jnp.minimum(mine * heads_q + jnp.arange(heads_q), QUERY_HEADS - 1) // HEADS_PER_GROUP
    kvmap = jnp.concatenate([kvmap.astype(jnp.int32), distance.astype(jnp.int32)])

    both = permute(jnp.concatenate([tokens, cotangent], axis=0))
    x_float = both[:rows].astype(f32)
    cot = both[rows:]
    normed_own = rms_scale(x_float, gains[0]).astype(bf16)

    if aligned:
        down_shards = jnp.concatenate(
            [
                pad_rows(w_attn_out.reshape(rows_o, D), pad_o),
                pad_rows(w_mamba_out.reshape(rows_m, D), pad_m),
                pad_rows(w_ffn_down.reshape(rows_f, D), pad_f),
            ],
            axis=0,
        )
        down_shards = permute(down_shards)
        down_shards, w_inner, w_gate_z, w_query = tie(down_shards, w_inner, w_gate_z, w_query)
        out_both = lax.all_gather(down_shards[: pad_o + pad_m], "rep", axis=0)
        w_o_part = out_both[:, :rows_o].reshape(R * rows_o, D)
        w_m_part = out_both[:, pad_o:].reshape(R * pad_m, D)
        down_late = down_shards[pad_o + pad_m :]
    else:
        w_o_part, w_m_part = rep_gather(w_attn_out, D), rep_gather(w_mamba_out, D)
        down_late = w_ffn_down

    wq, wk, wv = read(w_query, D), read(w_key, KV), read(w_value, KV)
    wx, wz = read(w_inner, MI), read(w_gate_z, MI)
    wbc, wdt = read(w_bc, 2 * NS), read(w_step, MH)
    wq = place_columns(wq, 0, F * width_q)
    column_blocks = []
    for d in range(F):
        cols = slice(per_dev * d, per_dev * (d + 1))
        column_blocks.append(
            jnp.concatenate(
                [
                    wk,
                    wv,
                    wq[:, width_q * d : width_q * (d + 1)],
                    place_columns(wx[:, cols], shift[d], channels),
                    place_columns(wz[:, cols], shift[d], channels),
                    wbc,
                    place_columns(
                        wdt[:, first_head[d] : first_head[d] + heads_s], 0, width_ssm - at_step
                    ),
                ],
                axis=1,
            )
        )
    in_sent = take_blocks(jnp.stack(column_blocks))
    in_got = send_to_peers(in_sent[1:])
    normed_own, in_sent[0] = tie(normed_own, in_sent[0])
    normed_got = tie(*send_to_peers([normed_own] * (F - 1)))
    in_got, w_ffn_gate, w_ffn_up = tie(in_got, w_ffn_gate, w_ffn_up)
    in_part = place_blocks(in_sent[0], in_got)
    spread_f = one_hot(
        width_f,
        hidden_dev,
        lambda c: jnp.where(c % pad_f < rows_f, c // pad_f * rows_f + c % pad_f, -1),
    )
    gate_up = jnp.stack([read(w_ffn_gate, FF), read(w_ffn_up, FF)])
    gate_up = gate_up.reshape(2, depth, F, hidden_dev).transpose(2, 1, 0, 3)
    if width_f != hidden_dev:
        gate_up = dot(gate_up.reshape(-1, hidden_dev), spread_f, 1, 1).astype(bf16)
    gate_up = gate_up.reshape(F, depth, 2 * width_f)
    normed = place_blocks(normed_own, normed_got).reshape(group, D)
    w_o_sent, normed = tie(w_o_part, normed)
    w_o_got = send_to_peers([w_o_sent] * (F - 1))
    w_att = collect(in_part[:, :, :width_att])
    w_ssm = collect(in_part[:, :, width_att:])

    proj_att = dot(w_att, normed, 0, 1)
    attn_args = (cosine, sine, seg_row, seg_col)
    attn_t, q_t, k_t, k_n, v_n = attn_fwd(
        kvmap, proj_att.reshape(-1, HEAD_SIZE, group), *attn_args, F
    )
    attn_t, w_o_got = tie(attn_t, w_o_got)
    attn_parts = take_blocks(attn_t.reshape(F, width_q, rows))
    attn_got = send_to_peers(attn_parts[1:])
    attn_parts[0], cot_sent = tie(attn_parts[0], cot)
    cot_parts = send_to_peers([cot_sent] * (F - 1))
    own_shift = (mine * per_dev) % HEAD_SIZE
    own_head = (mine * per_dev) // HEAD_SIZE

    def channel_source(c):
        c = c - own_shift
        return jnp.where((c >= 0) & (c < per_dev), c // rows_m * pad_m + c % rows_m, -1)

    spread_m = one_hot(channels, blocks * pad_m, channel_source)
    w_m = dot(spread_m, w_m_part, 1, 0).astype(bf16)

    proj_ssm = dot(w_ssm, normed, 0, 1)

    attn_got, gate_up, proj_ssm = tie(attn_got, gate_up, proj_ssm)
    gate_up = take_blocks(gate_up)
    gate_up_got = send_to_peers(gate_up[1:])
    w_gu = collect(place_blocks(gate_up[0], gate_up_got))
    if aligned:
        w_down = lax.all_gather(down_late, "rep", axis=0, tiled=True)
    else:
        w_down = rep_gather(down_late, D)

    def own_heads(v):
        v = jnp.pad(v, (0, STEP_ROWS))
        return lax.dynamic_slice_in_dim(v, own_head, STEP_ROWS, 0)

    ssm_args = (
        proj_ssm,
        own_heads(step_bias)[:, None],
        jnp.exp(own_heads(decay_log))[:, None],
        marks,
        seg_col_f,
        own_heads(skip_gain),
    )
    y_t, mixed_t, states = ssm_fwd(heads_s, *ssm_args)
    mixed_t, cot_parts = tie(mixed_t, cot_parts)
    mamba_parts = take_blocks(row_blocks(row_major(dot(mixed_t, w_m, 0, 0).astype(bf16))))
    mamba_got = send_to_peers(mamba_parts[1:])

    w_o_got, attn_got, mamba_parts[0] = tie(w_o_got, attn_got, mamba_parts[0])
    w_o = row_major(place_blocks(w_o_sent, w_o_got)).reshape(D, D)
    attn_tok = row_major(place_blocks(attn_parts[0], attn_got)).reshape(F * width_q, rows)[:D]
    attn_proj = dot(attn_tok, w_o, 0, 0)
    branch_attn = rms_scale(attn_proj, gains[1])
    mamba_got, branch_attn = tie(mamba_got, branch_attn)
    mamba_proj = add_up(mamba_parts[0], mamba_got)
    branch_mamba = rms_scale(mamba_proj, gains[2])
    mix = x_float + 0.5 * (branch_attn + branch_mamba)

    def by_distance(own, received):
        return jnp.concatenate([own] + list(received), axis=0)

    def scatter_start(partial):
        parts = [partial[rows * k : rows * (k + 1)] for k in range(F)]
        return parts[0], send_to_peers(parts[1:])

    normed_two = rms_scale(mix, gains[3]).astype(bf16)
    normed_two = by_distance(normed_two, send_to_peers([normed_two] * (F - 1)))
    cot_all = by_distance(cot, cot_parts)
    gate_and_up = dot(normed_two, w_gu, 1, 0)
    fgate, fup = gate_and_up[:, :width_f], gate_and_up[:, width_f:]
    hidden = (silu(fgate) * fup).astype(bf16)
    g_hidden = dot(cot_all, w_down, 1, 1)
    g_fgate = (g_hidden * fup * silu_slope(fgate)).astype(bf16)
    g_fup = (g_hidden * silu(fgate)).astype(bf16)
    g_gu = jnp.concatenate([g_fgate, g_fup], axis=1)
    g_gu, hidden = tie(g_gu, hidden)
    g_two_partial = row_major(dot(g_gu, w_gu, 1, 1).astype(bf16))
    g_two_own, g_two_got = scatter_start(g_two_partial)
    g_gu, hidden, g_two_own = tie(g_gu, hidden, g_two_own)
    grad_gu = dot(normed_two, g_gu, 0, 0).astype(bf16)
    grad_down = row_major(dot(hidden, cot_all, 0, 0).astype(bf16))
    g_two_got, grad_gu, grad_down = tie(g_two_got, grad_gu, grad_down)
    g_mix_norm, g_gain_three = norm_back(add_up(g_two_own, g_two_got), mix, gains[3])
    g_mix = cot.astype(f32) + g_mix_norm

    def over_rep(grad):
        if aligned:
            return lax.psum_scatter(grad, "rep", scatter_dimension=0, tiled=True)
        return grad

    def to_owners(part):
        return exchange(part.reshape(F, depth, part.shape[1]))

    def finish(matrix):
        flat = matrix.reshape(-1)
        if aligned:
            return flat.astype(f32)
        return lax.psum_scatter(flat, "rep", scatter_dimension=0, tiled=True).astype(f32)

    gu_part, down_part = over_rep(grad_gu), over_rep(grad_down)

    g_branch = 0.5 * g_mix
    g_attn_proj, g_gain_one = norm_back(g_branch, attn_proj, gains[1])
    g_attn_proj = g_attn_proj.astype(bf16)
    g_mamba_proj, g_gain_two = norm_back(g_branch, mamba_proj, gains[2])
    g_mamba_proj = g_mamba_proj.astype(bf16)
    g_attn_tok = row_major(dot(w_o, g_attn_proj, 1, 1).astype(bf16))
    g_attn_tok, attn_late, hidden = tie(g_attn_tok, attn_tok, hidden)
    g_attn_parts = jnp.pad(g_attn_tok, ((0, F * width_q - D), (0, 0)))
    g_attn_parts = take_blocks(g_attn_parts.reshape(F, heads_q, HEAD_SIZE, rows))
    g_attn_got = send_to_peers(g_attn_parts[1:])
    grad_o = row_major(dot(attn_late, g_attn_proj, 1, 0).astype(bf16))
    grad_o = take_blocks(row_blocks(grad_o))
    out_partial = row_major(dot(hidden, w_down, 1, 0).astype(bf16))
    g_attn_got, grad_o, out_partial = tie(g_attn_got, grad_o, out_partial)
    g_mamba_sent, g_attn_got = tie(g_mamba_proj, g_attn_got)
    g_mamba_got = send_to_peers([g_mamba_sent] * (F - 1))
    g_attn_blocks = jnp.stack([g_attn_parts[0]] + g_attn_got)
    g_att = attn_bwd(kvmap, g_attn_blocks, q_t, k_n, k_t, v_n, *attn_args)
    g_att = g_att.reshape(width_att, group)
    g_mamba_got, g_att, out_partial = tie(g_mamba_got, g_att, out_partial)
    out_own, out_got = scatter_start(out_partial)
    g_mamba_all = place_blocks(g_mamba_sent, g_mamba_got).reshape(group, D)
    g_gated = dot(w_m, g_mamba_all, 1, 1)
    grad_m = row_major(dot(mixed_t, g_mamba_all, 1, 0).astype(bf16))
    grad_m = row_major(dot(spread_m, grad_m, 0, 0).astype(bf16))
    g_gated, grad_m = tie(g_gated, grad_m)
    g_ssm, sums = ssm_bwd(heads_s, *ssm_args, g_gated, y_t, states)

    out_got, g_ssm, gu_part, down_part, grad_o = tie(out_got, g_ssm, gu_part, down_part, grad_o)
    grad_o_got = send_to_peers(grad_o[1:])
    g_in = jnp.concatenate([g_att, g_ssm], axis=0)
    grad_in = dot(normed, g_in, 0, 1).astype(bf16)
    g_att, g_ssm, grad_in = tie(g_att, g_ssm, grad_in)
    in_part = over_rep(grad_in)
    g_normed = dot(g_att, w_att, 0, 1) + dot(g_ssm, w_ssm, 0, 1)
    g_normed, grad_o_got = tie(row_major(g_normed.astype(bf16)), grad_o_got)
    g_normed = take_blocks(row_blocks(g_normed))
    g_normed_got = send_to_peers(g_normed[1:])
    grad_o = add_up(grad_o[0], grad_o_got).astype(bf16)
    if aligned:
        grad_o = jnp.pad(grad_o.reshape(R, rows_o, D), ((0, 0), (0, pad_o - rows_o), (0, 0)))
        joined = jnp.concatenate([grad_o, grad_m.reshape(R, pad_m, D)], axis=1)
        g_normed_got, gu_part, in_part, joined = tie(g_normed_got, gu_part, in_part, joined)
        joined = over_rep(joined.reshape(R * (pad_o + pad_m), D))
    g_normed = add_up(g_normed[0], g_normed_got)
    gu_back = to_owners(gu_part).reshape(F, depth, 2, width_f)
    if width_f != hidden_dev:
        gu_back = dot(gu_back.reshape(-1, width_f), spread_f, 1, 0).astype(bf16)
    gu_back = gu_back.reshape(F, depth, 2, hidden_dev).transpose(2, 1, 0, 3)
    grad_gate = finish(gu_back[0].reshape(depth, FF))
    grad_up = finish(gu_back[1].reshape(depth, FF))
    grad_down = finish(restore(down_part)[:rows_f])
    if aligned:
        joined = restore(joined)
        grad_attn_out = finish(joined[:rows_o])
        grad_mamba_out = finish(joined[pad_o : pad_o + rows_m])
    else:
        grad_attn_out, grad_mamba_out = finish(grad_o), finish(grad_m)
    g_x_norm, g_gain_zero = norm_back(g_normed, x_float, gains[0])
    grad_tokens = g_mix + g_x_norm
    output = restore((mix + add_up(out_own, out_got)).astype(bf16))
    if aligned:
        grad_tokens = dot(grad_tokens, order.astype(f32), 1, 0, lax.Precision.HIGH)

    head_sums = jnp.sum(sums, axis=1).reshape(3, STEP_ROWS)
    head_sums = lax.dynamic_update_slice(
        jnp.zeros((3, MH + STEP_ROWS), f32), head_sums, (0, own_head)
    )[:, :MH]
    small = jnp.concatenate(
        [g_gain_zero, g_gain_one, g_gain_two, g_gain_three, head_sums.reshape(-1)]
    )
    in_back = to_owners(in_part)
    att_back, ssm_back = in_back[:, :, :width_att], in_back[:, :, width_att:]
    wide_att = att_back[:, :, : 2 * KV].astype(f32)
    grad_query = jnp.concatenate([att_back[d][:, 2 * KV :] for d in range(F)], axis=1)
    grad_query = finish(grad_query[:, :D])
    grad_key = finish(jnp.sum(wide_att[:, :, :KV], axis=0))
    grad_value = finish(jnp.sum(wide_att[:, :, KV:], axis=0))

    wide_ssm = ssm_back[:, :, at_small:].astype(f32)

    def channel_columns(start):
        return finish(
            jnp.concatenate(
                [
                    ssm_back[d][:, start + shift[d] : start + shift[d] + per_dev]
                    for d in range(F)
                ],
                axis=1,
            )
        )

    grad_inner = channel_columns(0)
    grad_gate_z = channel_columns(channels)
    grad_bc = finish(jnp.sum(wide_ssm[:, :, : 2 * NS], axis=0))
    grad_step = finish(
        sum(
            place_columns(wide_ssm[d][:, 2 * NS : 2 * NS + heads_s], first_head[d], MH)
            for d in range(F)
        )
    )

    small_rows = pad_to(small.shape[0], 1024) // 128
    small = jnp.pad(small, (0, small_rows * 128 - small.shape[0])).reshape(small_rows, 128)
    small = all_sum(small).reshape(-1)
    gain_grads = small[: 4 * D].reshape(4, D)
    bias_grad, decay_grad, skip_grad = (
        small[4 * D + MH * i : 4 * D + MH * (i + 1)] for i in range(3)
    )
    if aligned:
        gain_grads = gain_grads.reshape(4, R, F, depth).transpose(0, 2, 1, 3).reshape(4, D)
    return (
        output,
        grad_tokens,
        grad_query,
        grad_key,
        grad_value,
        grad_attn_out,
        grad_inner,
        grad_gate_z,
        grad_bc,
        grad_step,
        grad_mamba_out,
        grad_gate,
        grad_up,
        grad_down,
        gain_grads,
        bias_grad,
        decay_grad,
        skip_grad,
    )


def solution(mesh):
    split_tokens = P(("rep", "fsdp"), None)
    flat = P(("fsdp", "rep"))
    placed = (split_tokens, P("rep", None)) + (flat,) * 12 + (P(),) * 4 + (split_tokens,)
    return jax.shard_map(
        local,
        mesh=mesh,
        in_specs=placed,
        out_specs=(split_tokens, split_tokens) + (flat,) * 12 + (P(),) * 4,
        check_vma=False,
    )
```

```python
import functools
import math

import jax
import jax.numpy as jnp
from jax import lax
from jax.experimental import pallas as pl
from jax.experimental.layout import Layout, with_layout_constraint
from jax.experimental.pallas import tpu as pltpu
from jax.sharding import PartitionSpec as P

D = 1600
QUERY_HEADS = 25
KEY_VALUE_HEADS = 5
HEAD_SIZE = 64
WIN = 1024
MI = 3200
NS = 16
FF = 5504
MH = 50
KV = KEY_VALUE_HEADS * HEAD_SIZE
HEADS_PER_GROUP = QUERY_HEADS // KEY_VALUE_HEADS
SCALE = HEAD_SIZE ** (-0.5)
CHUNK = 128
QUERY_BLOCK = 256
STEP_ROWS = 16
VMEM_BYTES = 50 * 1024 * 1024

epsilon = 1e-06
masked_score = -1e30
highest = lax.Precision.HIGHEST
f32 = jnp.float32
bf16 = jnp.bfloat16


def rms_scale(value_rows, gain):
    return (
        value_rows
        * lax.rsqrt(jnp.mean(value_rows * value_rows, axis=-1, keepdims=True) + epsilon)
        * gain
    )


def norm_back(grad_in, value_rows, gain):
    factor = lax.rsqrt(jnp.mean(value_rows * value_rows, axis=-1, keepdims=True) + epsilon)
    weighted = grad_in * gain
    spread = jnp.mean(weighted * value_rows, axis=-1, keepdims=True)
    return (
        factor * weighted - value_rows * factor * factor * factor * spread,
        jnp.sum(grad_in * value_rows * factor, axis=0),
    )


def silu(value_rows):
    return value_rows * jax.nn.sigmoid(value_rows)


def silu_slope(value_rows):
    sigmoid_v = jax.nn.sigmoid(value_rows)
    return sigmoid_v * (1.0 + value_rows * (1.0 - sigmoid_v))


def dot(a, b, ca, cb, precision=None):
    return lax.dot_general(
        a, b, (((ca,), (cb,)), ((), ())), precision=precision, preferred_element_type=f32
    )


def sequence_layout(seq_lengths, position):
    seq_ends = jnp.cumsum(seq_lengths, dtype=jnp.int32)
    seq_starts = seq_ends - seq_lengths
    segment = jnp.sum(
        (position[:, None] >= seq_ends[None, :]).astype(jnp.int32), axis=1, dtype=jnp.int32
    )
    labels = jnp.arange(seq_lengths.shape[0], dtype=jnp.int32)
    seq_begin = jnp.sum(
        jnp.where(segment[:, None] == labels[None, :], seq_starts[None, :], 0),
        axis=1,
        dtype=jnp.int32,
    )
    return (segment, (position - seq_begin).astype(f32))


def key_range(i):
    low = max(0, i * QUERY_BLOCK - (WIN - 1)) // QUERY_BLOCK * QUERY_BLOCK
    return low, (i + 1) * QUERY_BLOCK


def fill_mask(seg_col, seg_row, mask, blocks):
    for i in range(blocks):
        low, high = key_range(i)
        cols = slice(i * QUERY_BLOCK, (i + 1) * QUERY_BLOCK)
        shape = (high - low, QUERY_BLOCK)
        key = lax.broadcasted_iota(jnp.int32, shape, 0) + low
        query = lax.broadcasted_iota(jnp.int32, shape, 1) + i * QUERY_BLOCK
        gap = query - key
        visible = (seg_col[low:high, :] == seg_row[:, cols]) & (gap >= 0) & (gap < WIN)
        mask[low:high, cols] = jnp.where(visible, 0.0, masked_score)


def rotate(value, cosine, sine):
    half = HEAD_SIZE // 2
    a, b = value[:half], value[half:]
    return jnp.concatenate([a * cosine - b * sine, b * cosine + a * sine], axis=0)


def attn_fwd_kernel(
    kvmap, kv_ref, q_ref, cosine, sine, seg_row, seg_col, o_ref, qt_ref, kt_ref, kn_ref, vn_ref, mask, vt, *, blocks
):
    h = pl.program_id(0)

    @pl.when(h == 0)
    def _():
        fill_mask(seg_col, seg_row, mask, blocks)
        for c in range(KEY_VALUE_HEADS):
            k = rotate(kv_ref[c], cosine[...], sine[...])
            kt_ref[c] = k.astype(bf16)
            kn_ref[c] = k.T.astype(bf16)
            v = kv_ref[KEY_VALUE_HEADS + c]
            vt[c] = v.astype(bf16)
            vn_ref[c] = v.T.astype(bf16)

    kv = kvmap[h]
    tokens = o_ref.shape[3]
    for i in range(blocks):
        low, high = key_range(i)
        start, stop = i * QUERY_BLOCK, (i + 1) * QUERY_BLOCK
        cols = slice(start, stop)
        q = (rotate(q_ref[0, :, cols], cosine[:, cols], sine[:, cols]) * SCALE).astype(bf16)
        qt_ref[0, :, cols] = q
        s = dot(kn_ref[kv, low:high, :], q, 1, 0) + mask[low:high, cols]
        p = jnp.exp(s - jnp.max(s, axis=0, keepdims=True))
        total = jnp.sum(p, axis=0, keepdims=True)
        o = dot(vt[kv, :, low:high], p.astype(bf16), 1, 0)
        o = (o / total).astype(bf16)
        for d in range(o_ref.shape[0]):
            first, last = max(start, d * tokens), min(stop, (d + 1) * tokens)
            if first < last:
                part = o[:, first - start : last - start]
                o_ref[d, 0, :, first - d * tokens : last - d * tokens] = part


def attn_fwd(kvmap, proj, cosine, sine, seg_row, seg_col, devices):
    heads = proj.shape[0] - 2 * KEY_VALUE_HEADS
    group = proj.shape[2]
    tokens = group // devices
    per_head = pl.BlockSpec((1, HEAD_SIZE, group), lambda h, m: (h, 0, 0))
    angle = pl.BlockSpec((HEAD_SIZE // 2, group), lambda h, m: (0, 0))
    kv_t = (KEY_VALUE_HEADS, HEAD_SIZE, group)
    kv_n = (KEY_VALUE_HEADS, group, HEAD_SIZE)
    whole_t = pl.BlockSpec(kv_t, lambda h, m: (0, 0, 0))
    whole_n = pl.BlockSpec(kv_n, lambda h, m: (0, 0, 0))
    return pl.pallas_call(
        functools.partial(attn_fwd_kernel, blocks=group // QUERY_BLOCK),
        out_shape=(
            jax.ShapeDtypeStruct((devices, heads, HEAD_SIZE, tokens), bf16),
            jax.ShapeDtypeStruct((heads, HEAD_SIZE, group), bf16),
            jax.ShapeDtypeStruct(kv_t, bf16),
            jax.ShapeDtypeStruct(kv_n, bf16),
            jax.ShapeDtypeStruct(kv_n, bf16),
        ),
        grid_spec=pltpu.PrefetchScalarGridSpec(
            num_scalar_prefetch=1,
            grid=(heads,),
            in_specs=[
                pl.BlockSpec((2 * KEY_VALUE_HEADS, HEAD_SIZE, group), lambda h, m: (0, 0, 0)),
                pl.BlockSpec((1, HEAD_SIZE, group), lambda h, m: (h + 2 * KEY_VALUE_HEADS, 0, 0)),
                angle,
                angle,
                pl.BlockSpec((1, group), lambda h, m: (0, 0)),
                pl.BlockSpec((group, 1), lambda h, m: (0, 0)),
            ],
            out_specs=(
                pl.BlockSpec((devices, 1, HEAD_SIZE, tokens), lambda h, m: (0, h, 0, 0)),
                per_head,
                whole_t,
                whole_n,
                whole_n,
            ),
            scratch_shapes=[pltpu.VMEM((group, group), f32), pltpu.VMEM(kv_t, bf16)],
        ),
        compiler_params=pltpu.CompilerParams(vmem_limit_bytes=VMEM_BYTES),
        cost_estimate=pl.CostEstimate(
            flops=group * group, bytes_accessed=group * HEAD_SIZE, transcendentals=group,
        ),
        name="attn_fwd",
    )(kvmap, proj, proj, cosine, sine, seg_row, seg_col)


def attn_bwd_kernel(kvmap, *refs, blocks, devices):
    do_parts = refs[:devices]
    q_ref, kn_ref, kt_ref, vn_ref, cosine, sine, seg_row, seg_col = refs[devices : devices + 8]
    g_ref, mask, dk, dv, do_all = refs[devices + 8 :]
    h = pl.program_id(0)

    @pl.when(h == 0)
    def _():
        fill_mask(seg_col, seg_row, mask, blocks)
        dk[...] = jnp.zeros(dk.shape, f32)
        dv[...] = jnp.zeros(dv.shape, f32)

    kv = kvmap[h]
    tokens = do_parts[0].shape[3]
    for d in range(devices):
        do_all[:, d * tokens : (d + 1) * tokens] = do_parts[d][0, 0]
    for i in range(blocks):
        low, high = key_range(i)
        cols = slice(i * QUERY_BLOCK, (i + 1) * QUERY_BLOCK)
        q = q_ref[0, :, cols]
        do = do_all[:, cols]
        s = dot(kn_ref[kv, low:high, :], q, 1, 0) + mask[low:high, cols]
        p = jnp.exp(s - jnp.max(s, axis=0, keepdims=True))
        p = p * (1.0 / jnp.sum(p, axis=0, keepdims=True))
        dp = dot(vn_ref[kv, low:high, :], do, 1, 0)
        delta = jnp.sum(p * dp, axis=0, keepdims=True)
        ds = (p * (dp - delta)).astype(bf16)
        dv[kv, low:high, :] += dot(p.astype(bf16), do, 1, 1)
        dk[kv, low:high, :] += dot(ds, q, 1, 1)
        dq = dot(kt_ref[kv, :, low:high], ds, 1, 0) * SCALE
        dq = rotate(dq, cosine[:, cols], -sine[:, cols])
        g_ref[2 * KEY_VALUE_HEADS + h, :, cols] = dq.astype(bf16)

    @pl.when(h == pl.num_programs(0) - 1)
    def _():
        for c in range(KEY_VALUE_HEADS):
            g_ref[c] = rotate(dk[c].T, cosine[...], -sine[...]).astype(bf16)
            g_ref[KEY_VALUE_HEADS + c] = dv[c].T.astype(bf16)


def attn_bwd(kvmap, do_blocks, q_t, k_n, k_t, v_n, cosine, sine, seg_row, seg_col):
    devices, heads, _, tokens = do_blocks.shape
    group = q_t.shape[2]
    angle = pl.BlockSpec((HEAD_SIZE // 2, group), lambda h, m: (0, 0))
    kv_t = (KEY_VALUE_HEADS, HEAD_SIZE, group)
    kv_n = (KEY_VALUE_HEADS, group, HEAD_SIZE)
    whole_n = pl.BlockSpec(kv_n, lambda h, m: (0, 0, 0))
    out = (2 * KEY_VALUE_HEADS + heads, HEAD_SIZE, group)

    def block_spec(d):
        return pl.BlockSpec((1, 1, HEAD_SIZE, tokens), lambda h, m: (m[heads + d], h, 0, 0))

    return pl.pallas_call(
        functools.partial(attn_bwd_kernel, blocks=group // QUERY_BLOCK, devices=devices),
        out_shape=jax.ShapeDtypeStruct(out, bf16),
        grid_spec=pltpu.PrefetchScalarGridSpec(
            num_scalar_prefetch=1,
            grid=(heads,),
            in_specs=[block_spec(d) for d in range(devices)]
            + [
                pl.BlockSpec((1, HEAD_SIZE, group), lambda h, m: (h, 0, 0)),
                whole_n,
                pl.BlockSpec(kv_t, lambda h, m: (0, 0, 0)),
                whole_n,
                angle,
                angle,
                pl.BlockSpec((1, group), lambda h, m: (0, 0)),
                pl.BlockSpec((group, 1), lambda h, m: (0, 0)),
            ],
            out_specs=pl.BlockSpec(out, lambda h, m: (0, 0, 0)),
            scratch_shapes=[
                pltpu.VMEM((group, group), f32),
                pltpu.VMEM(kv_n, f32),
                pltpu.VMEM(kv_n, f32),
                pltpu.VMEM((HEAD_SIZE, group), bf16),
            ],
        ),
        compiler_params=pltpu.CompilerParams(vmem_limit_bytes=VMEM_BYTES),
        cost_estimate=pl.CostEstimate(
            flops=group * group, bytes_accessed=group * HEAD_SIZE, transcendentals=group,
        ),
        name="attn_bwd",
    )(kvmap, *([do_blocks] * devices), q_t, k_n, k_t, v_n, cosine, sine, seg_row, seg_col)


def block_setup(p_ref, bias, decay, marks, seg_col, channels):
    at = 2 * channels
    b_t = p_ref[at : at + NS].astype(bf16)
    c_t = p_ref[at + NS : at + 2 * NS].astype(bf16)
    raw = p_ref[at + 2 * NS : at + 2 * NS + STEP_ROWS] + bias[...]
    step = jnp.maximum(raw, 0.0) + jnp.log1p(jnp.exp(-jnp.abs(raw)))
    rate = -step * decay[...]
    rows = lax.broadcasted_iota(jnp.int32, (CHUNK, CHUNK), 0)
    cols = lax.broadcasted_iota(jnp.int32, (CHUNK, CHUNK), 1)
    a_t = dot(rate, (rows <= cols).astype(f32), 1, 0, highest)
    a_n = a_t.T
    visible = (seg_col[...] == marks[0:1]) & (rows <= cols)
    hidden = jnp.where(visible, 0.0, masked_score)
    return b_t, c_t, raw, step, rate, a_t, a_n, rows, cols, hidden


def ssm_fwd_kernel(p_ref, bias, decay, marks, seg_col, skip, y_ref, mixed_ref, states, state, *, heads):
    channels = heads * HEAD_SIZE

    @pl.when(pl.program_id(0) == 0)
    def _():
        state[...] = jnp.zeros(state.shape, f32)

    states[0] = state[...]
    b_t, c_t, _, step, _, a_t, a_n, _, _, hidden = block_setup(
        p_ref, bias, decay, marks, seg_col, channels
    )
    block = dot(b_t, c_t, 0, 0)
    enter, leave, through = marks[1:2], marks[2:3], marks[3:4, 0:1]
    for h in range(heads):
        at = slice(h * HEAD_SIZE, (h + 1) * HEAD_SIZE)
        a_row = a_t[h : h + 1]
        a_end = a_t[h : h + 1, CHUNK - 1 :]
        x = p_ref[at].astype(bf16).astype(f32)
        z = p_ref[channels + h * HEAD_SIZE : channels + (h + 1) * HEAD_SIZE]
        mixing = (jnp.exp(a_row - a_n[:, h : h + 1] + hidden) * block).astype(bf16)
        xs = x * step[h : h + 1]
        y = dot(xs.astype(bf16), mixing, 1, 0)
        s = state[at]
        y = y + dot(s.astype(bf16), c_t, 1, 0) * (enter * jnp.exp(a_row)) + skip[h] * x
        y_ref[at] = y
        mixed_ref[at] = (y * silu(z)).astype(bf16)
        xw = (xs * (leave * jnp.exp(a_end - a_row))).astype(bf16)
        state[at] = through * jnp.exp(a_end) * s + dot(xw, b_t, 1, 1)


def ssm_specs(height, order):
    column = pl.BlockSpec((STEP_ROWS, 1), lambda c: (0, 0))
    return [
        pl.BlockSpec((height, CHUNK), lambda c: (0, order(c))),
        column,
        column,
        pl.BlockSpec((8, CHUNK), lambda c: (0, order(c))),
        pl.BlockSpec((CHUNK, 1), lambda c: (order(c), 0)),
        pl.BlockSpec(memory_space=pltpu.SMEM),
    ]


def ssm_fwd(heads, proj, bias, decay, marks, seg_col, skip):
    height, group = proj.shape
    channels = heads * HEAD_SIZE
    count = group // CHUNK
    by_block = pl.BlockSpec((channels, CHUNK), lambda c: (0, c))
    return pl.pallas_call(
        functools.partial(ssm_fwd_kernel, heads=heads),
        out_shape=(
            jax.ShapeDtypeStruct((channels, group), f32),
            jax.ShapeDtypeStruct((channels, group), bf16),
            jax.ShapeDtypeStruct((count, channels, NS), f32),
        ),
        grid=(count,),
        in_specs=ssm_specs(height, lambda c: c),
        out_specs=(by_block, by_block, pl.BlockSpec((1, channels, NS), lambda c: (c, 0, 0))),
        scratch_shapes=[pltpu.VMEM((channels, NS), f32)],
        compiler_params=pltpu.CompilerParams(vmem_limit_bytes=VMEM_BYTES),
        cost_estimate=pl.CostEstimate(
            flops=group * group, bytes_accessed=group * HEAD_SIZE, transcendentals=group,
        ),
        name="ssm_fwd",
    )(proj, bias, decay, marks, seg_col, skip)


def ssm_bwd_kernel(
    p_ref,
    bias,
    decay,
    marks,
    seg_col,
    skip,
    up_ref,
    y_ref,
    states,
    g_ref,
    sums,
    adjoint,
    after,
    before,
    gstep,
    grate,
    *,
    heads,
):
    channels = heads * HEAD_SIZE

    @pl.when(pl.program_id(0) == 0)
    def _():
        for ref in (adjoint, sums, after, before, gstep, grate):
            ref[...] = jnp.zeros(ref.shape, f32)

    b_t, c_t, raw, step_all, rate_all, a_t, a_n, rows, cols, hidden = block_setup(
        p_ref, bias, decay, marks, seg_col, channels
    )
    block = dot(b_t, c_t, 0, 0)
    enter, leave, through = marks[1:2], marks[2:3], marks[3:4, 0:1]
    from_here = (rows >= cols).astype(f32)
    from_here_low = from_here.astype(bf16)
    strictly = (rows < cols).astype(f32)
    pair_sum = jnp.zeros((CHUNK, CHUNK), f32)
    gc = jnp.zeros((NS, CHUNK), f32)
    gb = jnp.zeros((NS, CHUNK), f32)
    at_skip = 2 * STEP_ROWS
    for h in range(heads):
        at = slice(h * HEAD_SIZE, (h + 1) * HEAD_SIZE)
        at_gate = slice(channels + h * HEAD_SIZE, channels + (h + 1) * HEAD_SIZE)
        one = slice(h, h + 1)
        a_row = a_t[one]
        a_end = a_t[one, CHUNK - 1 :]
        step = step_all[one]
        x = p_ref[at].astype(bf16).astype(f32)
        z = p_ref[at_gate]
        g = up_ref[at]
        sigmoid_z = jax.nn.sigmoid(z)
        gy = g * z * sigmoid_z
        gz = g * y_ref[at] * sigmoid_z * (1.0 + z * (1.0 - sigmoid_z))
        g_ref[at_gate] = gz.astype(bf16)
        sums[at_skip + h : at_skip + h + 1] += jnp.sum(gy * x, axis=0, keepdims=True)
        reach = jnp.exp(a_row - a_n[:, one] + hidden)
        gy_low = gy.astype(bf16)
        xs = x * step
        u = dot(gy_low, (reach * block).astype(bf16), 1, 1)
        lam = adjoint[at]
        lam_low = lam.astype(bf16)
        out_weight = leave * jnp.exp(a_end - a_row)
        u_state = dot(lam_low, b_t, 1, 0) * out_weight
        u = u + u_state
        g_ref[at] = (step * u + skip[h] * gy).astype(bf16)
        gstep[one] = jnp.sum(x * u, axis=0, keepdims=True)
        before[one] = jnp.sum(xs * u_state, axis=0, keepdims=True)
        pairs = dot(xs.astype(bf16), gy_low, 0, 0) * reach
        pair_sum = pair_sum + pairs
        crossing = dot((pairs * block).astype(bf16), from_here_low, 1, 0)
        crossed = jnp.sum(crossing * strictly, axis=0, keepdims=True)
        gyw = gy * (enter * jnp.exp(a_row))
        gyw_low = gyw.astype(bf16)
        s = states[0, at]
        s_low = s.astype(bf16)
        after[one] = jnp.sum(gyw * dot(s_low, c_t, 1, 0), axis=0, keepdims=True)
        gc = gc + dot(s_low, gyw_low, 0, 0)
        gb = gb + dot(lam_low, (xs * out_weight).astype(bf16), 0, 0)
        passing = through * jnp.exp(a_end)
        product = jnp.sum(jnp.sum(lam * s, axis=1, keepdims=True), axis=0, keepdims=True)
        grate[one] = crossed + passing * product
        adjoint[at] = passing * lam + dot(gyw_low, c_t, 1, 1)
    grate_all = (
        grate[...]
        + dot(after[...], from_here, 1, 0, highest)
        + dot(before[...], strictly, 1, 0, highest)
    )
    pair_low = pair_sum.astype(bf16)
    small = 2 * channels
    g_ref[small : small + NS] = (gb + dot(c_t, pair_low, 1, 1)).astype(bf16)
    g_ref[small + NS : small + 2 * NS] = (gc + dot(b_t, pair_low, 1, 0)).astype(bf16)
    graw = (gstep[...] - grate_all * decay[...]) * jax.nn.sigmoid(raw)
    at_step = small + 2 * NS
    g_ref[at_step : at_step + STEP_ROWS] = graw.astype(bf16)
    rest = g_ref.shape[0] - at_step - STEP_ROWS
    g_ref[at_step + STEP_ROWS :] = jnp.zeros((rest, CHUNK), bf16)
    sums[:STEP_ROWS] += graw
    sums[STEP_ROWS:at_skip] += grate_all * rate_all


def ssm_bwd(heads, proj, bias, decay, marks, seg_col, skip, up_t, y_t, states):
    height, group = proj.shape
    channels = heads * HEAD_SIZE
    count = group // CHUNK

    def order(c):
        return count - 1 - c

    by_block = pl.BlockSpec((channels, CHUNK), lambda c: (0, order(c)))
    small = pltpu.VMEM((STEP_ROWS, CHUNK), f32)
    return pl.pallas_call(
        functools.partial(ssm_bwd_kernel, heads=heads),
        out_shape=(
            jax.ShapeDtypeStruct((height, group), bf16),
            jax.ShapeDtypeStruct((3 * STEP_ROWS, CHUNK), f32),
        ),
        grid=(count,),
        in_specs=ssm_specs(height, order)
        + [by_block, by_block, pl.BlockSpec((1, channels, NS), lambda c: (order(c), 0, 0))],
        out_specs=(
            pl.BlockSpec((height, CHUNK), lambda c: (0, order(c))),
            pl.BlockSpec((3 * STEP_ROWS, CHUNK), lambda c: (0, 0)),
        ),
        scratch_shapes=[pltpu.VMEM((channels, NS), f32), small, small, small, small],
        compiler_params=pltpu.CompilerParams(vmem_limit_bytes=VMEM_BYTES),
        cost_estimate=pl.CostEstimate(
            flops=group * group, bytes_accessed=group * HEAD_SIZE, transcendentals=group,
        ),
        name="ssm_bwd",
    )(proj, bias, decay, marks, seg_col, skip, up_t, y_t, states)


def ffn_middle_kernel(gate_up_ref, g_ref, hidden_ref, g_gu_ref):
    width = g_ref.shape[1]
    gate = gate_up_ref[:, :width].astype(f32)
    up = gate_up_ref[:, width:].astype(f32)
    g = g_ref[...].astype(f32)
    sigmoid_v = jax.nn.sigmoid(gate)
    passed = gate * sigmoid_v
    hidden_ref[...] = (passed * up).astype(bf16)
    slope = sigmoid_v * (1.0 + gate * (1.0 - sigmoid_v))
    g_gu_ref[:, :width] = (g * up * slope).astype(bf16)
    g_gu_ref[:, width:] = (g * passed).astype(bf16)


def ffn_middle(gate_up, g_hidden):
    group, width = g_hidden.shape
    height = 128
    narrow = pl.BlockSpec((height, width), lambda i: (i, 0))
    wide = pl.BlockSpec((height, 2 * width), lambda i: (i, 0))
    return pl.pallas_call(
        ffn_middle_kernel,
        out_shape=(
            jax.ShapeDtypeStruct((group, width), bf16),
            jax.ShapeDtypeStruct((group, 2 * width), bf16),
        ),
        grid=(group // height,),
        in_specs=[wide, narrow],
        out_specs=(narrow, wide),
        compiler_params=pltpu.CompilerParams(vmem_limit_bytes=VMEM_BYTES),
        name="ffn_middle",
    )(gate_up, g_hidden)


def weight_grads_kernel(rows_ref, g_ref, hidden_ref, cot_ref, wide_ref, down_ref, *, wide_steps):
    i = pl.program_id(0)

    @pl.when(i < wide_steps)
    def _():
        wide_ref[...] = dot(rows_ref[...], g_ref[...], 0, 0).astype(bf16)

    @pl.when(i >= wide_steps)
    def _():
        down_ref[...] = dot(hidden_ref[...], cot_ref[...], 0, 0).astype(bf16)


def ffn_weight_grads(rows, g_wide, hidden, cot):
    group, depth = rows.shape
    wide, width = g_wide.shape[1], hidden.shape[1]
    columns, height = 256, 128
    if wide % columns or width % height:
        return (
            dot(rows, g_wide, 0, 0).astype(bf16),
            row_major(dot(hidden, cot, 0, 0).astype(bf16)),
        )
    wide_steps, down_steps = wide // columns, width // height

    def first(i):
        return jnp.minimum(i, wide_steps - 1)

    def second(i):
        return jnp.maximum(i - wide_steps, 0)

    whole = pl.BlockSpec((group, depth), lambda i: (0, 0))
    return pl.pallas_call(
        functools.partial(weight_grads_kernel, wide_steps=wide_steps),
        out_shape=(
            jax.ShapeDtypeStruct((depth, wide), bf16),
            jax.ShapeDtypeStruct((width, depth), bf16),
        ),
        grid=(wide_steps + down_steps,),
        in_specs=[
            whole,
            pl.BlockSpec((group, columns), lambda i: (0, first(i))),
            pl.BlockSpec((group, height), lambda i: (0, second(i))),
            whole,
        ],
        out_specs=(
            pl.BlockSpec((depth, columns), lambda i: (0, first(i))),
            pl.BlockSpec((height, depth), lambda i: (second(i), 0)),
        ),
        compiler_params=pltpu.CompilerParams(vmem_limit_bytes=VMEM_BYTES),
        cost_estimate=pl.CostEstimate(flops=group * group, bytes_accessed=group, transcendentals=0),
        name="ffn_weight_grads",
    )(rows, g_wide, hidden, cot)


def pad_to(value, multiple):
    return -(-value // multiple) * multiple


def place_columns(block, start, width):
    return jnp.pad(block, ((0, 0), (start, width - start - block.shape[1])))


def peers(devices, k):
    return [(i, i ^ k) for i in range(devices)]


def one_hot(rows, cols, wanted):
    row = wanted(jnp.arange(rows, dtype=jnp.int32))
    return (row[:, None] == jnp.arange(cols, dtype=jnp.int32)[None, :]).astype(bf16)


def tie(*values):
    return lax.optimization_barrier(values)


def row_major(value):
    return with_layout_constraint(value, Layout(tuple(range(value.ndim))))


def send_to_peers(parts):
    devices = lax.axis_size("fsdp")
    return [lax.ppermute(parts[k - 1], "fsdp", peers(devices, k)) for k in range(1, devices)]


def gather_start(part):
    devices = lax.axis_size("fsdp")
    if devices != 4:
        return send_to_peers([part] * (devices - 1))
    half = part.shape[0] // 2
    one, two = (lax.ppermute(part, "fsdp", peers(devices, k)) for k in (1, 2))
    upper = lax.ppermute(two[:half], "fsdp", peers(devices, 1))
    lower = lax.ppermute(one[half:], "fsdp", peers(devices, 2))
    return [one, two, jnp.concatenate([upper, lower], axis=0)]


def place_blocks(own, received):
    devices, mine = lax.axis_size("fsdp"), lax.axis_index("fsdp")
    result = jnp.broadcast_to(own[None], (devices,) + own.shape)
    for k in range(1, devices):
        result = lax.dynamic_update_index_in_dim(result, received[k - 1], mine ^ k, 0)
    return result


def take_blocks(blocks):
    devices, mine = lax.axis_size("fsdp"), lax.axis_index("fsdp")
    return [lax.dynamic_index_in_dim(blocks, mine ^ k, 0, False) for k in range(devices)]


def exchange(blocks):
    parts = take_blocks(blocks)
    return place_blocks(parts[0], send_to_peers(parts[1:]))


def gather_rows(part, hold=lambda received: received):
    devices = lax.axis_size("fsdp")
    received = hold(send_to_peers([part] * (devices - 1)))
    return place_blocks(part, received).reshape((devices * part.shape[0],) + part.shape[1:])


def add_up(own, received):
    total = own.astype(f32)
    for part in received:
        total = total + part.astype(f32)
    return total


def row_blocks(partial):
    devices = lax.axis_size("fsdp")
    return partial.reshape((devices, partial.shape[0] // devices) + partial.shape[1:])


def scatter_rows(partial):
    parts = take_blocks(row_blocks(partial))
    return add_up(parts[0], send_to_peers(parts[1:]))


def all_sum(value):
    for axis in ("fsdp", "rep"):
        devices, k = lax.axis_size(axis), 1
        while k < devices:
            value = value + lax.ppermute(value, axis, peers(devices, k))
            k *= 2
    return value


def local(
    tokens,
    lengths,
    w_query,
    w_key,
    w_value,
    w_attn_out,
    w_inner,
    w_gate_z,
    w_bc,
    w_step,
    w_mamba_out,
    w_ffn_gate,
    w_ffn_up,
    w_ffn_down,
    norm_gains,
    step_bias,
    decay_log,
    skip_gain,
    cotangent,
):
    F, R = lax.axis_size("fsdp"), lax.axis_size("rep")
    mine = lax.axis_index("fsdp")
    rows = tokens.shape[0]
    group = rows * F
    aligned = D % (F * R) == 0 and FF % (F * R) == 0
    depth = D // (F * R) if aligned else D // F

    heads_q = -(-QUERY_HEADS // F)
    width_q = heads_q * HEAD_SIZE
    per_dev = MI // F
    first_head = [per_dev * d // HEAD_SIZE for d in range(F)]
    shift = [per_dev * d % HEAD_SIZE for d in range(F)]
    heads_s = max(-(-(s + per_dev) // HEAD_SIZE) for s in shift)
    channels = heads_s * HEAD_SIZE
    at_small = 2 * channels
    at_step = at_small + 2 * NS
    width_att = 2 * KV + width_q
    width_ssm = at_small + 64
    hidden_dev = FF // F
    blocks = R if aligned else 1
    rows_o, rows_m, rows_f = (D // F // blocks, per_dev // blocks, hidden_dev // blocks)
    pad_o, pad_m, pad_f = (pad_to(n, 8) for n in (rows_o, rows_m, rows_f))
    width_f = blocks * pad_f

    if aligned:

        def old_place(n):
            return (n // depth % F) * (R * depth) + n // (F * depth) * depth + n % depth

        order = one_hot(D, D, old_place)

        def permute(v):
            return dot(v, order, 1, 1).astype(v.dtype)

        def restore(v):
            return dot(v, order, 1, 0).astype(v.dtype)

        gains = norm_gains.reshape(4, F, R, depth).transpose(0, 2, 1, 3).reshape(4, D)
    else:

        def permute(v):
            return v

        restore = permute
        gains = norm_gains

    def pad_rows(matrix, height):
        return jnp.pad(matrix, ((0, height - matrix.shape[0]), (0, 0)))

    def rep_gather(flat, width):
        return lax.all_gather(flat, "rep", axis=0, tiled=True).reshape(-1, width)

    def read(flat, width):
        return flat.reshape(depth, width) if aligned else rep_gather(flat, width)

    def collect(part):
        if aligned:
            part = part.reshape(F * depth, part.shape[2])
            return lax.all_gather(part, "rep", axis=0, tiled=True)
        return part.reshape(D, part.shape[2])

    index = jnp.arange(group, dtype=jnp.int32)
    segment, place = sequence_layout(lengths[0], index)
    frequency = jnp.exp(
        jnp.arange(HEAD_SIZE // 2, dtype=f32) * (-2.0 * math.log(10000.0) / HEAD_SIZE)
    )
    angles = frequency[:, None] * place[None, :]
    cosine, sine = jnp.cos(angles), jnp.sin(angles)
    seg_row, seg_col = segment[None, :], segment[:, None]
    by_chunk = segment.reshape(group // CHUNK, CHUNK)
    last = by_chunk[:, -1:]
    prior = jnp.concatenate([jnp.full((1, 1), -1, jnp.int32), last[:-1]], axis=0)
    marks = jnp.stack(
        [
            by_chunk,
            (by_chunk == prior).astype(jnp.int32),
            (by_chunk == last).astype(jnp.int32),
            jnp.broadcast_to((last == prior).astype(jnp.int32), by_chunk.shape),
        ]
    ).reshape(4, group)
    marks = jnp.concatenate([marks, jnp.zeros((4, group), jnp.int32)], axis=0).astype(f32)
    seg_col_f = seg_col.astype(f32)
    distance = jnp.arange(F, dtype=jnp.int32) ^ mine
    kvmap = jnp.minimum(mine * heads_q + jnp.arange(heads_q), QUERY_HEADS - 1) // HEADS_PER_GROUP
    kvmap = jnp.concatenate([kvmap.astype(jnp.int32), distance.astype(jnp.int32)])

    both = permute(jnp.concatenate([tokens, cotangent], axis=0))
    x_float = both[:rows].astype(f32)
    cot = both[rows:]
    normed_own = rms_scale(x_float, gains[0]).astype(bf16)

    if aligned:
        down_shards = jnp.concatenate(
            [
                pad_rows(w_attn_out.reshape(rows_o, D), pad_o),
                pad_rows(w_mamba_out.reshape(rows_m, D), pad_m),
                pad_rows(w_ffn_down.reshape(rows_f, D), pad_f),
            ],
            axis=0,
        )
        down_shards = permute(down_shards)
        down_shards, w_inner, w_gate_z, w_query = tie(down_shards, w_inner, w_gate_z, w_query)
        out_both = lax.all_gather(down_shards[: pad_o + pad_m], "rep", axis=0)
        w_o_part = out_both[:, :rows_o].reshape(R * rows_o, D)
        w_m_part = out_both[:, pad_o:].reshape(R * pad_m, D)
        down_late = down_shards[pad_o + pad_m :]
    else:
        w_o_part, w_m_part = rep_gather(w_attn_out, D), rep_gather(w_mamba_out, D)
        down_late = w_ffn_down

    wq, wk, wv = read(w_query, D), read(w_key, KV), read(w_value, KV)
    wx, wz = read(w_inner, MI), read(w_gate_z, MI)
    wbc, wdt = read(w_bc, 2 * NS), read(w_step, MH)
    wq = place_columns(wq, 0, F * width_q)
    column_blocks = []
    for d in range(F):
        cols = slice(per_dev * d, per_dev * (d + 1))
        column_blocks.append(
            jnp.concatenate(
                [
                    wk,
                    wv,
                    wq[:, width_q * d : width_q * (d + 1)],
                    place_columns(wx[:, cols], shift[d], channels),
                    place_columns(wz[:, cols], shift[d], channels),
                    wbc,
                    place_columns(
                        wdt[:, first_head[d] : first_head[d] + heads_s], 0, width_ssm - at_step
                    ),
                ],
                axis=1,
            )
        )
    in_sent = take_blocks(jnp.stack(column_blocks))
    in_got = send_to_peers(in_sent[1:])
    normed_own, in_sent[0] = tie(normed_own, in_sent[0])
    normed_got = tie(*gather_start(normed_own))
    in_got, w_ffn_gate, w_ffn_up = tie(in_got, w_ffn_gate, w_ffn_up)
    in_part = place_blocks(in_sent[0], in_got)
    spread_f = one_hot(
        width_f,
        hidden_dev,
        lambda c: jnp.where(c % pad_f < rows_f, c // pad_f * rows_f + c % pad_f, -1),
    )
    gate_up = jnp.stack([read(w_ffn_gate, FF), read(w_ffn_up, FF)])
    gate_up = gate_up.reshape(2, depth, F, hidden_dev).transpose(2, 1, 0, 3)
    if width_f != hidden_dev:
        gate_up = dot(gate_up.reshape(-1, hidden_dev), spread_f, 1, 1).astype(bf16)
    gate_up = gate_up.reshape(F, depth, 2 * width_f)
    normed = place_blocks(normed_own, normed_got).reshape(group, D)
    w_o_sent, normed_late = tie(w_o_part, normed)
    w_o_got = send_to_peers([w_o_sent] * (F - 1))
    w_att = collect(in_part[:, :, :width_att])
    w_ssm = collect(in_part[:, :, width_att:])

    proj_att = dot(w_att, normed, 0, 1)
    attn_args = (cosine, sine, seg_row, seg_col)
    attn_t, q_t, k_t, k_n, v_n = attn_fwd(
        kvmap, proj_att.reshape(-1, HEAD_SIZE, group), *attn_args, F
    )
    attn_t, w_o_got = tie(attn_t, w_o_got)
    attn_parts = take_blocks(attn_t.reshape(F, width_q, rows))
    attn_got = send_to_peers(attn_parts[1:])
    attn_parts[0], cot_sent = tie(attn_parts[0], cot)
    cot_parts = send_to_peers([cot_sent] * (F - 1))
    own_shift = (mine * per_dev) % HEAD_SIZE
    own_head = (mine * per_dev) // HEAD_SIZE

    def channel_source(c):
        c = c - own_shift
        return jnp.where((c >= 0) & (c < per_dev), c // rows_m * pad_m + c % rows_m, -1)

    spread_m = one_hot(channels, blocks * pad_m, channel_source)
    w_m = dot(spread_m, w_m_part, 1, 0).astype(bf16)

    proj_ssm = dot(w_ssm, normed, 0, 1)

    def own_heads(v):
        v = jnp.pad(v, (0, STEP_ROWS))
        return lax.dynamic_slice_in_dim(v, own_head, STEP_ROWS, 0)

    ssm_args = (
        proj_ssm,
        own_heads(step_bias)[:, None],
        jnp.exp(own_heads(decay_log))[:, None],
        marks,
        seg_col_f,
        own_heads(skip_gain),
    )
    y_t, mixed_t, states = ssm_fwd(heads_s, *ssm_args)
    attn_got, gate_up, mixed_t = tie(attn_got, gate_up, mixed_t)
    gate_up = take_blocks(gate_up)
    gate_up_got = send_to_peers(gate_up[1:])
    w_gu = collect(place_blocks(gate_up[0], gate_up_got))
    if aligned:
        w_down = lax.all_gather(down_late, "rep", axis=0, tiled=True)
    else:
        w_down = rep_gather(down_late, D)

    mamba_parts = take_blocks(row_blocks(row_major(dot(mixed_t, w_m, 0, 0).astype(bf16))))
    mamba_got = send_to_peers(mamba_parts[1:])

    cot_parts, w_o_got, attn_got, mamba_parts[0] = tie(cot_parts, w_o_got, attn_got, mamba_parts[0])
    w_o = row_major(place_blocks(w_o_sent, w_o_got)).reshape(D, D)
    attn_tok = row_major(place_blocks(attn_parts[0], attn_got)).reshape(F * width_q, rows)[:D]
    attn_proj = dot(attn_tok, w_o, 0, 0)
    branch_attn = rms_scale(attn_proj, gains[1])
    def by_distance(own, received):
        return jnp.concatenate([own] + list(received), axis=0)

    cot_all = by_distance(cot, cot_parts)
    g_hidden = row_major(dot(cot_all, w_down, 1, 1).astype(bf16))
    mamba_got, branch_attn, g_hidden = tie(mamba_got, branch_attn, g_hidden)
    mamba_proj = add_up(mamba_parts[0], mamba_got)
    branch_mamba = rms_scale(mamba_proj, gains[2])
    mix = x_float + 0.5 * (branch_attn + branch_mamba)

    def scatter_start(partial):
        parts = [partial[rows * k : rows * (k + 1)] for k in range(F)]
        return parts[0], send_to_peers(parts[1:])

    normed_two = rms_scale(mix, gains[3]).astype(bf16)
    normed_two = by_distance(normed_two, gather_start(normed_two))
    gate_and_up = row_major(dot(normed_two, w_gu, 1, 0).astype(bf16))
    hidden, g_gu = ffn_middle(gate_and_up, g_hidden)
    g_two_partial = row_major(dot(g_gu, w_gu, 1, 1).astype(bf16))
    g_two_own, g_two_got = scatter_start(g_two_partial)
    g_gu, hidden, g_two_own = tie(g_gu, hidden, g_two_own)
    grad_gu, grad_down = ffn_weight_grads(normed_two, g_gu, hidden, cot_all)
    g_two_got, grad_gu, grad_down = tie(g_two_got, grad_gu, grad_down)
    g_mix_norm, g_gain_three = norm_back(add_up(g_two_own, g_two_got), mix, gains[3])
    g_mix = cot.astype(f32) + g_mix_norm

    def over_rep(grad):
        if aligned:
            return lax.psum_scatter(grad, "rep", scatter_dimension=0, tiled=True)
        return grad

    def to_owners(part):
        return exchange(part.reshape(F, depth, part.shape[1]))

    def finish(matrix):
        flat = matrix.reshape(-1)
        if aligned:
            return flat.astype(f32)
        return lax.psum_scatter(flat, "rep", scatter_dimension=0, tiled=True).astype(f32)

    gu_part, down_part = over_rep(grad_gu), over_rep(grad_down)

    g_branch = 0.5 * g_mix
    g_attn_proj, g_gain_one = norm_back(g_branch, attn_proj, gains[1])
    g_attn_proj = g_attn_proj.astype(bf16)
    g_mamba_proj, g_gain_two = norm_back(g_branch, mamba_proj, gains[2])
    g_mamba_proj = g_mamba_proj.astype(bf16)
    g_attn_tok = row_major(dot(w_o, g_attn_proj, 1, 1).astype(bf16))
    g_attn_tok, attn_late, hidden = tie(g_attn_tok, attn_tok, hidden)
    g_attn_parts = jnp.pad(g_attn_tok, ((0, F * width_q - D), (0, 0)))
    g_attn_parts = take_blocks(g_attn_parts.reshape(F, heads_q, HEAD_SIZE, rows))
    g_attn_got = send_to_peers(g_attn_parts[1:])
    grad_o = row_major(dot(attn_late, g_attn_proj, 1, 0).astype(bf16))
    grad_o = take_blocks(row_blocks(grad_o))
    out_partial = row_major(dot(hidden, w_down, 1, 0).astype(bf16))
    g_attn_got, grad_o, out_partial = tie(g_attn_got, grad_o, out_partial)
    g_mamba_sent, g_attn_got = tie(g_mamba_proj, g_attn_got)
    g_mamba_got = send_to_peers([g_mamba_sent] * (F - 1))
    g_attn_blocks = jnp.stack([g_attn_parts[0]] + g_attn_got)
    g_att = attn_bwd(kvmap, g_attn_blocks, q_t, k_n, k_t, v_n, *attn_args)
    g_att = g_att.reshape(width_att, group)
    g_mamba_got, g_att, out_partial = tie(g_mamba_got, g_att, out_partial)
    out_own, out_got = scatter_start(out_partial)
    g_mamba_all = place_blocks(g_mamba_sent, g_mamba_got).reshape(group, D)
    g_gated = dot(w_m, g_mamba_all, 1, 1)
    grad_m = row_major(dot(mixed_t, g_mamba_all, 1, 0).astype(bf16))
    grad_m = row_major(dot(spread_m, grad_m, 0, 0).astype(bf16))
    g_gated, grad_m = tie(g_gated, grad_m)
    g_ssm, sums = ssm_bwd(heads_s, *ssm_args, g_gated, y_t, states)

    out_got, g_ssm, gu_part, down_part, grad_o = tie(out_got, g_ssm, gu_part, down_part, grad_o)
    grad_o_got = send_to_peers(grad_o[1:])
    g_in = jnp.concatenate([g_att, g_ssm], axis=0)
    grad_in = dot(normed_late, g_in, 0, 1).astype(bf16)
    g_att, g_ssm, grad_in = tie(g_att, g_ssm, grad_in)
    in_part = over_rep(grad_in)
    g_normed = dot(g_att, w_att, 0, 1) + dot(g_ssm, w_ssm, 0, 1)
    g_normed, grad_o_got = tie(row_major(g_normed.astype(bf16)), grad_o_got)
    g_normed = take_blocks(row_blocks(g_normed))
    g_normed_got = send_to_peers(g_normed[1:])
    grad_o = add_up(grad_o[0], grad_o_got).astype(bf16)
    if aligned:
        grad_o = jnp.pad(grad_o.reshape(R, rows_o, D), ((0, 0), (0, pad_o - rows_o), (0, 0)))
        joined = jnp.concatenate([grad_o, grad_m.reshape(R, pad_m, D)], axis=1)
        g_normed_got[0], gu_part, in_part, joined = tie(g_normed_got[0], gu_part, in_part, joined)
        joined = over_rep(joined.reshape(R * (pad_o + pad_m), D))
    g_normed = add_up(g_normed[0], g_normed_got)
    gu_back = to_owners(gu_part).reshape(F, depth, 2, width_f)
    if width_f != hidden_dev:
        gu_back = dot(gu_back.reshape(-1, width_f), spread_f, 1, 0).astype(bf16)
    gu_back = gu_back.reshape(F, depth, 2, hidden_dev).transpose(2, 1, 0, 3)
    grad_gate = finish(gu_back[0].reshape(depth, FF))
    grad_up = finish(gu_back[1].reshape(depth, FF))
    grad_down = finish(restore(down_part)[:rows_f])
    g_x_norm, g_gain_zero = norm_back(g_normed, x_float, gains[0])
    grad_tokens = g_mix + g_x_norm
    output = restore((mix + add_up(out_own, out_got)).astype(bf16))
    if aligned:
        grad_tokens = dot(grad_tokens, order.astype(f32), 1, 0, lax.Precision.HIGH)

    head_sums = jnp.sum(sums, axis=1).reshape(3, STEP_ROWS)
    head_sums = lax.dynamic_update_slice(
        jnp.zeros((3, MH + STEP_ROWS), f32), head_sums, (0, own_head)
    )[:, :MH]
    small = jnp.concatenate(
        [g_gain_zero, g_gain_one, g_gain_two, g_gain_three, head_sums.reshape(-1)]
    )
    in_back = to_owners(in_part)
    att_back, ssm_back = in_back[:, :, :width_att], in_back[:, :, width_att:]
    wide_att = att_back[:, :, : 2 * KV].astype(f32)
    grad_query = jnp.concatenate([att_back[d][:, 2 * KV :] for d in range(F)], axis=1)
    grad_query = finish(grad_query[:, :D])
    grad_key = finish(jnp.sum(wide_att[:, :, :KV], axis=0))
    grad_value = finish(jnp.sum(wide_att[:, :, KV:], axis=0))

    wide_ssm = ssm_back[:, :, at_small:].astype(f32)

    def channel_columns(start):
        return finish(
            jnp.concatenate(
                [
                    ssm_back[d][:, start + shift[d] : start + shift[d] + per_dev]
                    for d in range(F)
                ],
                axis=1,
            )
        )

    grad_inner = channel_columns(0)
    grad_gate_z = channel_columns(channels)
    grad_bc = finish(jnp.sum(wide_ssm[:, :, : 2 * NS], axis=0))
    grad_step = finish(
        sum(
            place_columns(wide_ssm[d][:, 2 * NS : 2 * NS + heads_s], first_head[d], MH)
            for d in range(F)
        )
    )

    small_rows = pad_to(small.shape[0], 1024) // 128
    small = jnp.pad(small, (0, small_rows * 128 - small.shape[0])).reshape(small_rows, 128)
    small = all_sum(small).reshape(-1)
    if aligned:
        joined, small = tie(joined, small)
        joined = restore(joined)
        grad_attn_out = finish(joined[:rows_o])
        grad_mamba_out = finish(joined[pad_o : pad_o + rows_m])
    else:
        grad_attn_out, grad_mamba_out = finish(grad_o), finish(grad_m)
    gain_grads = small[: 4 * D].reshape(4, D)
    bias_grad, decay_grad, skip_grad = (
        small[4 * D + MH * i : 4 * D + MH * (i + 1)] for i in range(3)
    )
    if aligned:
        gain_grads = gain_grads.reshape(4, R, F, depth).transpose(0, 2, 1, 3).reshape(4, D)
    return (
        output,
        grad_tokens,
        grad_query,
        grad_key,
        grad_value,
        grad_attn_out,
        grad_inner,
        grad_gate_z,
        grad_bc,
        grad_step,
        grad_mamba_out,
        grad_gate,
        grad_up,
        grad_down,
        gain_grads,
        bias_grad,
        decay_grad,
        skip_grad,
    )


def solution(mesh):
    split_tokens = P(("rep", "fsdp"), None)
    flat = P(("fsdp", "rep"))
    placed = (split_tokens, P("rep", None)) + (flat,) * 12 + (P(),) * 4 + (split_tokens,)
    return jax.shard_map(
        local,
        mesh=mesh,
        in_specs=placed,
        out_specs=(split_tokens, split_tokens) + (flat,) * 12 + (P(),) * 4,
        check_vma=False,
    )
```

```python
import functools
import math

import jax
import jax.numpy as jnp
from jax import lax
from jax.experimental import pallas as pl
from jax.experimental.layout import Layout, with_layout_constraint
from jax.experimental.pallas import tpu as pltpu
from jax.sharding import PartitionSpec as P

D = 1600
QUERY_HEADS = 25
KEY_VALUE_HEADS = 5
HEAD_SIZE = 64
WIN = 1024
MI = 3200
NS = 16
FF = 5504
MH = 50
KV = KEY_VALUE_HEADS * HEAD_SIZE
HEADS_PER_GROUP = QUERY_HEADS // KEY_VALUE_HEADS
SCALE = HEAD_SIZE ** (-0.5)
CHUNK = 128
QUERY_BLOCK = 256
STEP_ROWS = 16
VMEM_BYTES = 50 * 1024 * 1024

epsilon = 1e-06
masked_score = -1e30
highest = lax.Precision.HIGHEST
f32 = jnp.float32
bf16 = jnp.bfloat16


def rms_scale(value_rows, gain):
    return (
        value_rows
        * lax.rsqrt(jnp.mean(value_rows * value_rows, axis=-1, keepdims=True) + epsilon)
        * gain
    )


def norm_back(grad_in, value_rows, gain):
    factor = lax.rsqrt(jnp.mean(value_rows * value_rows, axis=-1, keepdims=True) + epsilon)
    weighted = grad_in * gain
    spread = jnp.mean(weighted * value_rows, axis=-1, keepdims=True)
    return (
        factor * weighted - value_rows * factor * factor * factor * spread,
        jnp.sum(grad_in * value_rows * factor, axis=0),
    )


def silu(value_rows):
    return value_rows * jax.nn.sigmoid(value_rows)


def silu_slope(value_rows):
    sigmoid_v = jax.nn.sigmoid(value_rows)
    return sigmoid_v * (1.0 + value_rows * (1.0 - sigmoid_v))


def dot(a, b, ca, cb, precision=None):
    return lax.dot_general(
        a, b, (((ca,), (cb,)), ((), ())), precision=precision, preferred_element_type=f32
    )


def sequence_layout(seq_lengths, position):
    seq_ends = jnp.cumsum(seq_lengths, dtype=jnp.int32)
    seq_starts = seq_ends - seq_lengths
    segment = jnp.sum(
        (position[:, None] >= seq_ends[None, :]).astype(jnp.int32), axis=1, dtype=jnp.int32
    )
    labels = jnp.arange(seq_lengths.shape[0], dtype=jnp.int32)
    seq_begin = jnp.sum(
        jnp.where(segment[:, None] == labels[None, :], seq_starts[None, :], 0),
        axis=1,
        dtype=jnp.int32,
    )
    return (segment, (position - seq_begin).astype(f32))


def key_range(i):
    low = max(0, i * QUERY_BLOCK - (WIN - 1)) // QUERY_BLOCK * QUERY_BLOCK
    return low, (i + 1) * QUERY_BLOCK


def fill_mask(seg_col, seg_row, mask, blocks):
    for i in range(blocks):
        low, high = key_range(i)
        cols = slice(i * QUERY_BLOCK, (i + 1) * QUERY_BLOCK)
        shape = (high - low, QUERY_BLOCK)
        key = lax.broadcasted_iota(jnp.int32, shape, 0) + low
        query = lax.broadcasted_iota(jnp.int32, shape, 1) + i * QUERY_BLOCK
        gap = query - key
        visible = (seg_col[low:high, :] == seg_row[:, cols]) & (gap >= 0) & (gap < WIN)
        mask[low:high, cols] = jnp.where(visible, 0.0, masked_score)


def rotate(value, cosine, sine):
    half = HEAD_SIZE // 2
    a, b = value[:half], value[half:]
    return jnp.concatenate([a * cosine - b * sine, b * cosine + a * sine], axis=0)


def attn_fwd_kernel(
    kvmap, kv_ref, q_ref, cosine, sine, seg_row, seg_col, o_ref, qt_ref, kt_ref, kn_ref, vn_ref, mask, vt, *, blocks
):
    h = pl.program_id(0)

    @pl.when(h == 0)
    def _():
        fill_mask(seg_col, seg_row, mask, blocks)
        for c in range(KEY_VALUE_HEADS):
            k = rotate(kv_ref[c], cosine[...], sine[...])
            kt_ref[c] = k.astype(bf16)
            kn_ref[c] = k.T.astype(bf16)
            v = kv_ref[KEY_VALUE_HEADS + c]
            vt[c] = v.astype(bf16)
            vn_ref[c] = v.T.astype(bf16)

    kv = kvmap[h]
    tokens = o_ref.shape[3]
    for i in range(blocks):
        low, high = key_range(i)
        start, stop = i * QUERY_BLOCK, (i + 1) * QUERY_BLOCK
        cols = slice(start, stop)
        q = (rotate(q_ref[0, :, cols], cosine[:, cols], sine[:, cols]) * SCALE).astype(bf16)
        qt_ref[0, :, cols] = q
        s = dot(kn_ref[kv, low:high, :], q, 1, 0) + mask[low:high, cols]
        p = jnp.exp(s - jnp.max(s, axis=0, keepdims=True))
        total = jnp.sum(p, axis=0, keepdims=True)
        o = dot(vt[kv, :, low:high], p.astype(bf16), 1, 0)
        o = (o / total).astype(bf16)
        for d in range(o_ref.shape[0]):
            first, last = max(start, d * tokens), min(stop, (d + 1) * tokens)
            if first < last:
                part = o[:, first - start : last - start]
                o_ref[d, 0, :, first - d * tokens : last - d * tokens] = part


def attn_fwd(kvmap, proj, cosine, sine, seg_row, seg_col, devices):
    heads = proj.shape[0] - 2 * KEY_VALUE_HEADS
    group = proj.shape[2]
    tokens = group // devices
    per_head = pl.BlockSpec((1, HEAD_SIZE, group), lambda h, m: (h, 0, 0))
    angle = pl.BlockSpec((HEAD_SIZE // 2, group), lambda h, m: (0, 0))
    kv_t = (KEY_VALUE_HEADS, HEAD_SIZE, group)
    kv_n = (KEY_VALUE_HEADS, group, HEAD_SIZE)
    whole_t = pl.BlockSpec(kv_t, lambda h, m: (0, 0, 0))
    whole_n = pl.BlockSpec(kv_n, lambda h, m: (0, 0, 0))
    return pl.pallas_call(
        functools.partial(attn_fwd_kernel, blocks=group // QUERY_BLOCK),
        out_shape=(
            jax.ShapeDtypeStruct((devices, heads, HEAD_SIZE, tokens), bf16),
            jax.ShapeDtypeStruct((heads, HEAD_SIZE, group), bf16),
            jax.ShapeDtypeStruct(kv_t, bf16),
            jax.ShapeDtypeStruct(kv_n, bf16),
            jax.ShapeDtypeStruct(kv_n, bf16),
        ),
        grid_spec=pltpu.PrefetchScalarGridSpec(
            num_scalar_prefetch=1,
            grid=(heads,),
            in_specs=[
                pl.BlockSpec((2 * KEY_VALUE_HEADS, HEAD_SIZE, group), lambda h, m: (0, 0, 0)),
                pl.BlockSpec((1, HEAD_SIZE, group), lambda h, m: (h + 2 * KEY_VALUE_HEADS, 0, 0)),
                angle,
                angle,
                pl.BlockSpec((1, group), lambda h, m: (0, 0)),
                pl.BlockSpec((group, 1), lambda h, m: (0, 0)),
            ],
            out_specs=(
                pl.BlockSpec((devices, 1, HEAD_SIZE, tokens), lambda h, m: (0, h, 0, 0)),
                per_head,
                whole_t,
                whole_n,
                whole_n,
            ),
            scratch_shapes=[pltpu.VMEM((group, group), f32), pltpu.VMEM(kv_t, bf16)],
        ),
        compiler_params=pltpu.CompilerParams(vmem_limit_bytes=VMEM_BYTES),
        cost_estimate=pl.CostEstimate(
            flops=group * group, bytes_accessed=group * HEAD_SIZE, transcendentals=group,
        ),
        name="attn_fwd",
    )(kvmap, proj, proj, cosine, sine, seg_row, seg_col)


def attn_bwd_kernel(kvmap, *refs, blocks, devices):
    do_parts = refs[:devices]
    q_ref, kn_ref, kt_ref, vn_ref, cosine, sine, seg_row, seg_col = refs[devices : devices + 8]
    g_ref, mask, dk, dv, do_all = refs[devices + 8 :]
    h = pl.program_id(0)

    @pl.when(h == 0)
    def _():
        fill_mask(seg_col, seg_row, mask, blocks)
        dk[...] = jnp.zeros(dk.shape, f32)
        dv[...] = jnp.zeros(dv.shape, f32)

    kv = kvmap[h]
    tokens = do_parts[0].shape[3]
    for d in range(devices):
        do_all[:, d * tokens : (d + 1) * tokens] = do_parts[d][0, 0]
    for i in range(blocks):
        low, high = key_range(i)
        cols = slice(i * QUERY_BLOCK, (i + 1) * QUERY_BLOCK)
        q = q_ref[0, :, cols]
        do = do_all[:, cols]
        s = dot(kn_ref[kv, low:high, :], q, 1, 0) + mask[low:high, cols]
        p = jnp.exp(s - jnp.max(s, axis=0, keepdims=True))
        p = p * (1.0 / jnp.sum(p, axis=0, keepdims=True))
        dp = dot(vn_ref[kv, low:high, :], do, 1, 0)
        delta = jnp.sum(p * dp, axis=0, keepdims=True)
        ds = (p * (dp - delta)).astype(bf16)
        dv[kv, low:high, :] += dot(p.astype(bf16), do, 1, 1)
        dk[kv, low:high, :] += dot(ds, q, 1, 1)
        dq = dot(kt_ref[kv, :, low:high], ds, 1, 0) * SCALE
        dq = rotate(dq, cosine[:, cols], -sine[:, cols])
        g_ref[2 * KEY_VALUE_HEADS + h, :, cols] = dq.astype(bf16)

    @pl.when(h == pl.num_programs(0) - 1)
    def _():
        for c in range(KEY_VALUE_HEADS):
            g_ref[c] = rotate(dk[c].T, cosine[...], -sine[...]).astype(bf16)
            g_ref[KEY_VALUE_HEADS + c] = dv[c].T.astype(bf16)


def attn_bwd(kvmap, do_blocks, q_t, k_n, k_t, v_n, cosine, sine, seg_row, seg_col):
    devices, heads, _, tokens = do_blocks.shape
    group = q_t.shape[2]
    angle = pl.BlockSpec((HEAD_SIZE // 2, group), lambda h, m: (0, 0))
    kv_t = (KEY_VALUE_HEADS, HEAD_SIZE, group)
    kv_n = (KEY_VALUE_HEADS, group, HEAD_SIZE)
    whole_n = pl.BlockSpec(kv_n, lambda h, m: (0, 0, 0))
    out = (2 * KEY_VALUE_HEADS + heads, HEAD_SIZE, group)

    def block_spec(d):
        return pl.BlockSpec((1, 1, HEAD_SIZE, tokens), lambda h, m: (m[heads + d], h, 0, 0))

    return pl.pallas_call(
        functools.partial(attn_bwd_kernel, blocks=group // QUERY_BLOCK, devices=devices),
        out_shape=jax.ShapeDtypeStruct(out, bf16),
        grid_spec=pltpu.PrefetchScalarGridSpec(
            num_scalar_prefetch=1,
            grid=(heads,),
            in_specs=[block_spec(d) for d in range(devices)]
            + [
                pl.BlockSpec((1, HEAD_SIZE, group), lambda h, m: (h, 0, 0)),
                whole_n,
                pl.BlockSpec(kv_t, lambda h, m: (0, 0, 0)),
                whole_n,
                angle,
                angle,
                pl.BlockSpec((1, group), lambda h, m: (0, 0)),
                pl.BlockSpec((group, 1), lambda h, m: (0, 0)),
            ],
            out_specs=pl.BlockSpec(out, lambda h, m: (0, 0, 0)),
            scratch_shapes=[
                pltpu.VMEM((group, group), f32),
                pltpu.VMEM(kv_n, f32),
                pltpu.VMEM(kv_n, f32),
                pltpu.VMEM((HEAD_SIZE, group), bf16),
            ],
        ),
        compiler_params=pltpu.CompilerParams(vmem_limit_bytes=VMEM_BYTES),
        cost_estimate=pl.CostEstimate(
            flops=group * group, bytes_accessed=group * HEAD_SIZE, transcendentals=group,
        ),
        name="attn_bwd",
    )(kvmap, *([do_blocks] * devices), q_t, k_n, k_t, v_n, cosine, sine, seg_row, seg_col)


def block_setup(p_ref, bias, decay, marks, seg_col, channels):
    at = 2 * channels
    b_t = p_ref[at : at + NS].astype(bf16)
    c_t = p_ref[at + NS : at + 2 * NS].astype(bf16)
    raw = p_ref[at + 2 * NS : at + 2 * NS + STEP_ROWS] + bias[...]
    step = jnp.maximum(raw, 0.0) + jnp.log1p(jnp.exp(-jnp.abs(raw)))
    rate = -step * decay[...]
    rows = lax.broadcasted_iota(jnp.int32, (CHUNK, CHUNK), 0)
    cols = lax.broadcasted_iota(jnp.int32, (CHUNK, CHUNK), 1)
    a_t = dot(rate, (rows <= cols).astype(f32), 1, 0, highest)
    a_n = a_t.T
    visible = (seg_col[...] == marks[0:1]) & (rows <= cols)
    hidden = jnp.where(visible, 0.0, masked_score)
    return b_t, c_t, raw, step, rate, a_t, a_n, rows, cols, hidden


def ssm_fwd_kernel(p_ref, bias, decay, marks, seg_col, skip, y_ref, mixed_ref, states, state, *, heads):
    channels = heads * HEAD_SIZE

    @pl.when(pl.program_id(0) == 0)
    def _():
        state[...] = jnp.zeros(state.shape, f32)

    states[0] = state[...]
    b_t, c_t, _, step, _, a_t, a_n, _, _, hidden = block_setup(
        p_ref, bias, decay, marks, seg_col, channels
    )
    block = dot(b_t, c_t, 0, 0)
    enter, leave, through = marks[1:2], marks[2:3], marks[3:4, 0:1]
    for h in range(heads):
        at = slice(h * HEAD_SIZE, (h + 1) * HEAD_SIZE)
        a_row = a_t[h : h + 1]
        a_end = a_t[h : h + 1, CHUNK - 1 :]
        x = p_ref[at].astype(bf16).astype(f32)
        z = p_ref[channels + h * HEAD_SIZE : channels + (h + 1) * HEAD_SIZE]
        mixing = (jnp.exp(a_row - a_n[:, h : h + 1] + hidden) * block).astype(bf16)
        xs = x * step[h : h + 1]
        y = dot(xs.astype(bf16), mixing, 1, 0)
        s = state[at]
        y = y + dot(s.astype(bf16), c_t, 1, 0) * (enter * jnp.exp(a_row)) + skip[h] * x
        y_ref[at] = y
        mixed_ref[at] = (y * silu(z)).astype(bf16)
        xw = (xs * (leave * jnp.exp(a_end - a_row))).astype(bf16)
        state[at] = through * jnp.exp(a_end) * s + dot(xw, b_t, 1, 1)


def ssm_specs(height, order):
    column = pl.BlockSpec((STEP_ROWS, 1), lambda c: (0, 0))
    return [
        pl.BlockSpec((height, CHUNK), lambda c: (0, order(c))),
        column,
        column,
        pl.BlockSpec((8, CHUNK), lambda c: (0, order(c))),
        pl.BlockSpec((CHUNK, 1), lambda c: (order(c), 0)),
        pl.BlockSpec(memory_space=pltpu.SMEM),
    ]


def ssm_fwd(heads, proj, bias, decay, marks, seg_col, skip):
    height, group = proj.shape
    channels = heads * HEAD_SIZE
    count = group // CHUNK
    by_block = pl.BlockSpec((channels, CHUNK), lambda c: (0, c))
    return pl.pallas_call(
        functools.partial(ssm_fwd_kernel, heads=heads),
        out_shape=(
            jax.ShapeDtypeStruct((channels, group), f32),
            jax.ShapeDtypeStruct((channels, group), bf16),
            jax.ShapeDtypeStruct((count, channels, NS), f32),
        ),
        grid=(count,),
        in_specs=ssm_specs(height, lambda c: c),
        out_specs=(by_block, by_block, pl.BlockSpec((1, channels, NS), lambda c: (c, 0, 0))),
        scratch_shapes=[pltpu.VMEM((channels, NS), f32)],
        compiler_params=pltpu.CompilerParams(vmem_limit_bytes=VMEM_BYTES),
        cost_estimate=pl.CostEstimate(
            flops=group * group, bytes_accessed=group * HEAD_SIZE, transcendentals=group,
        ),
        name="ssm_fwd",
    )(proj, bias, decay, marks, seg_col, skip)


def ssm_bwd_kernel(
    p_ref,
    bias,
    decay,
    marks,
    seg_col,
    skip,
    up_ref,
    y_ref,
    states,
    g_ref,
    sums,
    adjoint,
    after,
    before,
    gstep,
    grate,
    *,
    heads,
):
    channels = heads * HEAD_SIZE

    @pl.when(pl.program_id(0) == 0)
    def _():
        for ref in (adjoint, sums, after, before, gstep, grate):
            ref[...] = jnp.zeros(ref.shape, f32)

    b_t, c_t, raw, step_all, rate_all, a_t, a_n, rows, cols, hidden = block_setup(
        p_ref, bias, decay, marks, seg_col, channels
    )
    block = dot(b_t, c_t, 0, 0)
    enter, leave, through = marks[1:2], marks[2:3], marks[3:4, 0:1]
    from_here = (rows >= cols).astype(f32)
    from_here_low = from_here.astype(bf16)
    strictly = (rows < cols).astype(f32)
    pair_sum = jnp.zeros((CHUNK, CHUNK), f32)
    gc = jnp.zeros((NS, CHUNK), f32)
    gb = jnp.zeros((NS, CHUNK), f32)
    at_skip = 2 * STEP_ROWS
    for h in range(heads):
        at = slice(h * HEAD_SIZE, (h + 1) * HEAD_SIZE)
        at_gate = slice(channels + h * HEAD_SIZE, channels + (h + 1) * HEAD_SIZE)
        one = slice(h, h + 1)
        a_row = a_t[one]
        a_end = a_t[one, CHUNK - 1 :]
        step = step_all[one]
        x = p_ref[at].astype(bf16).astype(f32)
        z = p_ref[at_gate]
        g = up_ref[at]
        sigmoid_z = jax.nn.sigmoid(z)
        gy = g * z * sigmoid_z
        gz = g * y_ref[at] * sigmoid_z * (1.0 + z * (1.0 - sigmoid_z))
        g_ref[at_gate] = gz.astype(bf16)
        sums[at_skip + h : at_skip + h + 1] += jnp.sum(gy * x, axis=0, keepdims=True)
        reach = jnp.exp(a_row - a_n[:, one] + hidden)
        gy_low = gy.astype(bf16)
        xs = x * step
        u = dot(gy_low, (reach * block).astype(bf16), 1, 1)
        lam = adjoint[at]
        lam_low = lam.astype(bf16)
        out_weight = leave * jnp.exp(a_end - a_row)
        u_state = dot(lam_low, b_t, 1, 0) * out_weight
        u = u + u_state
        g_ref[at] = (step * u + skip[h] * gy).astype(bf16)
        gstep[one] = jnp.sum(x * u, axis=0, keepdims=True)
        before[one] = jnp.sum(xs * u_state, axis=0, keepdims=True)
        pairs = dot(xs.astype(bf16), gy_low, 0, 0) * reach
        pair_sum = pair_sum + pairs
        crossing = dot((pairs * block).astype(bf16), from_here_low, 1, 0)
        crossed = jnp.sum(crossing * strictly, axis=0, keepdims=True)
        gyw = gy * (enter * jnp.exp(a_row))
        gyw_low = gyw.astype(bf16)
        s = states[0, at]
        s_low = s.astype(bf16)
        after[one] = jnp.sum(gyw * dot(s_low, c_t, 1, 0), axis=0, keepdims=True)
        gc = gc + dot(s_low, gyw_low, 0, 0)
        gb = gb + dot(lam_low, (xs * out_weight).astype(bf16), 0, 0)
        passing = through * jnp.exp(a_end)
        product = jnp.sum(jnp.sum(lam * s, axis=1, keepdims=True), axis=0, keepdims=True)
        grate[one] = crossed + passing * product
        adjoint[at] = passing * lam + dot(gyw_low, c_t, 1, 1)
    grate_all = (
        grate[...]
        + dot(after[...], from_here, 1, 0, highest)
        + dot(before[...], strictly, 1, 0, highest)
    )
    pair_low = pair_sum.astype(bf16)
    small = 2 * channels
    g_ref[small : small + NS] = (gb + dot(c_t, pair_low, 1, 1)).astype(bf16)
    g_ref[small + NS : small + 2 * NS] = (gc + dot(b_t, pair_low, 1, 0)).astype(bf16)
    graw = (gstep[...] - grate_all * decay[...]) * jax.nn.sigmoid(raw)
    at_step = small + 2 * NS
    g_ref[at_step : at_step + STEP_ROWS] = graw.astype(bf16)
    rest = g_ref.shape[0] - at_step - STEP_ROWS
    g_ref[at_step + STEP_ROWS :] = jnp.zeros((rest, CHUNK), bf16)
    sums[:STEP_ROWS] += graw
    sums[STEP_ROWS:at_skip] += grate_all * rate_all


def ssm_bwd(heads, proj, bias, decay, marks, seg_col, skip, up_t, y_t, states):
    height, group = proj.shape
    channels = heads * HEAD_SIZE
    count = group // CHUNK

    def order(c):
        return count - 1 - c

    by_block = pl.BlockSpec((channels, CHUNK), lambda c: (0, order(c)))
    small = pltpu.VMEM((STEP_ROWS, CHUNK), f32)
    return pl.pallas_call(
        functools.partial(ssm_bwd_kernel, heads=heads),
        out_shape=(
            jax.ShapeDtypeStruct((height, group), bf16),
            jax.ShapeDtypeStruct((3 * STEP_ROWS, CHUNK), f32),
        ),
        grid=(count,),
        in_specs=ssm_specs(height, order)
        + [by_block, by_block, pl.BlockSpec((1, channels, NS), lambda c: (order(c), 0, 0))],
        out_specs=(
            pl.BlockSpec((height, CHUNK), lambda c: (0, order(c))),
            pl.BlockSpec((3 * STEP_ROWS, CHUNK), lambda c: (0, 0)),
        ),
        scratch_shapes=[pltpu.VMEM((channels, NS), f32), small, small, small, small],
        compiler_params=pltpu.CompilerParams(vmem_limit_bytes=VMEM_BYTES),
        cost_estimate=pl.CostEstimate(
            flops=group * group, bytes_accessed=group * HEAD_SIZE, transcendentals=group,
        ),
        name="ssm_bwd",
    )(proj, bias, decay, marks, seg_col, skip, up_t, y_t, states)


def ffn_middle_kernel(gate_up_ref, g_ref, hidden_ref, g_gu_ref):
    width = g_ref.shape[1]
    gate = gate_up_ref[:, :width].astype(f32)
    up = gate_up_ref[:, width:].astype(f32)
    g = g_ref[...].astype(f32)
    sigmoid_v = jax.nn.sigmoid(gate)
    passed = gate * sigmoid_v
    hidden_ref[...] = (passed * up).astype(bf16)
    slope = sigmoid_v * (1.0 + gate * (1.0 - sigmoid_v))
    g_gu_ref[:, :width] = (g * up * slope).astype(bf16)
    g_gu_ref[:, width:] = (g * passed).astype(bf16)


def ffn_middle(gate_up, g_hidden):
    group, width = g_hidden.shape
    height = 128
    narrow = pl.BlockSpec((height, width), lambda i: (i, 0))
    wide = pl.BlockSpec((height, 2 * width), lambda i: (i, 0))
    return pl.pallas_call(
        ffn_middle_kernel,
        out_shape=(
            jax.ShapeDtypeStruct((group, width), bf16),
            jax.ShapeDtypeStruct((group, 2 * width), bf16),
        ),
        grid=(group // height,),
        in_specs=[wide, narrow],
        out_specs=(narrow, wide),
        compiler_params=pltpu.CompilerParams(vmem_limit_bytes=VMEM_BYTES),
        name="ffn_middle",
    )(gate_up, g_hidden)


def weight_grads_kernel(rows_ref, g_ref, hidden_ref, cot_ref, wide_ref, down_ref, *, wide_steps):
    i = pl.program_id(0)

    @pl.when(i < wide_steps)
    def _():
        wide_ref[...] = dot(rows_ref[...], g_ref[...], 0, 0).astype(bf16)

    @pl.when(i >= wide_steps)
    def _():
        down_ref[...] = dot(hidden_ref[...], cot_ref[...], 0, 0).astype(bf16)


def ffn_weight_grads(rows, g_wide, hidden, cot):
    group, depth = rows.shape
    wide, width = g_wide.shape[1], hidden.shape[1]
    columns, height = 256, 128
    if wide % columns or width % height:
        return (
            dot(rows, g_wide, 0, 0).astype(bf16),
            row_major(dot(hidden, cot, 0, 0).astype(bf16)),
        )
    wide_steps, down_steps = wide // columns, width // height

    def first(i):
        return jnp.minimum(i, wide_steps - 1)

    def second(i):
        return jnp.maximum(i - wide_steps, 0)

    whole = pl.BlockSpec((group, depth), lambda i: (0, 0))
    return pl.pallas_call(
        functools.partial(weight_grads_kernel, wide_steps=wide_steps),
        out_shape=(
            jax.ShapeDtypeStruct((depth, wide), bf16),
            jax.ShapeDtypeStruct((width, depth), bf16),
        ),
        grid=(wide_steps + down_steps,),
        in_specs=[
            whole,
            pl.BlockSpec((group, columns), lambda i: (0, first(i))),
            pl.BlockSpec((group, height), lambda i: (0, second(i))),
            whole,
        ],
        out_specs=(
            pl.BlockSpec((depth, columns), lambda i: (0, first(i))),
            pl.BlockSpec((height, depth), lambda i: (second(i), 0)),
        ),
        compiler_params=pltpu.CompilerParams(vmem_limit_bytes=VMEM_BYTES),
        cost_estimate=pl.CostEstimate(flops=group * group, bytes_accessed=group, transcendentals=0),
        name="ffn_weight_grads",
    )(rows, g_wide, hidden, cot)


def pad_to(value, multiple):
    return -(-value // multiple) * multiple


def place_columns(block, start, width):
    return jnp.pad(block, ((0, 0), (start, width - start - block.shape[1])))


def peers(devices, k):
    return [(i, i ^ k) for i in range(devices)]


def one_hot(rows, cols, wanted):
    row = wanted(jnp.arange(rows, dtype=jnp.int32))
    return (row[:, None] == jnp.arange(cols, dtype=jnp.int32)[None, :]).astype(bf16)


def tie(*values):
    return lax.optimization_barrier(values)


def row_major(value):
    return with_layout_constraint(value, Layout(tuple(range(value.ndim))))


def send_to_peers(parts):
    devices = lax.axis_size("fsdp")
    return [lax.ppermute(parts[k - 1], "fsdp", peers(devices, k)) for k in range(1, devices)]


def gather_start(part):
    devices = lax.axis_size("fsdp")
    if devices != 4:
        return send_to_peers([part] * (devices - 1))
    half = part.shape[0] // 2
    one, two = (lax.ppermute(part, "fsdp", peers(devices, k)) for k in (1, 2))
    upper = lax.ppermute(two[:half], "fsdp", peers(devices, 1))
    lower = lax.ppermute(one[half:], "fsdp", peers(devices, 2))
    return [one, two, jnp.concatenate([upper, lower], axis=0)]


def place_blocks(own, received):
    devices, mine = lax.axis_size("fsdp"), lax.axis_index("fsdp")
    result = jnp.broadcast_to(own[None], (devices,) + own.shape)
    for k in range(1, devices):
        result = lax.dynamic_update_index_in_dim(result, received[k - 1], mine ^ k, 0)
    return result


def take_blocks(blocks):
    devices, mine = lax.axis_size("fsdp"), lax.axis_index("fsdp")
    return [lax.dynamic_index_in_dim(blocks, mine ^ k, 0, False) for k in range(devices)]


def exchange(blocks):
    parts = take_blocks(blocks)
    return place_blocks(parts[0], send_to_peers(parts[1:]))


def gather_rows(part, hold=lambda received: received):
    devices = lax.axis_size("fsdp")
    received = hold(send_to_peers([part] * (devices - 1)))
    return place_blocks(part, received).reshape((devices * part.shape[0],) + part.shape[1:])


def add_up(own, received):
    total = own.astype(f32)
    for part in received:
        total = total + part.astype(f32)
    return total


def row_blocks(partial):
    devices = lax.axis_size("fsdp")
    return partial.reshape((devices, partial.shape[0] // devices) + partial.shape[1:])


def scatter_rows(partial):
    parts = take_blocks(row_blocks(partial))
    return add_up(parts[0], send_to_peers(parts[1:]))


def all_sum(value):
    for axis in ("fsdp", "rep"):
        devices, k = lax.axis_size(axis), 1
        while k < devices:
            value = value + lax.ppermute(value, axis, peers(devices, k))
            k *= 2
    return value


def local(
    tokens,
    lengths,
    w_query,
    w_key,
    w_value,
    w_attn_out,
    w_inner,
    w_gate_z,
    w_bc,
    w_step,
    w_mamba_out,
    w_ffn_gate,
    w_ffn_up,
    w_ffn_down,
    norm_gains,
    step_bias,
    decay_log,
    skip_gain,
    cotangent,
):
    F, R = lax.axis_size("fsdp"), lax.axis_size("rep")
    mine = lax.axis_index("fsdp")
    rows = tokens.shape[0]
    group = rows * F
    aligned = D % (F * R) == 0 and FF % (F * R) == 0
    depth = D // (F * R) if aligned else D // F

    heads_q = -(-QUERY_HEADS // F)
    width_q = heads_q * HEAD_SIZE
    per_dev = MI // F
    first_head = [per_dev * d // HEAD_SIZE for d in range(F)]
    shift = [per_dev * d % HEAD_SIZE for d in range(F)]
    heads_s = max(-(-(s + per_dev) // HEAD_SIZE) for s in shift)
    channels = heads_s * HEAD_SIZE
    at_small = 2 * channels
    at_step = at_small + 2 * NS
    width_att = 2 * KV + width_q
    width_ssm = at_small + 64
    hidden_dev = FF // F
    blocks = R if aligned else 1
    rows_o, rows_m, rows_f = (D // F // blocks, per_dev // blocks, hidden_dev // blocks)
    pad_o, pad_m, pad_f = (pad_to(n, 8) for n in (rows_o, rows_m, rows_f))
    width_f = blocks * pad_f

    if aligned:

        def old_place(n):
            return (n // depth % F) * (R * depth) + n // (F * depth) * depth + n % depth

        order = one_hot(D, D, old_place)

        def permute(v):
            return dot(v, order, 1, 1).astype(v.dtype)

        def restore(v):
            return dot(v, order, 1, 0).astype(v.dtype)

        gains = norm_gains.reshape(4, F, R, depth).transpose(0, 2, 1, 3).reshape(4, D)
    else:

        def permute(v):
            return v

        restore = permute
        gains = norm_gains

    def pad_rows(matrix, height):
        return jnp.pad(matrix, ((0, height - matrix.shape[0]), (0, 0)))

    def rep_gather(flat, width):
        return lax.all_gather(flat, "rep", axis=0, tiled=True).reshape(-1, width)

    def read(flat, width):
        return flat.reshape(depth, width) if aligned else rep_gather(flat, width)

    def collect(part):
        if aligned:
            part = part.reshape(F * depth, part.shape[2])
            return lax.all_gather(part, "rep", axis=0, tiled=True)
        return part.reshape(D, part.shape[2])

    index = jnp.arange(group, dtype=jnp.int32)
    segment, place = sequence_layout(lengths[0], index)
    frequency = jnp.exp(
        jnp.arange(HEAD_SIZE // 2, dtype=f32) * (-2.0 * math.log(10000.0) / HEAD_SIZE)
    )
    angles = frequency[:, None] * place[None, :]
    cosine, sine = jnp.cos(angles), jnp.sin(angles)
    seg_row, seg_col = segment[None, :], segment[:, None]
    by_chunk = segment.reshape(group // CHUNK, CHUNK)
    last = by_chunk[:, -1:]
    prior = jnp.concatenate([jnp.full((1, 1), -1, jnp.int32), last[:-1]], axis=0)
    marks = jnp.stack(
        [
            by_chunk,
            (by_chunk == prior).astype(jnp.int32),
            (by_chunk == last).astype(jnp.int32),
            jnp.broadcast_to((last == prior).astype(jnp.int32), by_chunk.shape),
        ]
    ).reshape(4, group)
    marks = jnp.concatenate([marks, jnp.zeros((4, group), jnp.int32)], axis=0).astype(f32)
    seg_col_f = seg_col.astype(f32)
    distance = jnp.arange(F, dtype=jnp.int32) ^ mine
    kvmap = jnp.minimum(mine * heads_q + jnp.arange(heads_q), QUERY_HEADS - 1) // HEADS_PER_GROUP
    kvmap = jnp.concatenate([kvmap.astype(jnp.int32), distance.astype(jnp.int32)])

    both = permute(jnp.concatenate([tokens, cotangent], axis=0))
    x_float = both[:rows].astype(f32)
    cot = both[rows:]
    normed_own = rms_scale(x_float, gains[0]).astype(bf16)

    if aligned:
        down_shards = jnp.concatenate(
            [
                pad_rows(w_attn_out.reshape(rows_o, D), pad_o),
                pad_rows(w_mamba_out.reshape(rows_m, D), pad_m),
                pad_rows(w_ffn_down.reshape(rows_f, D), pad_f),
            ],
            axis=0,
        )
        down_shards = permute(down_shards)
        down_shards, w_inner, w_gate_z, w_query = tie(down_shards, w_inner, w_gate_z, w_query)
        out_both = lax.all_gather(down_shards[: pad_o + pad_m], "rep", axis=0)
        w_o_part = out_both[:, :rows_o].reshape(R * rows_o, D)
        w_m_part = out_both[:, pad_o:].reshape(R * pad_m, D)
        down_late = down_shards[pad_o + pad_m :]
    else:
        w_o_part, w_m_part = rep_gather(w_attn_out, D), rep_gather(w_mamba_out, D)
        down_late = w_ffn_down

    wq, wk, wv = read(w_query, D), read(w_key, KV), read(w_value, KV)
    wx, wz = read(w_inner, MI), read(w_gate_z, MI)
    wbc, wdt = read(w_bc, 2 * NS), read(w_step, MH)
    wq = place_columns(wq, 0, F * width_q)
    column_blocks = []
    for d in range(F):
        cols = slice(per_dev * d, per_dev * (d + 1))
        column_blocks.append(
            jnp.concatenate(
                [
                    wk,
                    wv,
                    wq[:, width_q * d : width_q * (d + 1)],
                    place_columns(wx[:, cols], shift[d], channels),
                    place_columns(wz[:, cols], shift[d], channels),
                    wbc,
                    place_columns(
                        wdt[:, first_head[d] : first_head[d] + heads_s], 0, width_ssm - at_step
                    ),
                ],
                axis=1,
            )
        )
    in_sent = take_blocks(jnp.stack(column_blocks))
    in_got = send_to_peers(in_sent[1:])
    normed_own, in_sent[0] = tie(normed_own, in_sent[0])
    normed_got = tie(*gather_start(normed_own))
    in_got, w_ffn_gate, w_ffn_up = tie(in_got, w_ffn_gate, w_ffn_up)
    in_part = place_blocks(in_sent[0], in_got)
    spread_f = one_hot(
        width_f,
        hidden_dev,
        lambda c: jnp.where(c % pad_f < rows_f, c // pad_f * rows_f + c % pad_f, -1),
    )
    gate_up = jnp.stack([read(w_ffn_gate, FF), read(w_ffn_up, FF)])
    gate_up = gate_up.reshape(2, depth, F, hidden_dev).transpose(2, 1, 0, 3)
    if width_f != hidden_dev:
        gate_up = dot(gate_up.reshape(-1, hidden_dev), spread_f, 1, 1).astype(bf16)
    gate_up = gate_up.reshape(F, depth, 2 * width_f)
    normed = place_blocks(normed_own, normed_got).reshape(group, D)
    w_o_sent, normed_late = tie(w_o_part, normed)
    w_o_got = send_to_peers([w_o_sent] * (F - 1))
    w_att = collect(in_part[:, :, :width_att])
    w_ssm = collect(in_part[:, :, width_att:])

    proj_att = dot(w_att, normed, 0, 1)
    attn_args = (cosine, sine, seg_row, seg_col)
    attn_t, q_t, k_t, k_n, v_n = attn_fwd(
        kvmap, proj_att.reshape(-1, HEAD_SIZE, group), *attn_args, F
    )
    attn_t, w_o_got = tie(attn_t, w_o_got)
    attn_parts = take_blocks(attn_t.reshape(F, width_q, rows))
    attn_got = send_to_peers(attn_parts[1:])
    attn_parts[0], cot_sent = tie(attn_parts[0], cot)
    cot_parts = send_to_peers([cot_sent] * (F - 1))
    own_shift = (mine * per_dev) % HEAD_SIZE
    own_head = (mine * per_dev) // HEAD_SIZE

    def channel_source(c):
        c = c - own_shift
        return jnp.where((c >= 0) & (c < per_dev), c // rows_m * pad_m + c % rows_m, -1)

    spread_m = one_hot(channels, blocks * pad_m, channel_source)
    w_m = dot(spread_m, w_m_part, 1, 0).astype(bf16)

    proj_ssm = dot(w_ssm, normed, 0, 1)
    proj_ssm, cot_parts = tie(proj_ssm, cot_parts)

    def own_heads(v):
        v = jnp.pad(v, (0, STEP_ROWS))
        return lax.dynamic_slice_in_dim(v, own_head, STEP_ROWS, 0)

    ssm_args = (
        proj_ssm,
        own_heads(step_bias)[:, None],
        jnp.exp(own_heads(decay_log))[:, None],
        marks,
        seg_col_f,
        own_heads(skip_gain),
    )
    y_t, mixed_t, states = ssm_fwd(heads_s, *ssm_args)
    attn_got, gate_up, mixed_t = tie(attn_got, gate_up, mixed_t)
    gate_up = take_blocks(gate_up)
    gate_up_got = send_to_peers(gate_up[1:])
    mamba_parts = take_blocks(row_blocks(row_major(dot(mixed_t, w_m, 0, 0).astype(bf16))))
    mamba_got = send_to_peers(mamba_parts[1:])

    gate_up_got, mamba_parts[0] = tie(gate_up_got, mamba_parts[0])
    w_gu = collect(place_blocks(gate_up[0], gate_up_got))
    if aligned:
        w_down = lax.all_gather(down_late, "rep", axis=0, tiled=True)
    else:
        w_down = rep_gather(down_late, D)

    w_o_got, attn_got, mamba_parts[0] = tie(w_o_got, attn_got, mamba_parts[0])
    w_o = row_major(place_blocks(w_o_sent, w_o_got)).reshape(D, D)
    attn_tok = row_major(place_blocks(attn_parts[0], attn_got)).reshape(F * width_q, rows)[:D]
    attn_proj = dot(attn_tok, w_o, 0, 0)
    branch_attn = rms_scale(attn_proj, gains[1])
    def by_distance(own, received):
        return jnp.concatenate([own] + list(received), axis=0)

    cot_all = by_distance(cot, cot_parts)
    g_hidden = row_major(dot(cot_all, w_down, 1, 1).astype(bf16))
    mamba_got, branch_attn, g_hidden = tie(mamba_got, branch_attn, g_hidden)
    mamba_proj = add_up(mamba_parts[0], mamba_got)
    branch_mamba = rms_scale(mamba_proj, gains[2])
    mix = x_float + 0.5 * (branch_attn + branch_mamba)

    def scatter_start(partial):
        parts = [partial[rows * k : rows * (k + 1)] for k in range(F)]
        return parts[0], send_to_peers(parts[1:])

    normed_two = rms_scale(mix, gains[3]).astype(bf16)
    normed_two = by_distance(normed_two, gather_start(normed_two))
    gate_and_up = row_major(dot(normed_two, w_gu, 1, 0).astype(bf16))
    hidden, g_gu = ffn_middle(gate_and_up, g_hidden)
    g_two_partial = row_major(dot(g_gu, w_gu, 1, 1).astype(bf16))
    g_two_own, g_two_got = scatter_start(g_two_partial)
    g_gu, hidden, g_two_own = tie(g_gu, hidden, g_two_own)
    grad_gu, grad_down = ffn_weight_grads(normed_two, g_gu, hidden, cot_all)
    g_two_got, grad_gu, grad_down = tie(g_two_got, grad_gu, grad_down)
    g_mix_norm, g_gain_three = norm_back(add_up(g_two_own, g_two_got), mix, gains[3])
    g_mix = cot.astype(f32) + g_mix_norm

    def over_rep(grad):
        if aligned:
            return lax.psum_scatter(grad, "rep", scatter_dimension=0, tiled=True)
        return grad

    def to_owners(part):
        return exchange(part.reshape(F, depth, part.shape[1]))

    def finish(matrix):
        flat = matrix.reshape(-1)
        if aligned:
            return flat.astype(f32)
        return lax.psum_scatter(flat, "rep", scatter_dimension=0, tiled=True).astype(f32)

    gu_part, down_part = over_rep(grad_gu), over_rep(grad_down)

    g_branch = 0.5 * g_mix
    g_attn_proj, g_gain_one = norm_back(g_branch, attn_proj, gains[1])
    g_attn_proj = g_attn_proj.astype(bf16)
    g_mamba_proj, g_gain_two = norm_back(g_branch, mamba_proj, gains[2])
    g_mamba_proj = g_mamba_proj.astype(bf16)
    g_attn_tok = row_major(dot(w_o, g_attn_proj, 1, 1).astype(bf16))
    g_attn_tok, attn_late, hidden = tie(g_attn_tok, attn_tok, hidden)
    g_attn_parts = jnp.pad(g_attn_tok, ((0, F * width_q - D), (0, 0)))
    g_attn_parts = take_blocks(g_attn_parts.reshape(F, heads_q, HEAD_SIZE, rows))
    g_attn_got = send_to_peers(g_attn_parts[1:])
    grad_o = row_major(dot(attn_late, g_attn_proj, 1, 0).astype(bf16))
    grad_o = take_blocks(row_blocks(grad_o))
    out_partial = row_major(dot(hidden, w_down, 1, 0).astype(bf16))
    g_attn_got, grad_o, out_partial = tie(g_attn_got, grad_o, out_partial)
    g_mamba_sent, g_attn_got = tie(g_mamba_proj, g_attn_got)
    g_mamba_got = send_to_peers([g_mamba_sent] * (F - 1))
    g_attn_blocks = jnp.stack([g_attn_parts[0]] + g_attn_got)
    g_att = attn_bwd(kvmap, g_attn_blocks, q_t, k_n, k_t, v_n, *attn_args)
    g_att = g_att.reshape(width_att, group)
    g_mamba_got, g_att, out_partial = tie(g_mamba_got, g_att, out_partial)
    out_own, out_got = scatter_start(out_partial)
    g_mamba_all = place_blocks(g_mamba_sent, g_mamba_got).reshape(group, D)
    g_gated = dot(w_m, g_mamba_all, 1, 1)
    grad_m = row_major(dot(mixed_t, g_mamba_all, 1, 0).astype(bf16))
    grad_m = row_major(dot(spread_m, grad_m, 0, 0).astype(bf16))
    g_gated, grad_m = tie(g_gated, grad_m)
    g_ssm, sums = ssm_bwd(heads_s, *ssm_args, g_gated, y_t, states)

    out_got, g_ssm, gu_part, down_part, grad_o = tie(out_got, g_ssm, gu_part, down_part, grad_o)
    grad_o_got = send_to_peers(grad_o[1:])
    g_in = jnp.concatenate([g_att, g_ssm], axis=0)
    grad_in = dot(normed_late, g_in, 0, 1).astype(bf16)
    g_att, g_ssm, grad_in = tie(g_att, g_ssm, grad_in)
    in_part = over_rep(grad_in)
    g_normed = dot(g_att, w_att, 0, 1) + dot(g_ssm, w_ssm, 0, 1)
    g_normed = take_blocks(row_blocks(row_major(g_normed.astype(bf16))))
    g_normed_got = send_to_peers(g_normed[1:])
    grad_o = add_up(grad_o[0], grad_o_got).astype(bf16)
    if aligned:
        grad_o = jnp.pad(grad_o.reshape(R, rows_o, D), ((0, 0), (0, pad_o - rows_o), (0, 0)))
        joined = jnp.concatenate([grad_o, grad_m.reshape(R, pad_m, D)], axis=1)
        g_normed_got[0], gu_part, in_part, joined = tie(g_normed_got[0], gu_part, in_part, joined)
        joined = over_rep(joined.reshape(R * (pad_o + pad_m), D))
    g_normed = add_up(g_normed[0], g_normed_got)
    gu_back = to_owners(gu_part).reshape(F, depth, 2, width_f)
    if width_f != hidden_dev:
        gu_back = dot(gu_back.reshape(-1, width_f), spread_f, 1, 0).astype(bf16)
    gu_back = gu_back.reshape(F, depth, 2, hidden_dev).transpose(2, 1, 0, 3)
    grad_gate = finish(gu_back[0].reshape(depth, FF))
    grad_up = finish(gu_back[1].reshape(depth, FF))
    grad_down = finish(restore(down_part)[:rows_f])
    g_x_norm, g_gain_zero = norm_back(g_normed, x_float, gains[0])
    grad_tokens = g_mix + g_x_norm
    output = restore((mix + add_up(out_own, out_got)).astype(bf16))
    if aligned:
        grad_tokens = dot(grad_tokens, order.astype(f32), 1, 0, lax.Precision.HIGH)

    head_sums = jnp.sum(sums, axis=1).reshape(3, STEP_ROWS)
    head_sums = lax.dynamic_update_slice(
        jnp.zeros((3, MH + STEP_ROWS), f32), head_sums, (0, own_head)
    )[:, :MH]
    small = jnp.concatenate(
        [g_gain_zero, g_gain_one, g_gain_two, g_gain_three, head_sums.reshape(-1)]
    )
    in_back = to_owners(in_part)
    att_back, ssm_back = in_back[:, :, :width_att], in_back[:, :, width_att:]
    wide_att = att_back[:, :, : 2 * KV].astype(f32)
    grad_query = jnp.concatenate([att_back[d][:, 2 * KV :] for d in range(F)], axis=1)
    grad_query = finish(grad_query[:, :D])
    grad_key = finish(jnp.sum(wide_att[:, :, :KV], axis=0))
    grad_value = finish(jnp.sum(wide_att[:, :, KV:], axis=0))

    wide_ssm = ssm_back[:, :, at_small:].astype(f32)

    def channel_columns(start):
        return finish(
            jnp.concatenate(
                [
                    ssm_back[d][:, start + shift[d] : start + shift[d] + per_dev]
                    for d in range(F)
                ],
                axis=1,
            )
        )

    grad_inner = channel_columns(0)
    grad_gate_z = channel_columns(channels)
    grad_bc = finish(jnp.sum(wide_ssm[:, :, : 2 * NS], axis=0))
    grad_step = finish(
        sum(
            place_columns(wide_ssm[d][:, 2 * NS : 2 * NS + heads_s], first_head[d], MH)
            for d in range(F)
        )
    )

    small_rows = pad_to(small.shape[0], 1024) // 128
    small = jnp.pad(small, (0, small_rows * 128 - small.shape[0])).reshape(small_rows, 128)
    small = all_sum(small).reshape(-1)
    if aligned:
        joined, small = tie(joined, small)
        joined = restore(joined)
        grad_attn_out = finish(joined[:rows_o])
        grad_mamba_out = finish(joined[pad_o : pad_o + rows_m])
    else:
        grad_attn_out, grad_mamba_out = finish(grad_o), finish(grad_m)
    gain_grads = small[: 4 * D].reshape(4, D)
    bias_grad, decay_grad, skip_grad = (
        small[4 * D + MH * i : 4 * D + MH * (i + 1)] for i in range(3)
    )
    if aligned:
        gain_grads = gain_grads.reshape(4, R, F, depth).transpose(0, 2, 1, 3).reshape(4, D)
    return (
        output,
        grad_tokens,
        grad_query,
        grad_key,
        grad_value,
        grad_attn_out,
        grad_inner,
        grad_gate_z,
        grad_bc,
        grad_step,
        grad_mamba_out,
        grad_gate,
        grad_up,
        grad_down,
        gain_grads,
        bias_grad,
        decay_grad,
        skip_grad,
    )


def solution(mesh):
    split_tokens = P(("rep", "fsdp"), None)
    flat = P(("fsdp", "rep"))
    placed = (split_tokens, P("rep", None)) + (flat,) * 12 + (P(),) * 4 + (split_tokens,)
    return jax.shard_map(
        local,
        mesh=mesh,
        in_specs=placed,
        out_specs=(split_tokens, split_tokens) + (flat,) * 12 + (P(),) * 4,
        check_vma=False,
    )
```

```python
import functools
import math

import jax
import jax.numpy as jnp
from jax import lax
from jax.experimental import pallas as pl
from jax.experimental.layout import Layout, with_layout_constraint
from jax.experimental.pallas import tpu as pltpu
from jax.sharding import PartitionSpec as P

D = 1600
QUERY_HEADS = 25
KEY_VALUE_HEADS = 5
HEAD_SIZE = 64
WIN = 1024
MI = 3200
NS = 16
FF = 5504
MH = 50
KV = KEY_VALUE_HEADS * HEAD_SIZE
HEADS_PER_GROUP = QUERY_HEADS // KEY_VALUE_HEADS
SCALE = HEAD_SIZE ** (-0.5)
CHUNK = 128
QUERY_BLOCK = 256
STEP_ROWS = 16
VMEM_BYTES = 50 * 1024 * 1024

epsilon = 1e-06
masked_score = -1e30
highest = lax.Precision.HIGHEST
f32 = jnp.float32
bf16 = jnp.bfloat16


def rms_scale(value_rows, gain):
    return (
        value_rows
        * lax.rsqrt(jnp.mean(value_rows * value_rows, axis=-1, keepdims=True) + epsilon)
        * gain
    )


def norm_back(grad_in, value_rows, gain):
    factor = lax.rsqrt(jnp.mean(value_rows * value_rows, axis=-1, keepdims=True) + epsilon)
    weighted = grad_in * gain
    spread = jnp.mean(weighted * value_rows, axis=-1, keepdims=True)
    return (
        factor * weighted - value_rows * factor * factor * factor * spread,
        jnp.sum(grad_in * value_rows * factor, axis=0),
    )


def silu(value_rows):
    return value_rows * jax.nn.sigmoid(value_rows)


def silu_slope(value_rows):
    sigmoid_v = jax.nn.sigmoid(value_rows)
    return sigmoid_v * (1.0 + value_rows * (1.0 - sigmoid_v))


def dot(a, b, ca, cb, precision=None):
    return lax.dot_general(
        a, b, (((ca,), (cb,)), ((), ())), precision=precision, preferred_element_type=f32
    )


def sequence_layout(seq_lengths, position):
    seq_ends = jnp.cumsum(seq_lengths, dtype=jnp.int32)
    seq_starts = seq_ends - seq_lengths
    segment = jnp.sum(
        (position[:, None] >= seq_ends[None, :]).astype(jnp.int32), axis=1, dtype=jnp.int32
    )
    labels = jnp.arange(seq_lengths.shape[0], dtype=jnp.int32)
    seq_begin = jnp.sum(
        jnp.where(segment[:, None] == labels[None, :], seq_starts[None, :], 0),
        axis=1,
        dtype=jnp.int32,
    )
    return (segment, (position - seq_begin).astype(f32))


def key_range(i):
    low = max(0, i * QUERY_BLOCK - (WIN - 1)) // QUERY_BLOCK * QUERY_BLOCK
    return low, (i + 1) * QUERY_BLOCK


def fill_mask(seg_col, seg_row, mask, blocks):
    for i in range(blocks):
        low, high = key_range(i)
        cols = slice(i * QUERY_BLOCK, (i + 1) * QUERY_BLOCK)
        shape = (high - low, QUERY_BLOCK)
        key = lax.broadcasted_iota(jnp.int32, shape, 0) + low
        query = lax.broadcasted_iota(jnp.int32, shape, 1) + i * QUERY_BLOCK
        gap = query - key
        visible = (seg_col[low:high, :] == seg_row[:, cols]) & (gap >= 0) & (gap < WIN)
        mask[low:high, cols] = jnp.where(visible, 0.0, masked_score)


def rotate(value, cosine, sine):
    half = HEAD_SIZE // 2
    a, b = value[:half], value[half:]
    return jnp.concatenate([a * cosine - b * sine, b * cosine + a * sine], axis=0)


def attn_fwd_kernel(
    kvmap, kv_ref, q_ref, cosine, sine, seg_row, seg_col, o_ref, qt_ref, kt_ref, kn_ref, vn_ref, mask, vt, *, blocks
):
    h = pl.program_id(0)

    @pl.when(h == 0)
    def _():
        fill_mask(seg_col, seg_row, mask, blocks)
        for c in range(KEY_VALUE_HEADS):
            k = rotate(kv_ref[c], cosine[...], sine[...])
            kt_ref[c] = k.astype(bf16)
            kn_ref[c] = k.T.astype(bf16)
            v = kv_ref[KEY_VALUE_HEADS + c]
            vt[c] = v.astype(bf16)
            vn_ref[c] = v.T.astype(bf16)

    kv = kvmap[h]
    tokens = o_ref.shape[3]
    for i in range(blocks):
        low, high = key_range(i)
        start, stop = i * QUERY_BLOCK, (i + 1) * QUERY_BLOCK
        cols = slice(start, stop)
        q = (rotate(q_ref[0, :, cols], cosine[:, cols], sine[:, cols]) * SCALE).astype(bf16)
        qt_ref[0, :, cols] = q
        s = dot(kn_ref[kv, low:high, :], q, 1, 0) + mask[low:high, cols]
        p = jnp.exp(s - jnp.max(s, axis=0, keepdims=True))
        total = jnp.sum(p, axis=0, keepdims=True)
        o = dot(vt[kv, :, low:high], p.astype(bf16), 1, 0)
        o = (o / total).astype(bf16)
        for d in range(o_ref.shape[0]):
            first, last = max(start, d * tokens), min(stop, (d + 1) * tokens)
            if first < last:
                part = o[:, first - start : last - start]
                o_ref[d, 0, :, first - d * tokens : last - d * tokens] = part


def attn_fwd(kvmap, proj, cosine, sine, seg_row, seg_col, devices):
    heads = proj.shape[0] - 2 * KEY_VALUE_HEADS
    group = proj.shape[2]
    tokens = group // devices
    per_head = pl.BlockSpec((1, HEAD_SIZE, group), lambda h, m: (h, 0, 0))
    angle = pl.BlockSpec((HEAD_SIZE // 2, group), lambda h, m: (0, 0))
    kv_t = (KEY_VALUE_HEADS, HEAD_SIZE, group)
    kv_n = (KEY_VALUE_HEADS, group, HEAD_SIZE)
    whole_t = pl.BlockSpec(kv_t, lambda h, m: (0, 0, 0))
    whole_n = pl.BlockSpec(kv_n, lambda h, m: (0, 0, 0))
    return pl.pallas_call(
        functools.partial(attn_fwd_kernel, blocks=group // QUERY_BLOCK),
        out_shape=(
            jax.ShapeDtypeStruct((devices, heads, HEAD_SIZE, tokens), bf16),
            jax.ShapeDtypeStruct((heads, HEAD_SIZE, group), bf16),
            jax.ShapeDtypeStruct(kv_t, bf16),
            jax.ShapeDtypeStruct(kv_n, bf16),
            jax.ShapeDtypeStruct(kv_n, bf16),
        ),
        grid_spec=pltpu.PrefetchScalarGridSpec(
            num_scalar_prefetch=1,
            grid=(heads,),
            in_specs=[
                pl.BlockSpec((2 * KEY_VALUE_HEADS, HEAD_SIZE, group), lambda h, m: (0, 0, 0)),
                pl.BlockSpec((1, HEAD_SIZE, group), lambda h, m: (h + 2 * KEY_VALUE_HEADS, 0, 0)),
                angle,
                angle,
                pl.BlockSpec((1, group), lambda h, m: (0, 0)),
                pl.BlockSpec((group, 1), lambda h, m: (0, 0)),
            ],
            out_specs=(
                pl.BlockSpec((devices, 1, HEAD_SIZE, tokens), lambda h, m: (0, h, 0, 0)),
                per_head,
                whole_t,
                whole_n,
                whole_n,
            ),
            scratch_shapes=[pltpu.VMEM((group, group), f32), pltpu.VMEM(kv_t, bf16)],
        ),
        compiler_params=pltpu.CompilerParams(vmem_limit_bytes=VMEM_BYTES),
        cost_estimate=pl.CostEstimate(
            flops=group * group, bytes_accessed=group * HEAD_SIZE, transcendentals=group,
        ),
        name="attn_fwd",
    )(kvmap, proj, proj, cosine, sine, seg_row, seg_col)


def attn_bwd_kernel(kvmap, *refs, blocks, devices):
    do_parts = refs[:devices]
    q_ref, kn_ref, kt_ref, vn_ref, cosine, sine, seg_row, seg_col = refs[devices : devices + 8]
    g_ref, mask, dk, dv, do_all = refs[devices + 8 :]
    h = pl.program_id(0)

    @pl.when(h == 0)
    def _():
        fill_mask(seg_col, seg_row, mask, blocks)
        dk[...] = jnp.zeros(dk.shape, f32)
        dv[...] = jnp.zeros(dv.shape, f32)

    kv = kvmap[h]
    tokens = do_parts[0].shape[3]
    for d in range(devices):
        do_all[:, d * tokens : (d + 1) * tokens] = do_parts[d][0, 0]
    for i in range(blocks):
        low, high = key_range(i)
        cols = slice(i * QUERY_BLOCK, (i + 1) * QUERY_BLOCK)
        q = q_ref[0, :, cols]
        do = do_all[:, cols]
        s = dot(kn_ref[kv, low:high, :], q, 1, 0) + mask[low:high, cols]
        p = jnp.exp(s - jnp.max(s, axis=0, keepdims=True))
        p = p * (1.0 / jnp.sum(p, axis=0, keepdims=True))
        dp = dot(vn_ref[kv, low:high, :], do, 1, 0)
        delta = jnp.sum(p * dp, axis=0, keepdims=True)
        ds = (p * (dp - delta)).astype(bf16)
        dv[kv, low:high, :] += dot(p.astype(bf16), do, 1, 1)
        dk[kv, low:high, :] += dot(ds, q, 1, 1)
        dq = dot(kt_ref[kv, :, low:high], ds, 1, 0) * SCALE
        dq = rotate(dq, cosine[:, cols], -sine[:, cols])
        g_ref[2 * KEY_VALUE_HEADS + h, :, cols] = dq.astype(bf16)

    @pl.when(h == pl.num_programs(0) - 1)
    def _():
        for c in range(KEY_VALUE_HEADS):
            g_ref[c] = rotate(dk[c].T, cosine[...], -sine[...]).astype(bf16)
            g_ref[KEY_VALUE_HEADS + c] = dv[c].T.astype(bf16)


def attn_bwd(kvmap, do_blocks, q_t, k_n, k_t, v_n, cosine, sine, seg_row, seg_col):
    devices, heads, _, tokens = do_blocks.shape
    group = q_t.shape[2]
    angle = pl.BlockSpec((HEAD_SIZE // 2, group), lambda h, m: (0, 0))
    kv_t = (KEY_VALUE_HEADS, HEAD_SIZE, group)
    kv_n = (KEY_VALUE_HEADS, group, HEAD_SIZE)
    whole_n = pl.BlockSpec(kv_n, lambda h, m: (0, 0, 0))
    out = (2 * KEY_VALUE_HEADS + heads, HEAD_SIZE, group)

    def block_spec(d):
        return pl.BlockSpec((1, 1, HEAD_SIZE, tokens), lambda h, m: (m[heads + d], h, 0, 0))

    return pl.pallas_call(
        functools.partial(attn_bwd_kernel, blocks=group // QUERY_BLOCK, devices=devices),
        out_shape=jax.ShapeDtypeStruct(out, bf16),
        grid_spec=pltpu.PrefetchScalarGridSpec(
            num_scalar_prefetch=1,
            grid=(heads,),
            in_specs=[block_spec(d) for d in range(devices)]
            + [
                pl.BlockSpec((1, HEAD_SIZE, group), lambda h, m: (h, 0, 0)),
                whole_n,
                pl.BlockSpec(kv_t, lambda h, m: (0, 0, 0)),
                whole_n,
                angle,
                angle,
                pl.BlockSpec((1, group), lambda h, m: (0, 0)),
                pl.BlockSpec((group, 1), lambda h, m: (0, 0)),
            ],
            out_specs=pl.BlockSpec(out, lambda h, m: (0, 0, 0)),
            scratch_shapes=[
                pltpu.VMEM((group, group), f32),
                pltpu.VMEM(kv_n, f32),
                pltpu.VMEM(kv_n, f32),
                pltpu.VMEM((HEAD_SIZE, group), bf16),
            ],
        ),
        compiler_params=pltpu.CompilerParams(vmem_limit_bytes=VMEM_BYTES),
        cost_estimate=pl.CostEstimate(
            flops=group * group, bytes_accessed=group * HEAD_SIZE, transcendentals=group,
        ),
        name="attn_bwd",
    )(kvmap, *([do_blocks] * devices), q_t, k_n, k_t, v_n, cosine, sine, seg_row, seg_col)


def block_setup(p_ref, bias, decay, marks, seg_col, channels):
    at = 2 * channels
    b_t = p_ref[at : at + NS].astype(bf16)
    c_t = p_ref[at + NS : at + 2 * NS].astype(bf16)
    raw = p_ref[at + 2 * NS : at + 2 * NS + STEP_ROWS] + bias[...]
    step = jnp.maximum(raw, 0.0) + jnp.log1p(jnp.exp(-jnp.abs(raw)))
    rate = -step * decay[...]
    rows = lax.broadcasted_iota(jnp.int32, (CHUNK, CHUNK), 0)
    cols = lax.broadcasted_iota(jnp.int32, (CHUNK, CHUNK), 1)
    a_t = dot(rate, (rows <= cols).astype(f32), 1, 0, highest)
    a_n = a_t.T
    visible = (seg_col[...] == marks[0:1]) & (rows <= cols)
    hidden = jnp.where(visible, 0.0, masked_score)
    return b_t, c_t, raw, step, rate, a_t, a_n, rows, cols, hidden


def ssm_fwd_kernel(p_ref, bias, decay, marks, seg_col, skip, y_ref, mixed_ref, states, state, *, heads):
    channels = heads * HEAD_SIZE

    @pl.when(pl.program_id(0) == 0)
    def _():
        state[...] = jnp.zeros(state.shape, f32)

    states[0] = state[...]
    b_t, c_t, _, step, _, a_t, a_n, _, _, hidden = block_setup(
        p_ref, bias, decay, marks, seg_col, channels
    )
    block = dot(b_t, c_t, 0, 0)
    enter, leave, through = marks[1:2], marks[2:3], marks[3:4, 0:1]
    for h in range(heads):
        at = slice(h * HEAD_SIZE, (h + 1) * HEAD_SIZE)
        a_row = a_t[h : h + 1]
        a_end = a_t[h : h + 1, CHUNK - 1 :]
        x = p_ref[at].astype(bf16).astype(f32)
        z = p_ref[channels + h * HEAD_SIZE : channels + (h + 1) * HEAD_SIZE]
        mixing = (jnp.exp(a_row - a_n[:, h : h + 1] + hidden) * block).astype(bf16)
        xs = x * step[h : h + 1]
        y = dot(xs.astype(bf16), mixing, 1, 0)
        s = state[at]
        y = y + dot(s.astype(bf16), c_t, 1, 0) * (enter * jnp.exp(a_row)) + skip[h] * x
        y_ref[at] = y
        mixed_ref[at] = (y * silu(z)).astype(bf16)
        xw = (xs * (leave * jnp.exp(a_end - a_row))).astype(bf16)
        state[at] = through * jnp.exp(a_end) * s + dot(xw, b_t, 1, 1)


def ssm_specs(height, order):
    column = pl.BlockSpec((STEP_ROWS, 1), lambda c: (0, 0))
    return [
        pl.BlockSpec((height, CHUNK), lambda c: (0, order(c))),
        column,
        column,
        pl.BlockSpec((8, CHUNK), lambda c: (0, order(c))),
        pl.BlockSpec((CHUNK, 1), lambda c: (order(c), 0)),
        pl.BlockSpec(memory_space=pltpu.SMEM),
    ]


def ssm_fwd(heads, proj, bias, decay, marks, seg_col, skip):
    height, group = proj.shape
    channels = heads * HEAD_SIZE
    count = group // CHUNK
    by_block = pl.BlockSpec((channels, CHUNK), lambda c: (0, c))
    return pl.pallas_call(
        functools.partial(ssm_fwd_kernel, heads=heads),
        out_shape=(
            jax.ShapeDtypeStruct((channels, group), f32),
            jax.ShapeDtypeStruct((channels, group), bf16),
            jax.ShapeDtypeStruct((count, channels, NS), f32),
        ),
        grid=(count,),
        in_specs=ssm_specs(height, lambda c: c),
        out_specs=(by_block, by_block, pl.BlockSpec((1, channels, NS), lambda c: (c, 0, 0))),
        scratch_shapes=[pltpu.VMEM((channels, NS), f32)],
        compiler_params=pltpu.CompilerParams(vmem_limit_bytes=VMEM_BYTES),
        cost_estimate=pl.CostEstimate(
            flops=group * group, bytes_accessed=group * HEAD_SIZE, transcendentals=group,
        ),
        name="ssm_fwd",
    )(proj, bias, decay, marks, seg_col, skip)


def ssm_bwd_kernel(
    p_ref,
    bias,
    decay,
    marks,
    seg_col,
    skip,
    up_ref,
    y_ref,
    states,
    g_ref,
    sums,
    adjoint,
    after,
    before,
    gstep,
    grate,
    *,
    heads,
):
    channels = heads * HEAD_SIZE

    @pl.when(pl.program_id(0) == 0)
    def _():
        for ref in (adjoint, sums, after, before, gstep, grate):
            ref[...] = jnp.zeros(ref.shape, f32)

    b_t, c_t, raw, step_all, rate_all, a_t, a_n, rows, cols, hidden = block_setup(
        p_ref, bias, decay, marks, seg_col, channels
    )
    block = dot(b_t, c_t, 0, 0)
    enter, leave, through = marks[1:2], marks[2:3], marks[3:4, 0:1]
    from_here = (rows >= cols).astype(f32)
    from_here_low = from_here.astype(bf16)
    strictly = (rows < cols).astype(f32)
    pair_sum = jnp.zeros((CHUNK, CHUNK), f32)
    gc = jnp.zeros((NS, CHUNK), f32)
    gb = jnp.zeros((NS, CHUNK), f32)
    at_skip = 2 * STEP_ROWS
    for h in range(heads):
        at = slice(h * HEAD_SIZE, (h + 1) * HEAD_SIZE)
        at_gate = slice(channels + h * HEAD_SIZE, channels + (h + 1) * HEAD_SIZE)
        one = slice(h, h + 1)
        a_row = a_t[one]
        a_end = a_t[one, CHUNK - 1 :]
        step = step_all[one]
        x = p_ref[at].astype(bf16).astype(f32)
        z = p_ref[at_gate]
        g = up_ref[at]
        sigmoid_z = jax.nn.sigmoid(z)
        gy = g * z * sigmoid_z
        gz = g * y_ref[at] * sigmoid_z * (1.0 + z * (1.0 - sigmoid_z))
        g_ref[at_gate] = gz.astype(bf16)
        sums[at_skip + h : at_skip + h + 1] += jnp.sum(gy * x, axis=0, keepdims=True)
        reach = jnp.exp(a_row - a_n[:, one] + hidden)
        gy_low = gy.astype(bf16)
        xs = x * step
        u = dot(gy_low, (reach * block).astype(bf16), 1, 1)
        lam = adjoint[at]
        lam_low = lam.astype(bf16)
        out_weight = leave * jnp.exp(a_end - a_row)
        u_state = dot(lam_low, b_t, 1, 0) * out_weight
        u = u + u_state
        g_ref[at] = (step * u + skip[h] * gy).astype(bf16)
        gstep[one] = jnp.sum(x * u, axis=0, keepdims=True)
        before[one] = jnp.sum(xs * u_state, axis=0, keepdims=True)
        pairs = dot(xs.astype(bf16), gy_low, 0, 0) * reach
        pair_sum = pair_sum + pairs
        crossing = dot((pairs * block).astype(bf16), from_here_low, 1, 0)
        crossed = jnp.sum(crossing * strictly, axis=0, keepdims=True)
        gyw = gy * (enter * jnp.exp(a_row))
        gyw_low = gyw.astype(bf16)
        s = states[0, at]
        s_low = s.astype(bf16)
        after[one] = jnp.sum(gyw * dot(s_low, c_t, 1, 0), axis=0, keepdims=True)
        gc = gc + dot(s_low, gyw_low, 0, 0)
        gb = gb + dot(lam_low, (xs * out_weight).astype(bf16), 0, 0)
        passing = through * jnp.exp(a_end)
        product = jnp.sum(jnp.sum(lam * s, axis=1, keepdims=True), axis=0, keepdims=True)
        grate[one] = crossed + passing * product
        adjoint[at] = passing * lam + dot(gyw_low, c_t, 1, 1)
    grate_all = (
        grate[...]
        + dot(after[...], from_here, 1, 0, highest)
        + dot(before[...], strictly, 1, 0, highest)
    )
    pair_low = pair_sum.astype(bf16)
    small = 2 * channels
    g_ref[small : small + NS] = (gb + dot(c_t, pair_low, 1, 1)).astype(bf16)
    g_ref[small + NS : small + 2 * NS] = (gc + dot(b_t, pair_low, 1, 0)).astype(bf16)
    graw = (gstep[...] - grate_all * decay[...]) * jax.nn.sigmoid(raw)
    at_step = small + 2 * NS
    g_ref[at_step : at_step + STEP_ROWS] = graw.astype(bf16)
    rest = g_ref.shape[0] - at_step - STEP_ROWS
    g_ref[at_step + STEP_ROWS :] = jnp.zeros((rest, CHUNK), bf16)
    sums[:STEP_ROWS] += graw
    sums[STEP_ROWS:at_skip] += grate_all * rate_all


def ssm_bwd(heads, proj, bias, decay, marks, seg_col, skip, up_t, y_t, states):
    height, group = proj.shape
    channels = heads * HEAD_SIZE
    count = group // CHUNK

    def order(c):
        return count - 1 - c

    by_block = pl.BlockSpec((channels, CHUNK), lambda c: (0, order(c)))
    small = pltpu.VMEM((STEP_ROWS, CHUNK), f32)
    return pl.pallas_call(
        functools.partial(ssm_bwd_kernel, heads=heads),
        out_shape=(
            jax.ShapeDtypeStruct((height, group), bf16),
            jax.ShapeDtypeStruct((3 * STEP_ROWS, CHUNK), f32),
        ),
        grid=(count,),
        in_specs=ssm_specs(height, order)
        + [by_block, by_block, pl.BlockSpec((1, channels, NS), lambda c: (order(c), 0, 0))],
        out_specs=(
            pl.BlockSpec((height, CHUNK), lambda c: (0, order(c))),
            pl.BlockSpec((3 * STEP_ROWS, CHUNK), lambda c: (0, 0)),
        ),
        scratch_shapes=[pltpu.VMEM((channels, NS), f32), small, small, small, small],
        compiler_params=pltpu.CompilerParams(vmem_limit_bytes=VMEM_BYTES),
        cost_estimate=pl.CostEstimate(
            flops=group * group, bytes_accessed=group * HEAD_SIZE, transcendentals=group,
        ),
        name="ssm_bwd",
    )(proj, bias, decay, marks, seg_col, skip, up_t, y_t, states)


def ffn_middle_kernel(gate_up_ref, g_ref, hidden_ref, g_gu_ref):
    width = g_ref.shape[1]
    gate = gate_up_ref[:, :width].astype(f32)
    up = gate_up_ref[:, width:].astype(f32)
    g = g_ref[...].astype(f32)
    sigmoid_v = jax.nn.sigmoid(gate)
    passed = gate * sigmoid_v
    hidden_ref[...] = (passed * up).astype(bf16)
    slope = sigmoid_v * (1.0 + gate * (1.0 - sigmoid_v))
    g_gu_ref[:, :width] = (g * up * slope).astype(bf16)
    g_gu_ref[:, width:] = (g * passed).astype(bf16)


def ffn_middle(gate_up, g_hidden):
    group, width = g_hidden.shape
    height = 128
    narrow = pl.BlockSpec((height, width), lambda i: (i, 0))
    wide = pl.BlockSpec((height, 2 * width), lambda i: (i, 0))
    return pl.pallas_call(
        ffn_middle_kernel,
        out_shape=(
            jax.ShapeDtypeStruct((group, width), bf16),
            jax.ShapeDtypeStruct((group, 2 * width), bf16),
        ),
        grid=(group // height,),
        in_specs=[wide, narrow],
        out_specs=(narrow, wide),
        compiler_params=pltpu.CompilerParams(vmem_limit_bytes=VMEM_BYTES),
        name="ffn_middle",
    )(gate_up, g_hidden)


def weight_grads_kernel(rows_ref, g_ref, hidden_ref, cot_ref, wide_ref, down_ref, *, wide_steps):
    i = pl.program_id(0)

    @pl.when(i < wide_steps)
    def _():
        wide_ref[...] = dot(rows_ref[...], g_ref[...], 0, 0).astype(bf16)

    @pl.when(i >= wide_steps)
    def _():
        down_ref[...] = dot(hidden_ref[...], cot_ref[...], 0, 0).astype(bf16)


def ffn_weight_grads(rows, g_wide, hidden, cot):
    group, depth = rows.shape
    wide, width = g_wide.shape[1], hidden.shape[1]
    columns, height = 256, 128
    if wide % columns or width % height:
        return (
            dot(rows, g_wide, 0, 0).astype(bf16),
            row_major(dot(hidden, cot, 0, 0).astype(bf16)),
        )
    wide_steps, down_steps = wide // columns, width // height

    def first(i):
        return jnp.minimum(i, wide_steps - 1)

    def second(i):
        return jnp.maximum(i - wide_steps, 0)

    whole = pl.BlockSpec((group, depth), lambda i: (0, 0))
    return pl.pallas_call(
        functools.partial(weight_grads_kernel, wide_steps=wide_steps),
        out_shape=(
            jax.ShapeDtypeStruct((depth, wide), bf16),
            jax.ShapeDtypeStruct((width, depth), bf16),
        ),
        grid=(wide_steps + down_steps,),
        in_specs=[
            whole,
            pl.BlockSpec((group, columns), lambda i: (0, first(i))),
            pl.BlockSpec((group, height), lambda i: (0, second(i))),
            whole,
        ],
        out_specs=(
            pl.BlockSpec((depth, columns), lambda i: (0, first(i))),
            pl.BlockSpec((height, depth), lambda i: (second(i), 0)),
        ),
        compiler_params=pltpu.CompilerParams(vmem_limit_bytes=VMEM_BYTES),
        cost_estimate=pl.CostEstimate(flops=group * group, bytes_accessed=group, transcendentals=0),
        name="ffn_weight_grads",
    )(rows, g_wide, hidden, cot)


def pad_to(value, multiple):
    return -(-value // multiple) * multiple


def place_columns(block, start, width):
    return jnp.pad(block, ((0, 0), (start, width - start - block.shape[1])))


def peers(devices, k):
    return [(i, i ^ k) for i in range(devices)]


def one_hot(rows, cols, wanted):
    row = wanted(jnp.arange(rows, dtype=jnp.int32))
    return (row[:, None] == jnp.arange(cols, dtype=jnp.int32)[None, :]).astype(bf16)


def tie(*values):
    return lax.optimization_barrier(values)


def row_major(value):
    return with_layout_constraint(value, Layout(tuple(range(value.ndim))))


def send_to_peers(parts):
    devices = lax.axis_size("fsdp")
    return [lax.ppermute(parts[k - 1], "fsdp", peers(devices, k)) for k in range(1, devices)]


def gather_start(part):
    devices = lax.axis_size("fsdp")
    if devices != 4:
        return send_to_peers([part] * (devices - 1))
    half = part.shape[0] // 2
    one, two = (lax.ppermute(part, "fsdp", peers(devices, k)) for k in (1, 2))
    upper = lax.ppermute(two[:half], "fsdp", peers(devices, 1))
    lower = lax.ppermute(one[half:], "fsdp", peers(devices, 2))
    return [one, two, jnp.concatenate([upper, lower], axis=0)]


def place_blocks(own, received):
    devices, mine = lax.axis_size("fsdp"), lax.axis_index("fsdp")
    result = jnp.broadcast_to(own[None], (devices,) + own.shape)
    for k in range(1, devices):
        result = lax.dynamic_update_index_in_dim(result, received[k - 1], mine ^ k, 0)
    return result


def take_blocks(blocks):
    devices, mine = lax.axis_size("fsdp"), lax.axis_index("fsdp")
    return [lax.dynamic_index_in_dim(blocks, mine ^ k, 0, False) for k in range(devices)]


def exchange(blocks):
    parts = take_blocks(blocks)
    return place_blocks(parts[0], send_to_peers(parts[1:]))


def gather_rows(part, hold=lambda received: received):
    devices = lax.axis_size("fsdp")
    received = hold(send_to_peers([part] * (devices - 1)))
    return place_blocks(part, received).reshape((devices * part.shape[0],) + part.shape[1:])


def add_up(own, received):
    total = own.astype(f32)
    for part in received:
        total = total + part.astype(f32)
    return total


def row_blocks(partial):
    devices = lax.axis_size("fsdp")
    return partial.reshape((devices, partial.shape[0] // devices) + partial.shape[1:])


def scatter_rows(partial):
    parts = take_blocks(row_blocks(partial))
    return add_up(parts[0], send_to_peers(parts[1:]))


def all_sum(value):
    for axis in ("fsdp", "rep"):
        devices, k = lax.axis_size(axis), 1
        while k < devices:
            value = value + lax.ppermute(value, axis, peers(devices, k))
            k *= 2
    return value


def local(
    tokens,
    lengths,
    w_query,
    w_key,
    w_value,
    w_attn_out,
    w_inner,
    w_gate_z,
    w_bc,
    w_step,
    w_mamba_out,
    w_ffn_gate,
    w_ffn_up,
    w_ffn_down,
    norm_gains,
    step_bias,
    decay_log,
    skip_gain,
    cotangent,
):
    F, R = lax.axis_size("fsdp"), lax.axis_size("rep")
    mine = lax.axis_index("fsdp")
    rows = tokens.shape[0]
    group = rows * F
    aligned = D % (F * R) == 0 and FF % (F * R) == 0
    depth = D // (F * R) if aligned else D // F

    heads_q = -(-QUERY_HEADS // F)
    width_q = heads_q * HEAD_SIZE
    per_dev = MI // F
    first_head = [per_dev * d // HEAD_SIZE for d in range(F)]
    shift = [per_dev * d % HEAD_SIZE for d in range(F)]
    heads_s = max(-(-(s + per_dev) // HEAD_SIZE) for s in shift)
    channels = heads_s * HEAD_SIZE
    at_small = 2 * channels
    at_step = at_small + 2 * NS
    width_att = 2 * KV + width_q
    width_ssm = at_small + 64
    hidden_dev = FF // F
    blocks = R if aligned else 1
    rows_o, rows_m, rows_f = (D // F // blocks, per_dev // blocks, hidden_dev // blocks)
    pad_o, pad_m, pad_f = (pad_to(n, 8) for n in (rows_o, rows_m, rows_f))
    width_f = blocks * pad_f

    if aligned:

        def old_place(n):
            return (n // depth % F) * (R * depth) + n // (F * depth) * depth + n % depth

        order = one_hot(D, D, old_place)

        def permute(v):
            return dot(v, order, 1, 1).astype(v.dtype)

        def restore(v):
            return dot(v, order, 1, 0).astype(v.dtype)

        gains = norm_gains.reshape(4, F, R, depth).transpose(0, 2, 1, 3).reshape(4, D)
    else:

        def permute(v):
            return v

        restore = permute
        gains = norm_gains

    def pad_rows(matrix, height):
        return jnp.pad(matrix, ((0, height - matrix.shape[0]), (0, 0)))

    def rep_gather(flat, width):
        return lax.all_gather(flat, "rep", axis=0, tiled=True).reshape(-1, width)

    def read(flat, width):
        return flat.reshape(depth, width) if aligned else rep_gather(flat, width)

    def collect(part):
        if aligned:
            part = part.reshape(F * depth, part.shape[2])
            return lax.all_gather(part, "rep", axis=0, tiled=True)
        return part.reshape(D, part.shape[2])

    index = jnp.arange(group, dtype=jnp.int32)
    segment, place = sequence_layout(lengths[0], index)
    frequency = jnp.exp(
        jnp.arange(HEAD_SIZE // 2, dtype=f32) * (-2.0 * math.log(10000.0) / HEAD_SIZE)
    )
    angles = frequency[:, None] * place[None, :]
    cosine, sine = jnp.cos(angles), jnp.sin(angles)
    seg_row, seg_col = segment[None, :], segment[:, None]
    by_chunk = segment.reshape(group // CHUNK, CHUNK)
    last = by_chunk[:, -1:]
    prior = jnp.concatenate([jnp.full((1, 1), -1, jnp.int32), last[:-1]], axis=0)
    marks = jnp.stack(
        [
            by_chunk,
            (by_chunk == prior).astype(jnp.int32),
            (by_chunk == last).astype(jnp.int32),
            jnp.broadcast_to((last == prior).astype(jnp.int32), by_chunk.shape),
        ]
    ).reshape(4, group)
    marks = jnp.concatenate([marks, jnp.zeros((4, group), jnp.int32)], axis=0).astype(f32)
    seg_col_f = seg_col.astype(f32)
    distance = jnp.arange(F, dtype=jnp.int32) ^ mine
    kvmap = jnp.minimum(mine * heads_q + jnp.arange(heads_q), QUERY_HEADS - 1) // HEADS_PER_GROUP
    kvmap = jnp.concatenate([kvmap.astype(jnp.int32), distance.astype(jnp.int32)])

    both = permute(jnp.concatenate([tokens, cotangent], axis=0))
    x_float = both[:rows].astype(f32)
    cot = both[rows:]
    normed_own = rms_scale(x_float, gains[0]).astype(bf16)

    if aligned:
        down_shards = jnp.concatenate(
            [
                pad_rows(w_attn_out.reshape(rows_o, D), pad_o),
                pad_rows(w_mamba_out.reshape(rows_m, D), pad_m),
                pad_rows(w_ffn_down.reshape(rows_f, D), pad_f),
            ],
            axis=0,
        )
        down_shards = permute(down_shards)
        down_shards, w_inner, w_gate_z, w_query = tie(down_shards, w_inner, w_gate_z, w_query)
        out_both = lax.all_gather(down_shards[: pad_o + pad_m], "rep", axis=0)
        w_o_part = out_both[:, :rows_o].reshape(R * rows_o, D)
        w_m_part = out_both[:, pad_o:].reshape(R * pad_m, D)
        down_late = down_shards[pad_o + pad_m :]
    else:
        w_o_part, w_m_part = rep_gather(w_attn_out, D), rep_gather(w_mamba_out, D)
        down_late = w_ffn_down

    wq, wk, wv = read(w_query, D), read(w_key, KV), read(w_value, KV)
    wx, wz = read(w_inner, MI), read(w_gate_z, MI)
    wbc, wdt = read(w_bc, 2 * NS), read(w_step, MH)
    wq = place_columns(wq, 0, F * width_q)
    column_blocks = []
    for d in range(F):
        cols = slice(per_dev * d, per_dev * (d + 1))
        column_blocks.append(
            jnp.concatenate(
                [
                    wk,
                    wv,
                    wq[:, width_q * d : width_q * (d + 1)],
                    place_columns(wx[:, cols], shift[d], channels),
                    place_columns(wz[:, cols], shift[d], channels),
                    wbc,
                    place_columns(
                        wdt[:, first_head[d] : first_head[d] + heads_s], 0, width_ssm - at_step
                    ),
                ],
                axis=1,
            )
        )
    in_sent = take_blocks(jnp.stack(column_blocks))
    in_got = send_to_peers(in_sent[1:])
    normed_own, in_sent[0] = tie(normed_own, in_sent[0])
    normed_got = tie(*gather_start(normed_own))
    in_got, w_ffn_gate, w_ffn_up = tie(in_got, w_ffn_gate, w_ffn_up)
    in_part = place_blocks(in_sent[0], in_got)
    spread_f = one_hot(
        width_f,
        hidden_dev,
        lambda c: jnp.where(c % pad_f < rows_f, c // pad_f * rows_f + c % pad_f, -1),
    )
    gate_up = jnp.stack([read(w_ffn_gate, FF), read(w_ffn_up, FF)])
    gate_up = gate_up.reshape(2, depth, F, hidden_dev).transpose(2, 1, 0, 3)
    if width_f != hidden_dev:
        gate_up = dot(gate_up.reshape(-1, hidden_dev), spread_f, 1, 1).astype(bf16)
    gate_up = gate_up.reshape(F, depth, 2 * width_f)
    normed = place_blocks(normed_own, normed_got).reshape(group, D)
    w_o_sent, normed_late = tie(w_o_part, normed)
    w_o_got = send_to_peers([w_o_sent] * (F - 1))
    w_att = collect(in_part[:, :, :width_att])
    w_ssm = collect(in_part[:, :, width_att:])

    proj_att = dot(w_att, normed, 0, 1)
    attn_args = (cosine, sine, seg_row, seg_col)
    attn_t, q_t, k_t, k_n, v_n = attn_fwd(
        kvmap, proj_att.reshape(-1, HEAD_SIZE, group), *attn_args, F
    )
    attn_t, w_o_got = tie(attn_t, w_o_got)
    attn_parts = take_blocks(attn_t.reshape(F, width_q, rows))
    attn_got = send_to_peers(attn_parts[1:])
    attn_parts[0], cot_sent = tie(attn_parts[0], cot)
    cot_parts = send_to_peers([cot_sent] * (F - 1))
    own_shift = (mine * per_dev) % HEAD_SIZE
    own_head = (mine * per_dev) // HEAD_SIZE

    def channel_source(c):
        c = c - own_shift
        return jnp.where((c >= 0) & (c < per_dev), c // rows_m * pad_m + c % rows_m, -1)

    spread_m = one_hot(channels, blocks * pad_m, channel_source)
    w_m = dot(spread_m, w_m_part, 1, 0).astype(bf16)

    proj_ssm = dot(w_ssm, normed, 0, 1)
    proj_ssm, cot_parts = tie(proj_ssm, cot_parts)

    def own_heads(v):
        v = jnp.pad(v, (0, STEP_ROWS))
        return lax.dynamic_slice_in_dim(v, own_head, STEP_ROWS, 0)

    ssm_args = (
        proj_ssm,
        own_heads(step_bias)[:, None],
        jnp.exp(own_heads(decay_log))[:, None],
        marks,
        seg_col_f,
        own_heads(skip_gain),
    )
    y_t, mixed_t, states = ssm_fwd(heads_s, *ssm_args)
    attn_got, gate_up, mixed_t = tie(attn_got, gate_up, mixed_t)
    gate_up = take_blocks(gate_up)
    gate_up_got = send_to_peers(gate_up[1:])
    mamba_parts = take_blocks(row_blocks(row_major(dot(mixed_t, w_m, 0, 0).astype(bf16))))
    mamba_got = send_to_peers(mamba_parts[1:])

    gate_up_got, mamba_parts[0] = tie(gate_up_got, mamba_parts[0])
    w_gu = collect(place_blocks(gate_up[0], gate_up_got))
    if aligned:
        w_down = lax.all_gather(down_late, "rep", axis=0, tiled=True)
    else:
        w_down = rep_gather(down_late, D)

    w_o_got, attn_got, mamba_parts[0] = tie(w_o_got, attn_got, mamba_parts[0])
    w_o = row_major(place_blocks(w_o_sent, w_o_got)).reshape(D, D)
    attn_tok = row_major(place_blocks(attn_parts[0], attn_got)).reshape(F * width_q, rows)[:D]
    attn_proj = dot(attn_tok, w_o, 0, 0)
    branch_attn = rms_scale(attn_proj, gains[1])
    def by_distance(own, received):
        return jnp.concatenate([own] + list(received), axis=0)

    cot_all = by_distance(cot, cot_parts)
    g_hidden = row_major(dot(cot_all, w_down, 1, 1).astype(bf16))
    mamba_got, branch_attn, g_hidden = tie(mamba_got, branch_attn, g_hidden)
    mamba_proj = add_up(mamba_parts[0], mamba_got)
    branch_mamba = rms_scale(mamba_proj, gains[2])
    mix = x_float + 0.5 * (branch_attn + branch_mamba)

    def scatter_start(partial):
        parts = [partial[rows * k : rows * (k + 1)] for k in range(F)]
        return parts[0], send_to_peers(parts[1:])

    normed_two = rms_scale(mix, gains[3]).astype(bf16)
    normed_two = by_distance(normed_two, gather_start(normed_two))
    gate_and_up = row_major(dot(normed_two, w_gu, 1, 0).astype(bf16))
    hidden, g_gu = ffn_middle(gate_and_up, g_hidden)
    g_two_partial = row_major(dot(g_gu, w_gu, 1, 1).astype(bf16))
    g_two_own, g_two_got = scatter_start(g_two_partial)
    g_gu, hidden, g_two_own = tie(g_gu, hidden, g_two_own)
    grad_gu, grad_down = ffn_weight_grads(normed_two, g_gu, hidden, cot_all)
    g_two_got, grad_gu, grad_down = tie(g_two_got, grad_gu, grad_down)
    g_mix_norm, g_gain_three = norm_back(add_up(g_two_own, g_two_got), mix, gains[3])
    g_mix = cot.astype(f32) + g_mix_norm

    def over_rep(grad):
        if aligned:
            return lax.psum_scatter(grad, "rep", scatter_dimension=0, tiled=True)
        return grad

    def to_owners(part):
        return exchange(part.reshape(F, depth, part.shape[1]))

    def finish(matrix):
        flat = matrix.reshape(-1)
        if aligned:
            return flat.astype(f32)
        return lax.psum_scatter(flat, "rep", scatter_dimension=0, tiled=True).astype(f32)

    gu_part, down_part = over_rep(grad_gu), over_rep(grad_down)

    g_branch = 0.5 * g_mix
    g_attn_proj, g_gain_one = norm_back(g_branch, attn_proj, gains[1])
    g_attn_proj = g_attn_proj.astype(bf16)
    g_mamba_proj, g_gain_two = norm_back(g_branch, mamba_proj, gains[2])
    g_mamba_proj = g_mamba_proj.astype(bf16)
    g_attn_tok = row_major(dot(w_o, g_attn_proj, 1, 1).astype(bf16))
    g_attn_tok, attn_late, hidden = tie(g_attn_tok, attn_tok, hidden)
    g_attn_parts = jnp.pad(g_attn_tok, ((0, F * width_q - D), (0, 0)))
    g_attn_parts = take_blocks(g_attn_parts.reshape(F, heads_q, HEAD_SIZE, rows))
    g_attn_got = send_to_peers(g_attn_parts[1:])
    grad_o = row_major(dot(attn_late, g_attn_proj, 1, 0).astype(bf16))
    grad_o = take_blocks(row_blocks(grad_o))
    out_partial = row_major(dot(hidden, w_down, 1, 0).astype(bf16))
    g_attn_got, grad_o, out_partial = tie(g_attn_got, grad_o, out_partial)
    g_mamba_sent, g_attn_got = tie(g_mamba_proj, g_attn_got)
    g_mamba_got = send_to_peers([g_mamba_sent] * (F - 1))
    g_attn_blocks = jnp.stack([g_attn_parts[0]] + g_attn_got)
    g_att = attn_bwd(kvmap, g_attn_blocks, q_t, k_n, k_t, v_n, *attn_args)
    g_att = g_att.reshape(width_att, group)
    g_mamba_got, g_att, out_partial = tie(g_mamba_got, g_att, out_partial)
    out_own, out_got = scatter_start(out_partial)
    g_mamba_all = place_blocks(g_mamba_sent, g_mamba_got).reshape(group, D)
    g_gated = dot(w_m, g_mamba_all, 1, 1)
    grad_m = row_major(dot(mixed_t, g_mamba_all, 1, 0).astype(bf16))
    grad_m = row_major(dot(spread_m, grad_m, 0, 0).astype(bf16))
    g_gated, grad_m = tie(g_gated, grad_m)
    g_ssm, sums = ssm_bwd(heads_s, *ssm_args, g_gated, y_t, states)

    out_got, g_ssm, gu_part, down_part, grad_o = tie(out_got, g_ssm, gu_part, down_part, grad_o)
    grad_o_got = send_to_peers(grad_o[1:])
    g_in = jnp.concatenate([g_att, g_ssm], axis=0)
    grad_in = dot(normed_late, g_in, 0, 1).astype(bf16)
    g_att, g_ssm, grad_in = tie(g_att, g_ssm, grad_in)
    in_part = over_rep(grad_in)
    g_normed = dot(g_att, w_att, 0, 1) + dot(g_ssm, w_ssm, 0, 1)
    g_normed = take_blocks(row_blocks(row_major(g_normed.astype(bf16))))
    g_normed_got = send_to_peers(g_normed[1:])
    grad_o = add_up(grad_o[0], grad_o_got).astype(bf16)
    if aligned:
        grad_o = jnp.pad(grad_o.reshape(R, rows_o, D), ((0, 0), (0, pad_o - rows_o), (0, 0)))
        joined = jnp.concatenate([grad_o, grad_m.reshape(R, pad_m, D)], axis=1)
        g_normed_got[0], gu_part, in_part = tie(g_normed_got[0], gu_part, in_part)
        joined = over_rep(joined.reshape(R * (pad_o + pad_m), D))
    g_normed = add_up(g_normed[0], g_normed_got)
    gu_back = to_owners(gu_part).reshape(F, depth, 2, width_f)
    if width_f != hidden_dev:
        gu_back = dot(gu_back.reshape(-1, width_f), spread_f, 1, 0).astype(bf16)
    gu_back = gu_back.reshape(F, depth, 2, hidden_dev).transpose(2, 1, 0, 3)
    grad_gate = finish(gu_back[0].reshape(depth, FF))
    grad_up = finish(gu_back[1].reshape(depth, FF))
    grad_down = finish(restore(down_part)[:rows_f])
    g_x_norm, g_gain_zero = norm_back(g_normed, x_float, gains[0])
    grad_tokens = g_mix + g_x_norm
    output = restore((mix + add_up(out_own, out_got)).astype(bf16))
    if aligned:
        grad_tokens = dot(grad_tokens, order.astype(f32), 1, 0, lax.Precision.HIGH)

    head_sums = jnp.sum(sums, axis=1).reshape(3, STEP_ROWS)
    head_sums = lax.dynamic_update_slice(
        jnp.zeros((3, MH + STEP_ROWS), f32), head_sums, (0, own_head)
    )[:, :MH]
    small = jnp.concatenate(
        [g_gain_zero, g_gain_one, g_gain_two, g_gain_three, head_sums.reshape(-1)]
    )
    in_back = to_owners(in_part)
    att_back, ssm_back = in_back[:, :, :width_att], in_back[:, :, width_att:]
    wide_att = att_back[:, :, : 2 * KV].astype(f32)
    grad_query = jnp.concatenate([att_back[d][:, 2 * KV :] for d in range(F)], axis=1)
    grad_query = finish(grad_query[:, :D])
    grad_key = finish(jnp.sum(wide_att[:, :, :KV], axis=0))
    grad_value = finish(jnp.sum(wide_att[:, :, KV:], axis=0))

    wide_ssm = ssm_back[:, :, at_small:].astype(f32)

    def channel_columns(start):
        return finish(
            jnp.concatenate(
                [
                    ssm_back[d][:, start + shift[d] : start + shift[d] + per_dev]
                    for d in range(F)
                ],
                axis=1,
            )
        )

    grad_inner = channel_columns(0)
    grad_gate_z = channel_columns(channels)
    grad_bc = finish(jnp.sum(wide_ssm[:, :, : 2 * NS], axis=0))
    grad_step = finish(
        sum(
            place_columns(wide_ssm[d][:, 2 * NS : 2 * NS + heads_s], first_head[d], MH)
            for d in range(F)
        )
    )

    small_rows = pad_to(small.shape[0], 1024) // 128
    small = jnp.pad(small, (0, small_rows * 128 - small.shape[0])).reshape(small_rows, 128)
    small = all_sum(small).reshape(-1)
    if aligned:
        joined, small = tie(joined, small)
        joined = restore(joined)
        grad_attn_out = finish(joined[:rows_o])
        grad_mamba_out = finish(joined[pad_o : pad_o + rows_m])
    else:
        grad_attn_out, grad_mamba_out = finish(grad_o), finish(grad_m)
    gain_grads = small[: 4 * D].reshape(4, D)
    bias_grad, decay_grad, skip_grad = (
        small[4 * D + MH * i : 4 * D + MH * (i + 1)] for i in range(3)
    )
    if aligned:
        gain_grads = gain_grads.reshape(4, R, F, depth).transpose(0, 2, 1, 3).reshape(4, D)
    return (
        output,
        grad_tokens,
        grad_query,
        grad_key,
        grad_value,
        grad_attn_out,
        grad_inner,
        grad_gate_z,
        grad_bc,
        grad_step,
        grad_mamba_out,
        grad_gate,
        grad_up,
        grad_down,
        gain_grads,
        bias_grad,
        decay_grad,
        skip_grad,
    )


def solution(mesh):
    split_tokens = P(("rep", "fsdp"), None)
    flat = P(("fsdp", "rep"))
    placed = (split_tokens, P("rep", None)) + (flat,) * 12 + (P(),) * 4 + (split_tokens,)
    return jax.shard_map(
        local,
        mesh=mesh,
        in_specs=placed,
        out_specs=(split_tokens, split_tokens) + (flat,) * 12 + (P(),) * 4,
        check_vma=False,
    )
```
